32 devices in a mesh: frame: 16 (over z, y, core), seq: 2 (over x).
Axes of the slice: x: 2, y: 2, z: 4, core: 2. Of those that a mesh axis runs over, the one named last changes fastest.
Arguments:
- tokens: bfloat16 [4, 3136, 384], P('seq', 'frame'), may hold values from -6 to 6
- segments: int32 [4, 3136], P('seq', 'frame'), may hold values from 0 to 3, as said below
- g_attn: float32 [384], replicated, may hold values from 0.1 to 1.9
- w_qkv: bfloat16 [384, 1152], replicated, may hold values from -0.3125 to 0.3125
- w_out: bfloat16 [384, 384], replicated, may hold values from -6 to 6
- g_mlp: float32 [384], replicated, may hold values from 0.1 to 1.9
- w_up: bfloat16 [384, 1536], replicated, may hold values from -0.3125 to 0.3125
- w_down: bfloat16 [1536, 384], replicated, may hold values from -0.15625 to 0.15625
- g_learn: float32 [384], replicated, may hold values from 0.1 to 1.9
- conv_first: bfloat16 [8, 3, 3, 384], replicated, may hold values from -0.109375 to 0.109375
- conv_rest: bfloat16 [3, 8, 3, 3, 8], replicated, may hold values from -0.75 to 0.75
- d_learned: bfloat16 [4, 128, 384], P('seq', 'frame'), may hold values from -6 to 6
Outputs:
- learned: bfloat16 [4, 128, 384], P('seq', 'frame')
- d_tokens: float32 [4, 3136, 384], P('seq', 'frame')
- d_g_attn: float32 [384], replicated
- d_w_qkv: float32 [384, 1152], replicated
- d_w_out: float32 [384, 384], replicated
- d_g_mlp: float32 [384], replicated
- d_w_up: float32 [384, 1536], replicated
- d_w_down: float32 [1536, 384], replicated
- d_g_learn: float32 [384], replicated
- d_conv_first: float32 [8, 3, 3, 384], replicated
- d_conv_rest: float32 [3, 8, 3, 3, 8], replicated
The draws below stay inside these ranges and needn't reach their ends.
Inputs may be any that keep to these rules, and one draw needn't show every extreme that they name: `segments`: within a sequence the clip numbers never fall, are equal on all 196 tokens of a frame and start at 0; a sequence is one clip (all 0) or four clips of whole frames; among the 2 sequences of each index of seq at least one is one clip and at least one holds four.
All inputs are finite; a program needn't handle non-finite values.
Results may differ from the reference program's by a relative error of at most 0.019.
Values may be sent and summed in bfloat16 or wider, within the bound.
A program may use at most 192 MiB of HBM per device.

```python
import jax
import jax.numpy as jnp
from jax import lax

D = 384
HEADS = 6
HEAD_DIM = 64
FF = 1536
MAPS = 8
GRID = 14
SEQ_DEV = 2
SEQS = 4
FRAMES = 16
FRAME_TOKENS = 196
TOKENS_SEQ = 3136
LEARNED_SEQ = 128


def draw_segments(key, part):
    key = jax.random.fold_in(key, 7)
    kind_key, coin_key, cut_key = jax.random.split(key, 3)
    groups = SEQS // SEQ_DEV
    ranking = jax.vmap(lambda subkey: jax.random.permutation(subkey, SEQ_DEV))(jax.random.split(kind_key, groups))
    coin_flip = jax.random.randint(coin_key, (groups, SEQ_DEV), 0, 2)
    single = ((ranking == 0) | (ranking >= 2) & (coin_flip == 1)).reshape(SEQS)
    cut_frames = jax.vmap(lambda subkey: jax.random.permutation(subkey, FRAMES - 1)[:3] + 1)(jax.random.split(cut_key, SEQS))
    frame_pos = jnp.arange(FRAMES, dtype=jnp.int32)
    clip_ids = jnp.sum((cut_frames[:, None, :].astype(jnp.int32) <= frame_pos[None, :, None]).astype(jnp.int32), axis=2)
    clip_ids = jnp.where(single[:, None], 0, clip_ids)
    return jnp.repeat(clip_ids, FRAME_TOKENS, axis=1).astype(jnp.int32)


def levels(stream_key, dims, pieces, smallest, largest):
    loudness = 1.0
    for axis_at, blocks in pieces:
        draws = jax.random.uniform(jax.random.fold_in(jax.random.fold_in(stream_key, 6), axis_at), (blocks,), jnp.float32, smallest / len(pieces), largest / len(pieces))
        loudness = loudness * jnp.repeat(jnp.exp(draws), dims[axis_at] // blocks).reshape((-1,) + (1,) * (len(dims) - 1 - axis_at))
    return loudness


def normal_values(key, extent, deviation, bound, cuts=(), held_as=jnp.bfloat16):
    drawn = jax.random.normal(key, extent, jnp.float32) * deviation
    if len(cuts) > 0:
        drawn = levels(key, extent, cuts, -0.22, 0.18) * drawn
    return jnp.clip(drawn, min=-bound, max=bound).astype(held_as)


def setup_inputs(seed: int = 0) -> dict:
    keys = jax.random.split(jax.random.key(seed), 13)
    tokens = normal_values(keys[0], (SEQS, TOKENS_SEQ, D), 1.0, 6.0, ((0, 2), (1, 16)))
    segments = draw_segments(jax.random.fold_in(keys[12], 71), 0)
    g_attn = jnp.clip(1.0 + 0.18 * jax.random.normal(keys[2], (D,), jnp.float32), 0.1, 1.9)
    w_qkv = normal_values(keys[3], (D, 3 * D), D ** -0.5, 0.3125)
    w_out = normal_values(keys[4], (D, D), 1 ** -0.5, 6.0)
    g_mlp = jnp.clip(1.0 + 0.18 * jax.random.normal(keys[5], (D,), jnp.float32), 0.1, 1.9)
    w_up = normal_values(keys[6], (D, FF), D ** -0.5, 0.3125)
    w_down = normal_values(keys[7], (FF, D), FF ** -0.5, 0.15625)
    g_learn = jnp.clip(1.0 + 0.18 * jax.random.normal(keys[8], (D,), jnp.float32), 0.1, 1.9)
    conv_first = normal_values(keys[9], (MAPS, 3, 3, D), (9 * D) ** -0.5, 0.109375)
    conv_rest = normal_values(keys[10], (3, MAPS, 3, 3, MAPS), (9 * MAPS) ** -0.5, 0.75)
    d_learned = normal_values(keys[11], (SEQS, LEARNED_SEQ, D), 1.0, 6.0, ((0, 2), (1, 16)))
    return {"tokens": tokens, "segments": segments, "g_attn": g_attn, "w_qkv": w_qkv, "w_out": w_out, "g_mlp": g_mlp, "w_up": w_up, "w_down": w_down, "g_learn": g_learn, "conv_first": conv_first, "conv_rest": conv_rest, "d_learned": d_learned}


@jax.custom_vjp
def low(v):
    return lax.optimization_barrier(v.astype(jnp.bfloat16)).astype(jnp.float32)

@jax.custom_vjp
def low_back(v):
    return v

def low_keep(v):
    return (low(v), None)

def low_pass(kept, grad):
    return (grad,)

def back_keep(v):
    return (v, None)

def back_low(kept, grad):
    return (low(grad),)
low.defvjp(low_keep, low_pass)
low_back.defvjp(back_keep, back_low)

def matmul_hi(left, right):
    return jnp.dot(left, right, preferred_element_type=jnp.float32, precision=lax.Precision.HIGHEST)

def layer_norm(values, gain):
    average = lax.optimization_barrier(jnp.mean(values, axis=-1, keepdims=True))
    centered = values - average
    variance = lax.optimization_barrier(jnp.mean(centered * centered, axis=-1, keepdims=True))
    return centered * lax.rsqrt(variance + 1e-06) * gain

def gelu_tanh(values):
    return 0.5 * values * (1.0 + jnp.tanh(0.7978845608028654 * (values + 0.044715 * values * values * values)))

def conv_grid(field, weight):
    grid_side = field.shape[1]
    padded = jnp.pad(field, ((0, 0), (1, 1), (1, 1), (0, 0)))
    result = jnp.zeros(field.shape[:3] + (weight.shape[0],), jnp.float32)
    for shift_row in range(3):
        for shift_col in range(3):
            window = padded[:, shift_row:shift_row + grid_side, shift_col:shift_col + grid_side, :]
            result = result + jnp.einsum('fxyc,oc->fxyo', window, weight[:, shift_row, shift_col, :], precision=lax.Precision.HIGHEST)
    return result

def map_tail(first_out, conv_rest, frames):
    current = first_out
    for layer_idx in range(3):
        current = conv_grid(gelu_tanh(current), conv_rest[layer_idx])
    map_weights = 1.0 / (1.0 + jnp.exp(-current))
    cell_count = frames.shape[1] * frames.shape[2]
    pooled = jnp.einsum('fxym,fxyd->fmd', map_weights, frames, precision=lax.Precision.HIGHEST) / cell_count
    return pooled.reshape(-1, frames.shape[3])

def sequence_forward(inputs, seg_ids, g_attn, w_qkv, w_out, g_mlp, w_up, w_down, g_learn, conv_first, conv_rest):
    length = inputs.shape[0]
    hidden_one = low(layer_norm(inputs, g_attn))
    projected = matmul_hi(hidden_one, w_qkv)
    queries = low_back(low(projected[:, :D])).reshape(length, HEADS, HEAD_DIM)
    key_rows = low_back(low(projected[:, D:2 * D])).reshape(length, HEADS, HEAD_DIM)
    value_rows = low_back(low(projected[:, 2 * D:])).reshape(length, HEADS, HEAD_DIM)
    block_len = 4 * FRAME_TOKENS
    query_blocks = queries.reshape(length // block_len, block_len, HEADS, HEAD_DIM)
    seg_blocks = seg_ids.reshape(length // block_len, block_len)

    def attend(pair):
        query_block, seg_block = pair
        scores = jnp.einsum('qhd,khd->hqk', query_block, key_rows, precision=lax.Precision.HIGHEST) * HEAD_DIM ** (-0.5)
        scores = low_back(scores)
        allowed = seg_block[:, None] == seg_ids[None, :]
        scores = jnp.where(allowed[None], scores, -1e+30)
        row_max = lax.optimization_barrier(jnp.max(scores, axis=-1, keepdims=True))
        expon = jnp.exp(scores - row_max)
        attn_prob = expon / lax.optimization_barrier(jnp.sum(expon, axis=-1, keepdims=True))
        return jnp.einsum('hqk,khd->qhd', low(attn_prob), value_rows, precision=lax.Precision.HIGHEST)
    mixed = lax.map(jax.checkpoint(attend), (query_blocks, seg_blocks)).reshape(length, D)
    attended = low_back(low(mixed))
    after_attn = inputs + low_back(matmul_hi(attended, w_out))
    hidden_two = low(layer_norm(after_attn, g_mlp))
    pre_act = low_back(matmul_hi(hidden_two, w_up))
    activated = low(gelu_tanh(pre_act))
    block_out = after_attn + low_back(matmul_hi(activated, w_down))
    frames = block_out.reshape(FRAMES, GRID, GRID, D)
    hidden_three = low(layer_norm(frames, g_learn))
    first_out = low_back(conv_grid(hidden_three, conv_first))
    return map_tail(first_out, conv_rest, frames)

def reference(tokens, segments, g_attn, w_qkv, w_out, g_mlp, w_up, w_down, g_learn, conv_first, conv_rest, d_learned):

    def forward(inputs, gain_a, weight_qkv, weight_out, gain_m, weight_up, weight_down, gain_l, conv_one, conv_more):

        def one_sequence(pair):
            return sequence_forward(pair[0], pair[1], gain_a, weight_qkv, weight_out, gain_m, weight_up, weight_down, gain_l, conv_one, conv_more)
        return lax.map(jax.checkpoint(one_sequence), (inputs, segments))
    learned, pullback = jax.vjp(forward, tokens.astype(jnp.float32), g_attn.astype(jnp.float32), w_qkv.astype(jnp.float32), w_out.astype(jnp.float32), g_mlp.astype(jnp.float32), w_up.astype(jnp.float32), w_down.astype(jnp.float32), g_learn.astype(jnp.float32), conv_first.astype(jnp.float32), conv_rest.astype(jnp.float32))
    grads = pullback(d_learned.astype(jnp.float32))
    return (learned.astype(jnp.bfloat16), grads[0], grads[1], grads[2], grads[3], grads[4], grads[5], grads[6], grads[7], grads[8], grads[9])
```

```python
import functools

import jax
import jax.numpy as jnp
import numpy as np
from jax import lax
from jax.experimental import pallas as pl
from jax.experimental.pallas import tpu as pltpu
from jax.sharding import PartitionSpec as P

HEADS = 6
HEAD_DIM = 64
MAPS = 8
GRID = 14
CELLS = GRID * GRID
PAIRS = HEADS // 2
WIDE = 512
BIG = 1e30
LSE0 = 4
DEL0 = 4 + 3 * HEADS
AUG_END = 4 + 6 * HEADS
F32 = jnp.float32
BF16 = jnp.bfloat16
HIGH = lax.Precision.HIGHEST
MESH = pl.DeviceIdType.MESH
VMEM = pltpu.VMEM
MIB = 1 << 20


def nn(a, b, precision=None):
    return lax.dot_general(a, b, (((1,), (0,)), ((), ())), precision=precision, preferred_element_type=F32)


def nt(a, b, precision=None):
    return lax.dot_general(a, b, (((1,), (1,)), ((), ())), precision=precision, preferred_element_type=F32)


def tn(a, b, precision=None):
    return lax.dot_general(a, b, (((0,), (0,)), ((), ())), precision=precision, preferred_element_type=F32)


def iota(shape, dim):
    return lax.broadcasted_iota(jnp.int32, shape, dim)


def sixteen(v):
    return jnp.concatenate([v, jnp.zeros((8, v.shape[1]), v.dtype)], axis=0)


def normed(x):
    centered = x - jnp.mean(x, axis=-1, keepdims=True)
    rstd = lax.rsqrt(jnp.mean(centered * centered, axis=-1, keepdims=True) + 1e-06)
    return centered * rstd, rstd


def norm_back(vhat, rstd, dout, gain):
    e = dout * gain
    mean_e = jnp.mean(e, axis=-1, keepdims=True)
    mean_ev = jnp.mean(e * vhat, axis=-1, keepdims=True)
    return rstd * (e - mean_e - vhat * mean_ev), jnp.sum(dout * vhat, axis=0, keepdims=True)


C0 = 0.7978845608028654
C1 = 0.044715


def gelu(u):
    return 0.5 * u * (1.0 + jnp.tanh(C0 * (u + C1 * u * u * u)))


def gelu_grad(u):
    t = jnp.tanh(C0 * (u + C1 * u * u * u))
    return 0.5 * (1.0 + t) + 0.5 * u * (1.0 - t * t) * (C0 + (3.0 * C0 * C1) * u * u)


def flip(v, b):
    return v + b * (1 - 2 * ((v // b) % 2))


def bit_of(v, b):
    return (v // b) % 2


def rc(src, dst, send, recv, dev):
    return pltpu.make_async_remote_copy(
        src_ref=src, dst_ref=dst, send_sem=send, recv_sem=recv, device_id=dev, device_id_type=MESH
    )


def greet(partners):
    barrier = pltpu.get_barrier_semaphore()
    for dev in partners:
        pl.semaphore_signal(barrier, inc=1, device_id=dev, device_id_type=MESH)
    pl.semaphore_wait(barrier, len(partners))


def gather_half(half, own_slots, slot_ref, send, recv, fi, si, counter):
    g = fi % half
    other_bits = []
    b = 2
    while b < half:
        other_bits.append(b)
        b *= 2
    n = len(other_bits)
    parts = []
    for k, (base, ready) in enumerate(own_slots):
        order = other_bits[k % n :] + other_bits[: k % n] if n else []
        parts.append((base, ready, order))
    sends = []

    def push(slot, bit):
        k = counter[0]
        counter[0] += 1
        ref = slot_ref(slot)
        cp = rc(ref, ref, send.at[k], recv.at[slot], (flip(fi, bit), si))
        cp.start()
        sends.append(cp)

    def wait_slot(slot):
        ref = slot_ref(slot)
        rc(ref, ref, send.at[0], recv.at[slot], (flip(fi, 1), si)).wait_recv()

    arrived = []
    for base, ready, order in parts:
        if ready is not None:
            ready()
        for bit in order:
            push(base + g, bit)
        push(base + g, 1)
    for step in range(n):
        for base, _, order in parts:
            have = [g]
            for bit in order[:step]:
                have = have + [flip(h, bit) for h in have]
            new = [flip(h, order[step]) for h in have]
            for slot in new:
                wait_slot(base + slot)
                for bit in order[step + 1 :]:
                    push(base + slot, bit)
                push(base + slot, 1)
    for base, _, order in parts:
        have = [g]
        for bit in order:
            have = have + [flip(h, bit) for h in have]
        for h in have:
            wait_slot(base + flip(h, 1))
    for cp in sends:
        cp.wait_send()


def half_partners(half, fi, si):
    out = []
    b = 1
    while b < half:
        out.append((flip(fi, b), si))
        b *= 2
    return out


def token_gather_kernel(frames, cells, tokens, segments, d_learned, xg_ref, xp_ref, slots, send, recv):
    half = frames // 2
    fi = lax.axis_index("frame")
    si = lax.axis_index("seq")
    mine = fi // half
    partner = (fi + half * (1 - 2 * mine), si)
    rows, width = xp_ref.shape[1:]
    for k in range(2):
        body = tokens[k].astype(F32)[0:cells]
        seg = jnp.broadcast_to(segments[k : k + 1, 0:1].astype(F32), (1, width))
        dl = d_learned[k]
        pad = jnp.zeros((rows - body.shape[0] - 1 - MAPS, width), F32)
        xp_ref[k] = jnp.concatenate([body, seg, dl, pad], axis=0).astype(BF16)
    greet(half_partners(half, fi, si) + [partner])
    counter = [1]
    cp = rc(xp_ref.at[1 - mine], slots.at[fi], send.at[0], recv.at[fi], partner)
    cp.start()
    slots[fi] = xp_ref[mine]

    def partner_here():
        slot = fi + half * (1 - 2 * mine)
        rc(slots.at[slot], slots.at[slot], send.at[0], recv.at[slot], partner).wait_recv()

    gather_half(
        half,
        [(half * mine, None), (half * (1 - mine), partner_here)],
        lambda s: slots.at[s],
        send,
        recv,
        fi,
        si,
        counter,
    )
    cp.wait_send()
    xg_ref[...] = slots[...]


def da_gather_kernel(frames, rows, da_ref, dag_ref, slots, send, recv):
    half = frames // 2
    fi = lax.axis_index("frame")
    si = lax.axis_index("seq")
    greet(half_partners(half, fi, si))
    g = fi % half
    slots[:, pl.ds(pl.multiple_of(g * rows, rows), rows), :] = da_ref[:, :rows, :]
    slots[:, pl.ds(pl.multiple_of((g + half) * rows, rows), rows), :] = da_ref[:, rows:, :]
    gather_half(
        half,
        [(0, None), (half, None)],
        lambda s: slots.at[:, pl.ds(pl.multiple_of(s * rows, rows), rows), :],
        send,
        recv,
        fi,
        si,
        [0],
    )
    dag_ref[...] = slots[...]


def aug_masks(h):
    lane = iota((1, 128), 1)
    seg = lane < 4
    lse = seg | ((lane >= LSE0 + 3 * h) & (lane < LSE0 + 3 * h + 3))
    dlt = (lane >= DEL0 + 3 * h) & (lane < DEL0 + 3 * h + 3)
    return lse.astype(F32).astype(BF16), dlt.astype(F32).astype(BF16)


def pieces(value, which):
    hi = value.astype(BF16).astype(F32)
    rest = value - hi
    mid = rest.astype(BF16).astype(F32)
    low = rest - mid
    return jnp.where(which == 0, hi, jnp.where(which == 1, mid, low))


def half_masks():
    lane = iota((1, 128), 1)
    first = (lane < HEAD_DIM).astype(F32).astype(BF16)
    return first, (lane >= HEAD_DIM).astype(F32).astype(BF16)


def layer_kernel(
    frames,
    rows,
    cells,
    xg,
    g_attn,
    w_qkv,
    w_out,
    g_mlp,
    w_up,
    w_down,
    g_learn,
    first9,
    rest27,
    tapmask,
    blockones,
    qkv,
    augk,
    da_ext,
    dx2_ref,
    learned,
    grads,
    augq,
    o_scr,
    x2_scr,
    y_scr,
    vhat2_scr,
    vhat3_scr,
    rstd2_scr,
    rstd3_scr,
    dh2_scr,
    u_scr,
    hid_scr,
    h2_scr,
    a_scr,
    dm_scr,
    h3p,
    yp,
    dyp,
    w72_scr,
    spread_scr,
    rest_scr,
    gain_scr,
    conv_bw,
    conv_fw,
):
    fi = lax.axis_index("frame")
    half = frames // 2
    g = fi % half
    own = 2 * rows
    lane128 = iota((rows, 128), 1)
    row128 = iota((rows, 128), 0)
    valid_row = row128 < cells

    w72 = first9[...].reshape(72, 384)
    w72_scr[...] = sixteen(w72).astype(BF16)
    square_r, square_c = iota((128, 128), 0), iota((128, 128), 1)
    repeat = ((square_c & 7) == square_r).astype(F32)
    same_tap = (((square_r >> 3) == (square_c >> 3)) & (square_r < 72)).astype(F32)
    for layer in range(3):
        by_tap = rest27[9 * layer : 9 * layer + 9].reshape(72, MAPS)
        by_tap = jnp.concatenate([by_tap, jnp.zeros((72, 120), F32)], axis=1)
        conv_bw[layer] = sixteen(by_tap)
        by_tap = jnp.concatenate([by_tap, jnp.zeros((56, 128), F32)], axis=0)
        conv_fw[layer] = nn(repeat[0:16], nn(by_tap, repeat, HIGH) * same_tap, HIGH)

    def project(f, carry):
        x = xg[f].astype(F32)
        seg = x[cells : cells + 1, 0:128]
        x = jnp.where(iota(x.shape, 0) < cells, x, 0.0)
        vhat, _ = normed(x)
        h1 = (vhat * g_attn[...].reshape(1, -1)).astype(BF16)
        base = pl.multiple_of(f * rows, rows)
        whole = nn(h1, w_qkv[...])
        for b in range(9):
            part = whole[:, 128 * b : 128 * b + 128]
            if b < 3:
                part = part * HEAD_DIM**-0.5
            qkv[b, pl.ds(base, rows), :] = part.astype(BF16)
        same = (lane128.astype(F32) == seg) & valid_row
        augk[pl.ds(base, rows), :] = jnp.where(
            lane128 < 4, jnp.where(same, 0.0, -BIG), jnp.where(lane128 < AUG_END, -1.0, 0.0)
        ).astype(BF16)
        return carry

    lax.fori_loop(0, frames, project, 0)

    first, second = half_masks()
    ones = jnp.ones((frames * rows, 128), BF16)

    for k in range(2):
        f = g + half * k
        seg = xg[f].astype(F32)[cells : cells + 1, 0:128]
        same = (lane128.astype(F32) == seg) & valid_row & (lane128 < 4)
        augq[k * rows : (k + 1) * rows, :] = same.astype(F32)

    def attend(step, carry):
        p = step // 2
        k = step % 2
        f = g + half * k
        q = qkv[p, pl.ds(pl.multiple_of(f * rows, rows), rows), :]
        mine = pl.ds(pl.multiple_of(k * rows, rows), rows)
        aug = augq[mine, :]
        seg_aug = jnp.where(lane128 < 4, aug, 0.0).astype(BF16)
        keys = jnp.concatenate([qkv[3 + p], augk[...]], axis=1)
        values = jnp.concatenate([qkv[6 + p], ones], axis=1)
        outs = []
        for e, keep in enumerate((first, second)):
            s = nt(jnp.concatenate([q * keep, seg_aug], axis=1), keys)
            top = jnp.max(s, axis=1, keepdims=True)
            prob = jnp.exp(s - top).astype(BF16)
            o = nn(prob, values)
            total = o[:, 128:]
            outs.append(o[:, :128] / total)
            lse = top + jnp.log(total)
            lane0 = LSE0 + 3 * (2 * p + e)
            which = lane128 - lane0
            aug = jnp.where((which >= 0) & (which < 3), pieces(lse, which), aug)
        augq[mine, :] = aug
        o_scr[p, mine, :] = jnp.where(lane128 < HEAD_DIM, outs[0], outs[1])
        return carry

    lax.fori_loop(0, 2 * PAIRS, attend, 0)

    def apart(fn):
        pl.when(fi >= 0)(fn)

    @apart
    def _():
        a = jnp.concatenate([o_scr[p].astype(BF16) for p in range(PAIRS)], axis=1)
        a_scr[...] = a
        both = jnp.concatenate([xg[g], xg[g + half]], axis=0).astype(F32)
        r = iota(both.shape, 0)
        x = jnp.where((r < cells) | ((r >= rows) & (r < rows + cells)), both, 0.0)
        x2 = x + nn(a, w_out[...])
        x2_scr[...] = x2
        y_scr[...] = x2
        vhat, rstd = normed(x2)
        rstd2_scr[...] = jnp.broadcast_to(rstd, (own, 128))
        vhat2_scr[...] = vhat
        h2_scr[...] = (vhat * g_mlp[...].reshape(1, -1)).astype(BF16)

    def mlp(j, carry):
        cols = pl.ds(pl.multiple_of(384 * j, 384), 384)
        u = nn(h2_scr[...], w_up[:, cols])
        u_scr[j] = u
        hid = gelu(u).astype(BF16)
        hid_scr[j] = hid
        y_scr[...] += nn(hid, w_down[cols, :])
        return carry

    lax.fori_loop(0, 4, mlp, 0)

    @apart
    def _():
        y = y_scr[...]
        vhat, rstd = normed(y)
        vhat3_scr[...] = vhat
        rstd3_scr[...] = jnp.broadcast_to(rstd, (own, 128))
        h3 = (vhat * g_learn[...].reshape(1, -1)).astype(BF16)
        for k in range(2):
            yp[256 * k : 256 * k + rows, :] = y[k * rows : (k + 1) * rows, :]
            yp[256 * k + rows : 256 * k + 256, :] = jnp.zeros((256 - rows, 384), F32)
            h3p[256 * k : 256 * k + rows, :] = h3[k * rows : (k + 1) * rows, :]
            h3p[256 * k + rows : 256 * k + 256, :] = jnp.zeros((256 - rows, 384), BF16)

    def shift_of(t):
        return GRID * (t // 3 - 1) + (t % 3 - 1)

    def moved(v, s):
        return v if s == 0 else pltpu.roll(v, (-s) % WIDE, 1)

    def tap(t):
        return tapmask[t : t + 1, :]

    def im2col(v):
        parts = [moved(v, shift_of(t)) * tap(t) for t in range(9)]
        return jnp.concatenate(parts + [jnp.zeros((56, WIDE), F32)], axis=0)

    def spread_of(v):
        return jnp.concatenate([moved(v, -shift_of(t)) * tap(8 - t) for t in range(9)], axis=0)

    @apart
    def _():
        taps = nt(w72_scr[...], h3p[...])
        z1 = jnp.zeros((MAPS, WIDE), F32)
        for t in range(9):
            z1 = z1 + moved(taps[8 * t : 8 * t + 8, :], shift_of(t)) * tap(t)
        zs = [z1]
        cols_of = []
        for layer in range(3):
            col = im2col(gelu(zs[-1]))
            cols_of.append(col)
            zs.append(nn(conv_fw[layer], col, HIGH)[0:MAPS])
        maps = tap(4) / (1.0 + jnp.exp(-zs[3]))
        dmaps = []
        for k in range(2):
            f = g + half * k
            dl = xg[f].astype(F32)[cells + 1 : cells + 1 + MAPS, :] * (1.0 / cells)
            dl = sixteen(dl)
            mk = sixteen(maps[:, 256 * k : 256 * k + 256])
            yk = yp[256 * k : 256 * k + 256, :]
            learned[k] = nn(mk, yk, HIGH)[0:MAPS] * (1.0 / cells)
            dmaps.append(nt(dl, yk, HIGH)[0:MAPS])
            dyp[256 * k : 256 * k + 256, :] = tn(mk, dl, HIGH)
        dz = jnp.concatenate(dmaps, axis=1) * maps * (1.0 - maps)
        small = []
        for layer in (2, 1, 0):
            dw = nt(sixteen(dz), cols_of[layer], HIGH)[0:MAPS]
            small.insert(0, jnp.concatenate([dw, jnp.zeros((MAPS, 256), F32)], axis=1))
            dz = tn(conv_bw[layer], sixteen(spread_of(dz)), HIGH)[0:MAPS] * gelu_grad(zs[layer])
        dz = dz.astype(BF16).astype(F32) * tap(4)
        spread_scr[...] = sixteen(spread_of(dz)).astype(BF16)
        rest_scr[...] = jnp.concatenate(small + [jnp.zeros((8, 384), F32)], axis=0)

    @apart
    def _():
        dh3 = tn(spread_scr[...], w72_scr[...])
        dh3 = jnp.concatenate([dh3[0:rows], dh3[256 : 256 + rows]], axis=0)
        dy, dg3 = norm_back(vhat3_scr[...], rstd3_scr[:, 0:1], dh3, g_learn[...].reshape(1, -1))
        dy = dy + jnp.concatenate([dyp[0:rows, :], dyp[256 : 256 + rows, :]], axis=0)
        y_scr[...] = dy
        dm_scr[...] = dy.astype(BF16)
        dh2_scr[...] = jnp.zeros((own, 384), F32)
        gain_scr[...] = jnp.concatenate([dg3, jnp.zeros((7, 384), F32)], axis=0)

    def mlp_back(j, carry):
        cols = pl.ds(pl.multiple_of(384 * j, 384), 384)
        dm = dm_scr[...]
        du = (nt(dm, w_down[cols, :]) * gelu_grad(u_scr[j])).astype(BF16)
        grads[cols, :] = tn(h2_scr[...], du).astype(BF16)
        grads[pl.ds(pl.multiple_of(1536 + 384 * j, 384), 384), :] = tn(hid_scr[j], dm).astype(BF16)
        dh2_scr[...] += nt(du, w_up[:, cols])
        return carry

    lax.fori_loop(0, 4, mlp_back, 0)

    @apart
    def _():
        dx2, dg2 = norm_back(vhat2_scr[...], rstd2_scr[:, 0:1], dh2_scr[...], g_mlp[...].reshape(1, -1))
        dx2 = dx2 + y_scr[...]
        dx2_ref[...] = dx2
        dm_scr[...] = dx2.astype(BF16)
        gains = jnp.concatenate([dg2, gain_scr[0:1, :], jnp.zeros((6, 384), F32)], axis=0)
        d_first = nn(spread_scr[...], h3p[...])[0:72]
        small = [d_first, gains, rest_scr[...], jnp.zeros((16, 384), F32)]
        grads[3456:3584, :] = jnp.concatenate(small, axis=0).astype(BF16)

    @apart
    def _():
        dzz = dm_scr[...]
        grads[3072:3456, :] = tn(a_scr[...], dzz).astype(BF16)
        da = nt(dzz, w_out[...]).astype(BF16)
        prod = jnp.concatenate([o_scr[p] for p in range(PAIRS)], axis=1) * da.astype(F32)
        lane = iota((own, 128), 1)
        which = lane - DEL0
        which = which - 3 * (which // 3)
        delta = pieces(nn(prod, blockones[...], HIGH), which)
        full = jnp.where((lane >= DEL0) & (lane < AUG_END), delta, augq[...])
        for p in range(PAIRS):
            da_ext[p] = da[:, 128 * p : 128 * p + 128]
        da_ext[PAIRS] = full.astype(BF16)


def grad_pass(own_a, own_b, own_aug, all_a, all_b, all_aug, p, total, chunk, with_b):
    rows = own_a.shape[0]
    masks = half_masks()
    left_a, left_b = [], []
    for e in range(2):
        lse_mask, del_mask = aug_masks(2 * p + e)
        left_a.append(jnp.concatenate([own_a * masks[e], own_aug * lse_mask], axis=1))
        left_b.append(jnp.concatenate([own_b * masks[e], own_aug * del_mask], axis=1))

    def body(c, carry):
        here = pl.ds(pl.multiple_of(c * chunk, chunk), chunk)
        ra, rb, aug = all_a(here), all_b(here), all_aug(here)
        right_a = jnp.concatenate([ra, aug], axis=1)
        right_b = jnp.concatenate([rb, aug], axis=1)
        probs = [jnp.exp(nt(left_a[e], right_a)) for e in range(2)]
        ds = [(probs[e] * nt(left_b[e], right_b)).astype(BF16) for e in range(2)]
        new = [carry[0] + nn(jnp.concatenate(ds, axis=1), jnp.concatenate([ra * m for m in masks], axis=0))]
        if with_b:
            both = jnp.concatenate([prob.astype(BF16) for prob in probs], axis=1)
            new.append(carry[1] + nn(both, jnp.concatenate([rb * m for m in masks], axis=0)))
        return tuple(new)

    zero = tuple(jnp.zeros((rows, 128), F32) for _ in range(2 if with_b else 1))
    out = lax.fori_loop(0, total // chunk, body, zero, unroll=True)
    return out if with_b else out[0]


def back_kernel(
    frames, rows, cells, qkv, augk, da_ext, dag, dx2, xg, g_attn, w_qkv, learned, dtok, grads, dqkv
):
    fi = lax.axis_index("frame")
    half = frames // 2
    g = fi % half
    total = frames * rows

    def mine(ref, b):
        at = [ref[b, pl.ds(pl.multiple_of((g + half * k) * rows, rows), rows), :] for k in range(2)]
        return jnp.concatenate(at, axis=0)

    own_augk = jnp.concatenate(
        [augk[pl.ds(pl.multiple_of((g + half * k) * rows, rows), rows), :] for k in range(2)], axis=0
    )

    def query_pass(p, carry):
        dq = grad_pass(
            mine(qkv, p), da_ext[p], da_ext[PAIRS],
            lambda i: qkv[3 + p, i, :], lambda i: qkv[6 + p, i, :], lambda i: augk[i, :],
            p, total, 256, False,
        )
        dqkv[p] = (dq * HEAD_DIM**-0.5).astype(BF16)
        return carry

    lax.fori_loop(0, PAIRS, query_pass, 0)

    def key_pass(p, carry):
        dk, dv = grad_pass(
            mine(qkv, 3 + p), mine(qkv, 6 + p), own_augk,
            lambda i: qkv[p, i, :], lambda i: dag[p, i, :], lambda i: dag[PAIRS, i, :],
            p, total, 256, True,
        )
        dqkv[3 + p] = dk.astype(BF16)
        dqkv[6 + p] = dv.astype(BF16)
        return carry

    lax.fori_loop(0, PAIRS, key_pass, 0)

    x = jnp.concatenate([xg[g], xg[g + half]], axis=0).astype(F32)
    r = iota(x.shape, 0)
    x = jnp.where((r < cells) | ((r >= rows) & (r < rows + cells)), x, 0.0)
    vhat, rstd = normed(x)
    h1 = (vhat * g_attn[...].reshape(1, -1)).astype(BF16)
    dh1 = jnp.zeros(x.shape, F32)
    for b in range(3):
        d = jnp.concatenate([dqkv[3 * b + p] for p in range(PAIRS)], axis=1)
        dh1 = dh1 + nt(d, w_qkv[:, 384 * b : 384 * b + 384])
        grads[384 * b : 384 * b + 384, :] = tn(h1, d).astype(BF16)
    dx, dg = norm_back(vhat, rstd, dh1, g_attn[...].reshape(1, -1))
    grads[1152:1168, :] = jnp.concatenate([dg, jnp.zeros((15, 384), F32)], axis=0).astype(BF16)
    grads[1168:1536, :] = jnp.zeros((368, 384), BF16)
    dx = dx + dx2[...]
    for k in range(2):
        dtok[k, 0:cells, :] = dx[k * rows : k * rows + cells, :]
        tail = jnp.concatenate([learned[k], jnp.zeros((rows - cells - MAPS, 384), F32)], axis=0)
        dtok[k, cells:rows, :] = tail


def mesh_bits(frames, seqs):
    rest = []
    b = 1
    while b < seqs:
        rest.append(("seq", b))
        b *= 2
    b = 2
    while b < frames:
        rest.append(("frame", b))
        b *= 2
    return rest


def neighbour(axis, bit, fi, si):
    return (flip(fi, bit), si) if axis == "frame" else (fi, flip(si, bit))


def coord(axis, bit, fi, si):
    return bit_of(fi, bit) if axis == "frame" else bit_of(si, bit)


CH = 16


def sum_kernel(frames, seqs, rows, cells, early, late, dtok, early_out, late_out, dtok_out, learned_out, buf, land, out, tok_send, tok_land, send, recv, tsem):
    fi = lax.axis_index("frame")
    si = lax.axis_index("seq")
    half = frames // 2
    mine = fi // half
    partner = (fi + half * (1 - 2 * mine), si)
    rest = mesh_bits(frames, seqs)
    everyone = [("frame", 1)] + rest
    greet([neighbour(a, b, fi, si) for a, b in everyone])
    tok_send[...] = dtok[1 - mine].astype(BF16)
    tok_copy = rc(tok_send, tok_land, tsem.at[0], tsem.at[1], partner)
    tok_copy.start()
    n_early = early.shape[0]
    buf[0:n_early, :] = early[...]
    buf[n_early:, :] = late[...]
    third = 1536
    plan = []
    starts = [(0, third), (third, third), (2 * third, 512), (n_early, 1536)]
    for k, (start, length) in enumerate(starts):
        r = k % len(rest)
        plan.append((start, length, [("frame", 1)] + rest[r:] + rest[:r]))
    steps = len(everyone)
    halvings = min(5, steps)
    state = []
    at = 0
    for start, length, order in plan:
        state.append({"seg": start, "len": length, "land": at, "order": order, "hist": []})
        at += length + (steps - halvings) * (length >> halvings)
    sem = [0]

    def next_sem():
        sem[0] += 1
        return sem[0] - 1

    def ds(start, n):
        return pl.ds(pl.multiple_of(start, CH), n)

    for step in range(steps):
        flying = []
        for st in state:
            axis, bit = st["order"][step]
            c = coord(axis, bit, fi, si)
            k = next_sem()
            if step < halvings:
                n = st["len"] // 2
                keep, give = st["seg"] + c * n, st["seg"] + (1 - c) * n
            else:
                n = st["len"]
                keep = give = st["seg"]
            cp = rc(buf.at[ds(give, n), :], land.at[pl.ds(st["land"], n), :], send.at[k], recv.at[k], neighbour(axis, bit, fi, si))
            cp.start()
            flying.append((cp, keep, n))
        for st, (cp, keep, n) in zip(state, flying):
            cp.wait()
            at = st["land"]

            def add(i, carry, keep=keep, at=at):
                there = ds(keep + i * CH, CH)
                buf[there, :] = (buf[there, :].astype(F32) + land[ds(at + i * CH, CH), :].astype(F32)).astype(BF16)
                return carry

            lax.fori_loop(0, n // CH, add, 0)
            st["hist"].append((st["seg"], st["len"]))
            st["seg"], st["len"], st["land"] = keep, n, at + n
    for st in state:
        out[ds(st["seg"], st["len"]), :] = buf[ds(st["seg"], st["len"]), :]
    for step in reversed(range(halvings)):
        flying = []
        for st in state:
            axis, bit = st["order"][step]
            k = next_sem()
            there = out.at[ds(st["seg"], st["len"]), :]
            cp = rc(there, there, send.at[k], recv.at[k], neighbour(axis, bit, fi, si))
            cp.start()
            flying.append(cp)
        for st, cp in zip(state, flying):
            cp.wait()
            st["seg"], st["len"] = st["hist"][step]
    early_out[...] = out[0:n_early, :].astype(F32)
    late_out[...] = out[n_early:, :].astype(F32)
    tok_copy.wait()
    far = tok_land[...].astype(F32)
    dtok_out[mine] = dtok[mine][0:cells, :]
    dtok_out[1 - mine] = far[0:cells, :]
    learned_out[mine] = dtok[mine][cells : cells + MAPS, :]
    learned_out[1 - mine] = far[cells : cells + MAPS, :]


def vspec(n):
    return [pl.BlockSpec(memory_space=VMEM)] * n


def params(collective=None, mib=56):
    if collective is None:
        return pltpu.CompilerParams(vmem_limit_bytes=mib * MIB)
    return pltpu.CompilerParams(collective_id=collective, has_side_effects=True, vmem_limit_bytes=mib * MIB)


def tap_masks():
    p = np.arange(WIDE) % 256
    px, py = p // GRID, p % GRID
    out = np.zeros((16, WIDE), np.float32)
    for t in range(9):
        r, c = t // 3 - 1, t % 3 - 1
        out[t] = (p < CELLS) & (px + r >= 0) & (px + r < GRID) & (py + c >= 0) & (py + c < GRID)
    return out


def head_sums():
    out = np.zeros((HEADS * HEAD_DIM, 128), np.float32)
    for h in range(HEADS):
        out[h * HEAD_DIM : (h + 1) * HEAD_DIM, DEL0 + 3 * h : DEL0 + 3 * h + 3] = 1.0
    return out


def on_device(frames, seqs, tokens, segments, g_attn, w_qkv, w_out, g_mlp, w_up, w_down, g_learn, conv_first, conv_rest, d_learned):
    _, cells, width = tokens.shape
    rows = -(-(cells + 1 + MAPS) // 16) * 16
    own = 2 * rows
    total = frames * rows
    n_sems = 1 + 2 * frames * 4
    sds = jax.ShapeDtypeStruct
    xg = pl.pallas_call(
        functools.partial(token_gather_kernel, frames, cells),
        out_shape=sds((frames, rows, width), BF16),
        in_specs=vspec(3),
        out_specs=vspec(1)[0],
        scratch_shapes=[
            VMEM((2, rows, width), BF16),
            VMEM((frames, rows, width), BF16),
            pltpu.SemaphoreType.DMA((n_sems,)),
            pltpu.SemaphoreType.DMA((frames,)),
        ],
        compiler_params=params(0),
        name="tokens_to_half",
    )(jnp.pad(tokens, ((0, 0), (0, rows - cells), (0, 0))), segments, d_learned.astype(F32))
    first9 = conv_first.transpose(1, 2, 0, 3).reshape(9, MAPS, width).astype(F32)
    rest27 = conv_rest.transpose(0, 2, 3, 1, 4).reshape(27, MAPS, MAPS).astype(F32)
    qkv, augk, da_ext, dx2, learned, early = pl.pallas_call(
        functools.partial(layer_kernel, frames, rows, cells),
        out_shape=[
            sds((9, total, 128), BF16),
            sds((total, 128), BF16),
            sds((PAIRS + 1, own, 128), BF16),
            sds((own, width), F32),
            sds((2, MAPS, width), F32),
            sds((3584, width), BF16),
        ],
        in_specs=vspec(12),
        out_specs=vspec(6),
        scratch_shapes=[
            VMEM((own, 128), F32),
            VMEM((PAIRS, own, 128), F32),
            VMEM((own, width), F32),
            VMEM((own, width), F32),
            VMEM((own, width), F32),
            VMEM((own, width), F32),
            VMEM((own, 128), F32),
            VMEM((own, 128), F32),
            VMEM((own, width), F32),
            VMEM((4, own, width), F32),
            VMEM((4, own, width), BF16),
            VMEM((own, width), BF16),
            VMEM((own, width), BF16),
            VMEM((own, width), BF16),
            VMEM((WIDE, width), BF16),
            VMEM((WIDE, width), F32),
            VMEM((WIDE, width), F32),
            VMEM((80, width), BF16),
            VMEM((80, WIDE), BF16),
            VMEM((32, width), F32),
            VMEM((8, width), F32),
            VMEM((3, 80, 128), F32),
            VMEM((3, 16, 128), F32),
        ],
        compiler_params=params(),
        name="layer",
    )(
        xg, g_attn, w_qkv, w_out, g_mlp, w_up, w_down, g_learn, first9, rest27,
        jnp.asarray(tap_masks()), jnp.asarray(head_sums()),
    )
    dag = pl.pallas_call(
        functools.partial(da_gather_kernel, frames, rows),
        out_shape=sds((PAIRS + 1, total, 128), BF16),
        in_specs=vspec(1),
        out_specs=vspec(1)[0],
        scratch_shapes=[
            VMEM((PAIRS + 1, total, 128), BF16),
            pltpu.SemaphoreType.DMA((n_sems,)),
            pltpu.SemaphoreType.DMA((frames,)),
        ],
        compiler_params=params(1),
        name="grads_to_half",
    )(da_ext)
    dtok, late = pl.pallas_call(
        functools.partial(back_kernel, frames, rows, cells),
        out_shape=[sds((2, rows, width), F32), sds((1536, width), BF16)],
        in_specs=vspec(9),
        out_specs=vspec(2),
        scratch_shapes=[VMEM((9, own, 128), BF16)],
        compiler_params=params(),
        name="attention_back",
    )(qkv, augk, da_ext, dag, dx2, xg, g_attn, w_qkv, learned)
    n_all = 3584 + 1536
    early_sum, late_sum, d_tokens, learned_all = pl.pallas_call(
        functools.partial(sum_kernel, frames, seqs, rows, cells),
        out_shape=[
            sds((3584, width), F32),
            sds((1536, width), F32),
            sds((2, cells, width), F32),
            sds((2, MAPS, width), F32),
        ],
        in_specs=vspec(3),
        out_specs=vspec(4),
        scratch_shapes=[
            VMEM((n_all, width), BF16),
            VMEM((n_all + (n_all >> 5) * max(0, len(mesh_bits(frames, seqs)) - 4), width), BF16),
            VMEM((n_all, width), BF16),
            VMEM((rows, width), BF16),
            VMEM((rows, width), BF16),
            pltpu.SemaphoreType.DMA((64,)),
            pltpu.SemaphoreType.DMA((64,)),
            pltpu.SemaphoreType.DMA((2,)),
        ],
        compiler_params=params(2),
        name="sums",
    )(early, late, dtok)
    d_w_up = jnp.concatenate([early_sum[384 * j : 384 * j + 384] for j in range(4)], axis=1)
    d_w_qkv = jnp.concatenate([late_sum[384 * j : 384 * j + 384] for j in range(3)], axis=1)
    d_first = early_sum[3456 : 3456 + 72].reshape(3, 3, MAPS, width).transpose(2, 0, 1, 3)
    d_rest = early_sum[3536 : 3536 + 24, :72].reshape(3, MAPS, 3, 3, MAPS)
    return (
        learned_all.astype(BF16),
        d_tokens,
        late_sum[1152],
        d_w_qkv,
        early_sum[3072:3456],
        early_sum[3528],
        d_w_up,
        early_sum[1536:3072],
        early_sum[3529],
        d_first,
        d_rest,
    )


def solution(mesh):
    frames, seqs = mesh.shape["frame"], mesh.shape["seq"]
    both = P("seq", "frame", None)
    in_specs = (both, P("seq", "frame"), *([P()] * 9), both)
    out_specs = (both, both, *([P()] * 9))
    return jax.shard_map(
        functools.partial(on_device, frames, seqs),
        mesh=mesh,
        in_specs=in_specs,
        out_specs=out_specs,
        check_vma=False,
    )
```

```python
import functools

import jax
import jax.numpy as jnp
import numpy as np
from jax import lax
from jax.experimental import pallas as pl
from jax.experimental.pallas import tpu as pltpu
from jax.sharding import PartitionSpec as P

HEADS = 6
HEAD_DIM = 64
MAPS = 8
GRID = 14
CELLS = GRID * GRID
PAIRS = HEADS // 2
WIDE = 512
BIG = 1e30
LSE0 = 4
DEL0 = 4 + 3 * HEADS
AUG_END = 4 + 6 * HEADS
F32 = jnp.float32
BF16 = jnp.bfloat16
HIGH = lax.Precision.HIGHEST
MESH = pl.DeviceIdType.MESH
VMEM = pltpu.VMEM
MIB = 1 << 20


def nn(a, b, precision=None):
    return lax.dot_general(a, b, (((1,), (0,)), ((), ())), precision=precision, preferred_element_type=F32)


def nt(a, b, precision=None):
    return lax.dot_general(a, b, (((1,), (1,)), ((), ())), precision=precision, preferred_element_type=F32)


def tn(a, b, precision=None):
    return lax.dot_general(a, b, (((0,), (0,)), ((), ())), precision=precision, preferred_element_type=F32)


def iota(shape, dim):
    return lax.broadcasted_iota(jnp.int32, shape, dim)


def sixteen(v):
    return jnp.concatenate([v, jnp.zeros((8, v.shape[1]), v.dtype)], axis=0)


def normed(x):
    centered = x - jnp.mean(x, axis=-1, keepdims=True)
    rstd = lax.rsqrt(jnp.mean(centered * centered, axis=-1, keepdims=True) + 1e-06)
    return centered * rstd, rstd


def norm_back(vhat, rstd, dout, gain):
    e = dout * gain
    mean_e = jnp.mean(e, axis=-1, keepdims=True)
    mean_ev = jnp.mean(e * vhat, axis=-1, keepdims=True)
    return rstd * (e - mean_e - vhat * mean_ev), jnp.sum(dout * vhat, axis=0, keepdims=True)


C0 = 0.7978845608028654
C1 = 0.044715


def gelu(u):
    return 0.5 * u * (1.0 + jnp.tanh(C0 * (u + C1 * u * u * u)))


def gelu_grad(u):
    t = jnp.tanh(C0 * (u + C1 * u * u * u))
    return 0.5 * (1.0 + t) + 0.5 * u * (1.0 - t * t) * (C0 + (3.0 * C0 * C1) * u * u)


def flip(v, b):
    return v + b * (1 - 2 * ((v // b) % 2))


def bit_of(v, b):
    return (v // b) % 2


def rc(src, dst, send, recv, dev):
    return pltpu.make_async_remote_copy(
        src_ref=src, dst_ref=dst, send_sem=send, recv_sem=recv, device_id=dev, device_id_type=MESH
    )


def greet(partners):
    barrier = pltpu.get_barrier_semaphore()
    for dev in partners:
        pl.semaphore_signal(barrier, inc=1, device_id=dev, device_id_type=MESH)
    pl.semaphore_wait(barrier, len(partners))


def gather_half(half, own_slots, slot_ref, send, recv, fi, si, counter):
    g = fi % half
    other_bits = []
    b = 2
    while b < half:
        other_bits.append(b)
        b *= 2
    n = len(other_bits)
    parts = []
    for k, (base, ready) in enumerate(own_slots):
        order = other_bits[k % n :] + other_bits[: k % n] if n else []
        parts.append((base, ready, order))
    sends = []

    def push(slot, bit):
        k = counter[0]
        counter[0] += 1
        ref = slot_ref(slot)
        cp = rc(ref, ref, send.at[k], recv.at[slot], (flip(fi, bit), si))
        cp.start()
        sends.append(cp)

    def wait_slot(slot):
        ref = slot_ref(slot)
        rc(ref, ref, send.at[0], recv.at[slot], (flip(fi, 1), si)).wait_recv()

    arrived = []
    for base, ready, order in parts:
        if ready is not None:
            ready()
        for bit in order:
            push(base + g, bit)
        push(base + g, 1)
    for step in range(n):
        for base, _, order in parts:
            have = [g]
            for bit in order[:step]:
                have = have + [flip(h, bit) for h in have]
            new = [flip(h, order[step]) for h in have]
            for slot in new:
                wait_slot(base + slot)
                for bit in order[step + 1 :]:
                    push(base + slot, bit)
                push(base + slot, 1)
    for base, _, order in parts:
        have = [g]
        for bit in order:
            have = have + [flip(h, bit) for h in have]
        for h in have:
            wait_slot(base + flip(h, 1))
    for cp in sends:
        cp.wait_send()


def half_partners(half, fi, si):
    out = []
    b = 1
    while b < half:
        out.append((flip(fi, b), si))
        b *= 2
    return out


def token_gather_kernel(frames, cells, tokens, segments, d_learned, xg_ref, xp_ref, slots, send, recv):
    half = frames // 2
    fi = lax.axis_index("frame")
    si = lax.axis_index("seq")
    mine = fi // half
    partner = (fi + half * (1 - 2 * mine), si)
    rows, width = xp_ref.shape[1:]
    for k in range(2):
        body = tokens[k].astype(F32)[0:cells]
        seg = jnp.broadcast_to(segments[k : k + 1, 0:1].astype(F32), (1, width))
        dl = d_learned[k]
        pad = jnp.zeros((rows - body.shape[0] - 1 - MAPS, width), F32)
        xp_ref[k] = jnp.concatenate([body, seg, dl, pad], axis=0).astype(BF16)
    greet(half_partners(half, fi, si) + [partner])
    counter = [1]
    cp = rc(xp_ref.at[1 - mine], slots.at[fi], send.at[0], recv.at[fi], partner)
    cp.start()
    slots[fi] = xp_ref[mine]

    def partner_here():
        slot = fi + half * (1 - 2 * mine)
        rc(slots.at[slot], slots.at[slot], send.at[0], recv.at[slot], partner).wait_recv()

    gather_half(
        half,
        [(half * mine, None), (half * (1 - mine), partner_here)],
        lambda s: slots.at[s],
        send,
        recv,
        fi,
        si,
        counter,
    )
    cp.wait_send()
    xg_ref[...] = slots[...]


def staged_gather(half, bases, slot_ref, send, recv, fi, si):
    g = fi % half
    bits = []
    b = 2
    while b < half:
        bits.append(b)
        b *= 2
    n = len(bits)
    count = [0]
    sends = []

    def plan_push(slot, bit):
        count[0] += 1
        return slot, count[0] - 1, (flip(fi, bit), si)

    def copy(slot, k, dev):
        ref = slot_ref(slot)
        return rc(ref, ref, send.at[k], recv.at[slot], dev)

    stages = [[] for _ in range(n + 2)]
    for part, base in enumerate(bases):
        order = bits[part % n :] + bits[: part % n] if n else []
        first = [plan_push(base + g, bit) for bit in order] + [plan_push(base + g, 1)]
        stages[0].append((None, first))
        have = [g]
        for step, bit in enumerate(order):
            new = [flip(h, bit) for h in have]
            for h in new:
                follow = [plan_push(base + h, later) for later in order[step + 1 :]] + [plan_push(base + h, 1)]
                stages[step + 1].append((base + h, follow))
            have = have + new
        for h in have:
            stages[n + 1].append((base + flip(h, 1), []))
    for stage in stages:
        for _, pushes in stage:
            sends.extend(pushes)

    def run(i):
        for slot, pushes in stages[i]:
            if slot is not None:
                copy(slot, 0, (flip(fi, 1), si)).wait_recv()
            for push in pushes:
                copy(*push).start()
        if i == n + 1:
            for push in sends:
                copy(*push).wait_send()

    return run, n + 2


def aug_masks(h):
    lane = iota((1, 128), 1)
    seg = lane < 4
    lse = seg | ((lane >= LSE0 + 3 * h) & (lane < LSE0 + 3 * h + 3))
    dlt = (lane >= DEL0 + 3 * h) & (lane < DEL0 + 3 * h + 3)
    return lse.astype(F32).astype(BF16), dlt.astype(F32).astype(BF16)


def pieces(value, which):
    hi = value.astype(BF16).astype(F32)
    rest = value - hi
    mid = rest.astype(BF16).astype(F32)
    low = rest - mid
    return jnp.where(which == 0, hi, jnp.where(which == 1, mid, low))


def half_masks():
    lane = iota((1, 128), 1)
    first = (lane < HEAD_DIM).astype(F32).astype(BF16)
    return first, (lane >= HEAD_DIM).astype(F32).astype(BF16)


def layer_kernel(
    frames,
    rows,
    cells,
    xg,
    g_attn,
    w_qkv,
    w_out,
    g_mlp,
    w_up,
    w_down,
    g_learn,
    first9,
    rest27,
    tapmask,
    blockones,
    qkv,
    augk,
    da_ext,
    dx2_ref,
    learned,
    grads,
    own_x,
    augq,
    o_scr,
    x2_scr,
    y_scr,
    vhat2_scr,
    vhat3_scr,
    rstd2_scr,
    rstd3_scr,
    dh2_scr,
    u_scr,
    hid_scr,
    h2_scr,
    a_scr,
    dm_scr,
    h3p,
    yp,
    dyp,
    w72_scr,
    spread_scr,
    rest_scr,
    gain_scr,
    conv_bw,
    conv_fw,
):
    fi = lax.axis_index("frame")
    half = frames // 2
    g = fi % half
    own = 2 * rows
    lane128 = iota((rows, 128), 1)
    row128 = iota((rows, 128), 0)
    valid_row = row128 < cells

    w72 = first9[...].reshape(72, 384)
    w72_scr[...] = sixteen(w72).astype(BF16)
    square_r, square_c = iota((128, 128), 0), iota((128, 128), 1)
    repeat = ((square_c & 7) == square_r).astype(F32)
    same_tap = (((square_r >> 3) == (square_c >> 3)) & (square_r < 72)).astype(F32)
    for layer in range(3):
        by_tap = rest27[9 * layer : 9 * layer + 9].reshape(72, MAPS)
        by_tap = jnp.concatenate([by_tap, jnp.zeros((72, 120), F32)], axis=1)
        conv_bw[layer] = sixteen(by_tap)
        by_tap = jnp.concatenate([by_tap, jnp.zeros((56, 128), F32)], axis=0)
        conv_fw[layer] = nn(repeat[0:16], nn(by_tap, repeat, HIGH) * same_tap, HIGH)

    def project(f, carry):
        x = xg[f].astype(F32)
        seg = x[cells : cells + 1, 0:128]
        x = jnp.where(iota(x.shape, 0) < cells, x, 0.0)
        vhat, _ = normed(x)
        h1 = (vhat * g_attn[...].reshape(1, -1)).astype(BF16)
        base = pl.multiple_of(f * rows, rows)
        whole = nn(h1, w_qkv[...])
        for b in range(9):
            part = whole[:, 128 * b : 128 * b + 128]
            if b < 3:
                part = part * HEAD_DIM**-0.5
            qkv[b, pl.ds(base, rows), :] = part.astype(BF16)
        same = (lane128.astype(F32) == seg) & valid_row
        augk[pl.ds(base, rows), :] = jnp.where(
            lane128 < 4, jnp.where(same, 0.0, -BIG), jnp.where(lane128 < AUG_END, -1.0, 0.0)
        ).astype(BF16)
        return carry

    lax.fori_loop(0, frames, project, 0)

    first, second = half_masks()
    ones = jnp.ones((frames * rows, 128), BF16)

    for k in range(2):
        f = g + half * k
        seg = xg[f].astype(F32)[cells : cells + 1, 0:128]
        same = (lane128.astype(F32) == seg) & valid_row & (lane128 < 4)
        augq[k * rows : (k + 1) * rows, :] = same.astype(F32)

    def attend(step, carry):
        p = step // 2
        k = step % 2
        f = g + half * k
        q = qkv[p, pl.ds(pl.multiple_of(f * rows, rows), rows), :]
        mine = pl.ds(pl.multiple_of(k * rows, rows), rows)
        aug = augq[mine, :]
        seg_aug = jnp.where(lane128 < 4, aug, 0.0).astype(BF16)
        keys = jnp.concatenate([qkv[3 + p], augk[...]], axis=1)
        values = jnp.concatenate([qkv[6 + p], ones], axis=1)
        outs = []
        for e, keep in enumerate((first, second)):
            s = nt(jnp.concatenate([q * keep, seg_aug], axis=1), keys)
            top = jnp.max(s, axis=1, keepdims=True)
            prob = jnp.exp(s - top).astype(BF16)
            o = nn(prob, values)
            total = o[:, 128:]
            outs.append(o[:, :128] / total)
            lse = top + jnp.log(total)
            lane0 = LSE0 + 3 * (2 * p + e)
            which = lane128 - lane0
            aug = jnp.where((which >= 0) & (which < 3), pieces(lse, which), aug)
        augq[mine, :] = aug
        o_scr[p, mine, :] = jnp.where(lane128 < HEAD_DIM, outs[0], outs[1])
        return carry

    lax.fori_loop(0, 2 * PAIRS, attend, 0)

    def apart(fn):
        pl.when(fi >= 0)(fn)

    @apart
    def _():
        a = jnp.concatenate([o_scr[p].astype(BF16) for p in range(PAIRS)], axis=1)
        a_scr[...] = a
        own_x[0] = xg[g]
        own_x[1] = xg[g + half]
        both = jnp.concatenate([xg[g], xg[g + half]], axis=0).astype(F32)
        r = iota(both.shape, 0)
        x = jnp.where((r < cells) | ((r >= rows) & (r < rows + cells)), both, 0.0)
        x2 = x + nn(a, w_out[...])
        x2_scr[...] = x2
        y_scr[...] = x2
        vhat, rstd = normed(x2)
        rstd2_scr[...] = jnp.broadcast_to(rstd, (own, 128))
        vhat2_scr[...] = vhat
        h2_scr[...] = (vhat * g_mlp[...].reshape(1, -1)).astype(BF16)

    def mlp(j, carry):
        cols = pl.ds(pl.multiple_of(384 * j, 384), 384)
        u = nn(h2_scr[...], w_up[:, cols])
        u_scr[j] = u
        hid = gelu(u).astype(BF16)
        hid_scr[j] = hid
        y_scr[...] += nn(hid, w_down[cols, :])
        return carry

    lax.fori_loop(0, 4, mlp, 0)

    @apart
    def _():
        y = y_scr[...]
        vhat, rstd = normed(y)
        vhat3_scr[...] = vhat
        rstd3_scr[...] = jnp.broadcast_to(rstd, (own, 128))
        h3 = (vhat * g_learn[...].reshape(1, -1)).astype(BF16)
        for k in range(2):
            yp[256 * k : 256 * k + rows, :] = y[k * rows : (k + 1) * rows, :]
            yp[256 * k + rows : 256 * k + 256, :] = jnp.zeros((256 - rows, 384), F32)
            h3p[256 * k : 256 * k + rows, :] = h3[k * rows : (k + 1) * rows, :]
            h3p[256 * k + rows : 256 * k + 256, :] = jnp.zeros((256 - rows, 384), BF16)

    def shift_of(t):
        return GRID * (t // 3 - 1) + (t % 3 - 1)

    def moved(v, s):
        return v if s == 0 else pltpu.roll(v, (-s) % WIDE, 1)

    def tap(t):
        return tapmask[t : t + 1, :]

    def im2col(v):
        parts = [moved(v, shift_of(t)) * tap(t) for t in range(9)]
        return jnp.concatenate(parts + [jnp.zeros((56, WIDE), F32)], axis=0)

    def spread_of(v):
        return jnp.concatenate([moved(v, -shift_of(t)) * tap(8 - t) for t in range(9)], axis=0)

    @apart
    def _():
        taps = nt(w72_scr[...], h3p[...])
        z1 = jnp.zeros((MAPS, WIDE), F32)
        for t in range(9):
            z1 = z1 + moved(taps[8 * t : 8 * t + 8, :], shift_of(t)) * tap(t)
        zs = [z1]
        cols_of = []
        for layer in range(3):
            col = im2col(gelu(zs[-1]))
            cols_of.append(col)
            zs.append(nn(conv_fw[layer], col, HIGH)[0:MAPS])
        maps = tap(4) / (1.0 + jnp.exp(-zs[3]))
        dmaps = []
        for k in range(2):
            f = g + half * k
            dl = xg[f].astype(F32)[cells + 1 : cells + 1 + MAPS, :] * (1.0 / cells)
            dl = sixteen(dl)
            mk = sixteen(maps[:, 256 * k : 256 * k + 256])
            yk = yp[256 * k : 256 * k + 256, :]
            learned[k] = nn(mk, yk, HIGH)[0:MAPS] * (1.0 / cells)
            dmaps.append(nt(dl, yk, HIGH)[0:MAPS])
            dyp[256 * k : 256 * k + 256, :] = tn(mk, dl, HIGH)
        dz = jnp.concatenate(dmaps, axis=1) * maps * (1.0 - maps)
        small = []
        for layer in (2, 1, 0):
            dw = nt(sixteen(dz), cols_of[layer], HIGH)[0:MAPS]
            small.insert(0, jnp.concatenate([dw, jnp.zeros((MAPS, 256), F32)], axis=1))
            dz = tn(conv_bw[layer], sixteen(spread_of(dz)), HIGH)[0:MAPS] * gelu_grad(zs[layer])
        dz = dz.astype(BF16).astype(F32) * tap(4)
        spread_scr[...] = sixteen(spread_of(dz)).astype(BF16)
        rest_scr[...] = jnp.concatenate(small + [jnp.zeros((8, 384), F32)], axis=0)

    @apart
    def _():
        dh3 = tn(spread_scr[...], w72_scr[...])
        dh3 = jnp.concatenate([dh3[0:rows], dh3[256 : 256 + rows]], axis=0)
        dy, dg3 = norm_back(vhat3_scr[...], rstd3_scr[:, 0:1], dh3, g_learn[...].reshape(1, -1))
        dy = dy + jnp.concatenate([dyp[0:rows, :], dyp[256 : 256 + rows, :]], axis=0)
        y_scr[...] = dy
        dm_scr[...] = dy.astype(BF16)
        dh2_scr[...] = jnp.zeros((own, 384), F32)
        gain_scr[...] = jnp.concatenate([dg3, jnp.zeros((7, 384), F32)], axis=0)

    def mlp_back(j, carry):
        cols = pl.ds(pl.multiple_of(384 * j, 384), 384)
        dm = dm_scr[...]
        du = (nt(dm, w_down[cols, :]) * gelu_grad(u_scr[j])).astype(BF16)
        grads[cols, :] = tn(h2_scr[...], du).astype(BF16)
        grads[pl.ds(pl.multiple_of(1536 + 384 * j, 384), 384), :] = tn(hid_scr[j], dm).astype(BF16)
        dh2_scr[...] += nt(du, w_up[:, cols])
        return carry

    lax.fori_loop(0, 4, mlp_back, 0)

    @apart
    def _():
        dx2, dg2 = norm_back(vhat2_scr[...], rstd2_scr[:, 0:1], dh2_scr[...], g_mlp[...].reshape(1, -1))
        dx2 = dx2 + y_scr[...]
        dx2_ref[...] = dx2
        dm_scr[...] = dx2.astype(BF16)
        gains = jnp.concatenate([dg2, gain_scr[0:1, :], jnp.zeros((6, 384), F32)], axis=0)
        d_first = nn(spread_scr[...], h3p[...])[0:72]
        small = [d_first, gains, rest_scr[...], jnp.zeros((16, 384), F32)]
        grads[3456:3584, :] = jnp.concatenate(small, axis=0).astype(BF16)

    @apart
    def _():
        dzz = dm_scr[...]
        grads[3072:3456, :] = tn(a_scr[...], dzz).astype(BF16)
        da = nt(dzz, w_out[...]).astype(BF16)
        prod = jnp.concatenate([o_scr[p] for p in range(PAIRS)], axis=1) * da.astype(F32)
        lane = iota((own, 128), 1)
        which = lane - DEL0
        which = which - 3 * (which // 3)
        delta = pieces(nn(prod, blockones[...], HIGH), which)
        full = jnp.where((lane >= DEL0) & (lane < AUG_END), delta, augq[...])
        for p in range(PAIRS):
            da_ext[p] = da[:, 128 * p : 128 * p + 128]
        da_ext[PAIRS] = full.astype(BF16)


def grad_pass(own_a, own_b, own_aug, all_a, all_b, all_aug, p, count, split, chunk, with_b, at_point):
    masks = half_masks()
    left_a, left_b = [], []
    for e in range(2):
        lse_mask, del_mask = aug_masks(2 * p + e)
        left_a.append(jnp.concatenate([own_a * masks[e], own_aug * lse_mask], axis=1))
        left_b.append(jnp.concatenate([own_b * masks[e], own_aug * del_mask], axis=1))
    acc = [jnp.zeros((own_a.shape[0], 128), F32) for _ in range(2 if with_b else 1)]
    for c in range(count):
        here = pl.ds(c * chunk, chunk)
        ra, rb, aug = all_a(here), all_b(here), all_aug(here)
        right_a = jnp.concatenate([ra, aug], axis=1)
        right_b = jnp.concatenate([rb, aug], axis=1)
        probs = [jnp.exp(nt(left_a[e], right_a)) for e in range(2)]
        ds = [(probs[e] * nt(left_b[e], right_b)).astype(BF16) for e in range(2)]
        acc[0] = acc[0] + nn(jnp.concatenate(ds, axis=1), jnp.concatenate([ra * m for m in masks], axis=0))
        if with_b:
            both = jnp.concatenate([prob.astype(BF16) for prob in probs], axis=1)
            acc[1] = acc[1] + nn(both, jnp.concatenate([rb * m for m in masks], axis=0))
        if c + 1 == split:
            at_point(0)
    at_point(1)
    return acc if with_b else acc[0]


def mesh_bits(frames, seqs):
    rest = []
    b = 1
    while b < seqs:
        rest.append(("seq", b))
        b *= 2
    b = 2
    while b < frames:
        rest.append(("frame", b))
        b *= 2
    return rest


def neighbour(axis, bit, fi, si):
    return (flip(fi, bit), si) if axis == "frame" else (fi, flip(si, bit))


def coord(axis, bit, fi, si):
    return bit_of(fi, bit) if axis == "frame" else bit_of(si, bit)


TILE = 16


def at_tile(start, n):
    return pl.ds(start if isinstance(start, int) else pl.multiple_of(start, TILE), n)


def landing_rows(length, steps, halvings):
    return length + max(0, steps - halvings) * (length >> halvings)


class Piece:
    def __init__(self, start, length, order, halvings, land_at, sem_at, fi, si, buf, land, out, send, recv):
        self.refs = buf, land, out, send, recv
        self.steps = []
        seg = start
        n = length
        hist = []
        sem = sem_at
        for step, (axis, bit) in enumerate(order):
            dev = neighbour(axis, bit, fi, si)
            if step < halvings:
                hist.append((seg, n, dev))
                c = coord(axis, bit, fi, si)
                n = n // 2
                keep, give = seg + c * n, seg + (1 - c) * n
            else:
                keep = give = seg
            self.steps.append(("add", give, keep, n, land_at, dev, sem))
            seg = keep
            land_at += n
            sem += 1
        self.own = seg, n
        self.adds = len(order)
        for old, old_n, dev in reversed(hist):
            self.steps.append(("copy", seg, seg, n, 0, dev, sem))
            seg, n = old, old_n
            sem += 1
        self.sem_end = sem
        self.land_end = land_at
        self.total = len(self.steps)

    def copy(self, i):
        buf, land, out, send, recv = self.refs
        kind, give, _, n, at, dev, sem = self.steps[i]
        if kind == "add":
            return rc(buf.at[at_tile(give, n), :], land.at[at_tile(at, n), :], send.at[sem], recv.at[sem], dev)
        there = out.at[at_tile(give, n), :]
        return rc(there, there, send.at[sem], recv.at[sem], dev)

    def start(self, i):
        if i < self.total:
            self.copy(i).start()

    def finish(self, i):
        if i < 0 or i >= self.total:
            return
        buf, land, out, _, _ = self.refs
        self.copy(i).wait()
        kind, _, keep, n, at, _, _ = self.steps[i]
        if kind == "copy":
            return
        to = out if i == self.adds - 1 else buf
        chunk = TILE
        for k in (2, 3, 4, 6, 8):
            if n % (TILE * k) == 0:
                chunk = TILE * k

        def add(j, carry):
            here = at_tile(keep + j * chunk, chunk)
            there = at_tile(at + j * chunk, chunk)
            to[here, :] = (buf[here, :].astype(F32) + land[there, :].astype(F32)).astype(BF16)
            return carry

        lax.fori_loop(0, n // chunk, add, 0)


EARLY = 3584
LATE = 3 * 384 + 128
EARLY_CUTS = ((0, 1024), (1024, 1024), (2048, 1536))
LATE_CUTS = ((EARLY, 384), (EARLY + 384, 384), (EARLY + 768, 512))
EARLY_HALVINGS = 5
LATE_HALVINGS = 3


def back_kernel(
    frames, seqs, rows, cells,
    qkv_hbm, augk_hbm, early_hbm, da_ext, dx2, own_x, g_attn, w_qkv, learned,
    sums, own_tok, far_tok,
    qkv, augk, dag, dqkv, h1_scr, dh1_scr, buf, land, out, tok_send, tok_land,
    fsem, gsend, grecv, psend, precv, tsem,
):
    fi = lax.axis_index("frame")
    si = lax.axis_index("seq")
    half = frames // 2
    g = fi % half
    mine = fi // half
    total = frames * rows
    own = 2 * rows
    rest = mesh_bits(frames, seqs)
    fetch = [
        pltpu.make_async_copy(early_hbm, buf.at[pl.ds(0, EARLY), :], fsem.at[0]),
        pltpu.make_async_copy(qkv_hbm, qkv, fsem.at[1]),
        pltpu.make_async_copy(augk_hbm, augk, fsem.at[2]),
    ]
    for cp in fetch:
        cp.start()
    for k in range(2):
        there = pl.ds(pl.multiple_of((g + half * k) * rows, rows), rows)
        dag[:, there, :] = da_ext[:, k * rows : (k + 1) * rows, :]
    greet([neighbour(a, b, fi, si) for a, b in [("frame", 1)] + rest])
    gather, stages = staged_gather(
        half, [0, half], lambda s: dag.at[:, pl.ds(pl.multiple_of(s * rows, rows), rows), :], gsend, grecv, fi, si
    )
    gather(0)
    refs = fi, si, buf, land, out, psend, precv
    early, late = [], []
    land_at = sem_at = 0
    for group, cuts, halvings in ((early, EARLY_CUTS, EARLY_HALVINGS), (late, LATE_CUTS, LATE_HALVINGS)):
        for k, (start, length) in enumerate(cuts):
            r = k % len(rest)
            order = [("frame", 1)] + rest[r:] + rest[:r]
            piece = Piece(start, length, order, min(halvings, len(order)), land_at, sem_at, *refs)
            land_at, sem_at = piece.land_end, piece.sem_end
            group.append(piece)
    fetch[0].wait()
    for piece in early:
        piece.start(0)

    def early_point(i):
        for piece in early:
            piece.finish(i)
            piece.start(i + 1)

    x = own_x[...].reshape(own, 384).astype(F32)
    r = iota(x.shape, 0)
    x = jnp.where((r < cells) | ((r >= rows) & (r < rows + cells)), x, 0.0)
    vhat, _ = normed(x)
    h1_scr[...] = (vhat * g_attn[...].reshape(1, -1)).astype(BF16)
    dh1_scr[...] = jnp.zeros((own, 384), F32)
    buf[EARLY + 1152 :, :] = jnp.zeros((128, 384), BF16)
    fetch[1].wait()
    fetch[2].wait()

    def own_rows(b):
        at = [qkv[b, pl.ds(pl.multiple_of((g + half * k) * rows, rows), rows), :] for k in range(2)]
        return jnp.concatenate(at, axis=0)

    own_augk = jnp.concatenate(
        [augk[pl.ds(pl.multiple_of((g + half * k) * rows, rows), rows), :] for k in range(2)], axis=0
    )
    chunk = 256
    pieces_n = total // chunk
    split = (pieces_n + 1) // 2

    def query_pass(p, carry):
        def at_point(j):
            for k in range(PAIRS):
                i = 2 * k + j

                def point(i=i):
                    early_point(i)
                    stage = i // 2 + 1
                    if i % 2 == 1 and stage < stages - 1:
                        gather(stage)

                pl.when(p == k)(point)

        dq = grad_pass(
            own_rows(p), da_ext[p], da_ext[PAIRS],
            lambda i: qkv[3 + p, i, :], lambda i: qkv[6 + p, i, :], lambda i: augk[i, :],
            p, pieces_n, split, chunk, False, at_point,
        )
        dqkv[p] = (dq * HEAD_DIM**-0.5).astype(BF16)
        return carry

    lax.fori_loop(0, PAIRS, query_pass, 0)
    gather(stages - 1)

    def key_pass(p, carry):
        def at_point(j):
            for k in range(PAIRS):
                i = 2 * PAIRS + 2 * k + j

                def point(i=i, k=k):
                    early_point(i)
                    for m in range(k):
                        step = 2 * (k - m - 1) + j
                        late[m].finish(step)
                        late[m].start(step + 1)

                pl.when(p == k)(point)

        dk, dv = grad_pass(
            own_rows(3 + p), own_rows(6 + p), own_augk,
            lambda i: qkv[p, i, :], lambda i: dag[p, i, :], lambda i: dag[PAIRS, i, :],
            p, pieces_n, split, chunk, True, at_point,
        )
        d = jnp.concatenate([dqkv[p], dk.astype(BF16), dv.astype(BF16)], axis=1)
        buf[pl.ds(pl.multiple_of(EARLY + 384 * p, 128), 384), :] = tn(h1_scr[...], d).astype(BF16)
        w = jnp.concatenate(
            [w_qkv[:, pl.ds(pl.multiple_of(384 * b + 128 * p, 128), 128)] for b in range(3)], axis=1
        )
        dh1_scr[...] += nt(d, w)
        for k in range(PAIRS - 1):
            pl.when(p == k)(lambda k=k: late[k].start(0))
        return carry

    lax.fori_loop(0, PAIRS, key_pass, 0)
    dx, dg = norm_back(*normed(x), dh1_scr[...], g_attn[...].reshape(1, -1))
    buf[EARLY + 1152 : EARLY + 1168, :] = jnp.concatenate([dg, jnp.zeros((15, 384), F32)], axis=0).astype(BF16)
    late[2].start(0)
    dx = dx + dx2[...]
    for k in range(2):
        tail = jnp.concatenate([learned[k], jnp.zeros((rows - cells - MAPS, 384), F32)], axis=0)
        whole = jnp.concatenate([dx[k * rows : k * rows + cells, :], tail], axis=0)

        @pl.when(mine == k)
        def _():
            own_tok[...] = whole

        @pl.when(mine != k)
        def _():
            tok_send[...] = whole.astype(BF16)

    tok_copy = rc(tok_send, tok_land, tsem.at[0], tsem.at[1], (fi + half * (1 - 2 * mine), si))
    tok_copy.start()
    used = 4 * PAIRS
    done = [2 * (PAIRS - 1 - m) for m in range(PAIRS)]
    for i in range(max(max(p.total for p in early) - used, max(p.total - n for p, n in zip(late, done)))):
        early_point(used + i)
        for piece, n in zip(late, done):
            piece.finish(n + i)
            piece.start(n + i + 1)
    give = pltpu.make_async_copy(out, sums, fsem.at[0])
    give.start()
    tok_copy.wait()
    far_tok[...] = tok_land[...]
    give.wait()


def finish_kernel(cells, half, sums, own_tok, far_tok, d_tokens, learned, g_attn, w_qkv, w_out, g_mlp, w_up, w_down, g_learn, first, rest):
    for j in range(4):
        w_up[:, 384 * j : 384 * j + 384] = sums[384 * j : 384 * j + 384, :].astype(F32)
    w_down[...] = sums[1536:3072, :].astype(F32)
    w_out[...] = sums[3072:3456, :].astype(F32)
    small = sums[3456:3584, :].astype(F32)
    first[...] = small[0:72]
    rest[...] = small[80:104, 0:128]
    g_mlp[...] = small[72:73].reshape(-1)
    g_learn[...] = small[73:74].reshape(-1)
    for p in range(PAIRS):
        block = sums[EARLY + 384 * p : EARLY + 384 * p + 384, :].astype(F32)
        for b in range(3):
            w_qkv[:, 384 * b + 128 * p : 384 * b + 128 * p + 128] = block[:, 128 * b : 128 * b + 128]
    g_attn[...] = sums[EARLY + 1152 : EARLY + 1168, :].astype(F32)[0:1].reshape(-1)
    mine = lax.axis_index("frame") // half
    far = far_tok[...].astype(F32)
    near = own_tok[...]
    d_tokens[mine] = near[0:cells]
    d_tokens[1 - mine] = far[0:cells]
    learned[mine] = near[cells : cells + MAPS]
    learned[1 - mine] = far[cells : cells + MAPS]


def vspec(n):
    return [pl.BlockSpec(memory_space=VMEM)] * n


def params(collective=None, mib=56):
    if collective is None:
        return pltpu.CompilerParams(vmem_limit_bytes=mib * MIB)
    return pltpu.CompilerParams(collective_id=collective, has_side_effects=True, vmem_limit_bytes=mib * MIB)


def tap_masks():
    p = np.arange(WIDE) % 256
    px, py = p // GRID, p % GRID
    out = np.zeros((16, WIDE), np.float32)
    for t in range(9):
        r, c = t // 3 - 1, t % 3 - 1
        out[t] = (p < CELLS) & (px + r >= 0) & (px + r < GRID) & (py + c >= 0) & (py + c < GRID)
    return out


def head_sums():
    out = np.zeros((HEADS * HEAD_DIM, 128), np.float32)
    for h in range(HEADS):
        out[h * HEAD_DIM : (h + 1) * HEAD_DIM, DEL0 + 3 * h : DEL0 + 3 * h + 3] = 1.0
    return out


def on_device(frames, seqs, tokens, segments, g_attn, w_qkv, w_out, g_mlp, w_up, w_down, g_learn, conv_first, conv_rest, d_learned):
    _, cells, width = tokens.shape
    rows = -(-(cells + 1 + MAPS) // 16) * 16
    own = 2 * rows
    total = frames * rows
    n_sems = 1 + 2 * frames * 4
    sds = jax.ShapeDtypeStruct
    xg = pl.pallas_call(
        functools.partial(token_gather_kernel, frames, cells),
        out_shape=sds((frames, rows, width), BF16),
        in_specs=vspec(3),
        out_specs=vspec(1)[0],
        scratch_shapes=[
            VMEM((2, rows, width), BF16),
            VMEM((frames, rows, width), BF16),
            pltpu.SemaphoreType.DMA((n_sems,)),
            pltpu.SemaphoreType.DMA((frames,)),
        ],
        compiler_params=params(0),
        name="tokens_to_half",
    )(jnp.pad(tokens, ((0, 0), (0, rows - cells), (0, 0))), segments, d_learned.astype(F32))
    first9 = conv_first.transpose(1, 2, 0, 3).reshape(9, MAPS, width).astype(F32)
    rest27 = conv_rest.transpose(0, 2, 3, 1, 4).reshape(27, MAPS, MAPS).astype(F32)
    qkv, augk, da_ext, dx2, learned, early, own_x = pl.pallas_call(
        functools.partial(layer_kernel, frames, rows, cells),
        out_shape=[
            sds((9, total, 128), BF16),
            sds((total, 128), BF16),
            sds((PAIRS + 1, own, 128), BF16),
            sds((own, width), F32),
            sds((2, MAPS, width), F32),
            sds((EARLY, width), BF16),
            sds((2, rows, width), BF16),
        ],
        in_specs=vspec(12),
        out_specs=vspec(7),
        scratch_shapes=[
            VMEM((own, 128), F32),
            VMEM((PAIRS, own, 128), F32),
            VMEM((own, width), F32),
            VMEM((own, width), F32),
            VMEM((own, width), F32),
            VMEM((own, width), F32),
            VMEM((own, 128), F32),
            VMEM((own, 128), F32),
            VMEM((own, width), F32),
            VMEM((4, own, width), F32),
            VMEM((4, own, width), BF16),
            VMEM((own, width), BF16),
            VMEM((own, width), BF16),
            VMEM((own, width), BF16),
            VMEM((WIDE, width), BF16),
            VMEM((WIDE, width), F32),
            VMEM((WIDE, width), F32),
            VMEM((80, width), BF16),
            VMEM((80, WIDE), BF16),
            VMEM((32, width), F32),
            VMEM((8, width), F32),
            VMEM((3, 80, 128), F32),
            VMEM((3, 16, 128), F32),
        ],
        compiler_params=params(),
        name="layer",
    )(
        xg, g_attn, w_qkv, w_out, g_mlp, w_up, w_down, g_learn, first9, rest27,
        jnp.asarray(tap_masks()), jnp.asarray(head_sums()),
    )
    n_all = EARLY + LATE
    steps = 1 + len(mesh_bits(frames, seqs))
    land_n = sum(landing_rows(n, steps, EARLY_HALVINGS) for _, n in EARLY_CUTS)
    land_n += sum(landing_rows(n, steps, LATE_HALVINGS) for _, n in LATE_CUTS)
    anywhere = pl.BlockSpec(memory_space=pl.ANY)
    sums, own_tok, far_tok = pl.pallas_call(
        functools.partial(back_kernel, frames, seqs, rows, cells),
        out_shape=[sds((n_all, width), BF16), sds((rows, width), F32), sds((rows, width), BF16)],
        in_specs=[anywhere] * 3 + vspec(6),
        out_specs=[anywhere] + vspec(2),
        scratch_shapes=[
            VMEM((9, total, 128), BF16),
            VMEM((total, 128), BF16),
            VMEM((PAIRS + 1, total, 128), BF16),
            VMEM((PAIRS, own, 128), BF16),
            VMEM((own, width), BF16),
            VMEM((own, width), F32),
            VMEM((n_all, width), BF16),
            VMEM((land_n, width), BF16),
            VMEM((n_all, width), BF16),
            VMEM((rows, width), BF16),
            VMEM((rows, width), BF16),
            pltpu.SemaphoreType.DMA((3,)),
            pltpu.SemaphoreType.DMA((n_sems,)),
            pltpu.SemaphoreType.DMA((frames,)),
            pltpu.SemaphoreType.DMA((12 * steps,)),
            pltpu.SemaphoreType.DMA((12 * steps,)),
            pltpu.SemaphoreType.DMA((2,)),
        ],
        compiler_params=params(1),
        name="attention_back",
    )(qkv, augk, early, da_ext, dx2, own_x, g_attn, w_qkv, learned)
    d_tokens, learned_all, dg_attn, d_w_qkv, d_w_out, dg_mlp, d_w_up, d_w_down, dg_learn, first, rest = pl.pallas_call(
        functools.partial(finish_kernel, cells, frames // 2),
        out_shape=[
            sds((2, cells, width), F32),
            sds((2, MAPS, width), F32),
            sds((width,), F32),
            sds((width, 3 * width), F32),
            sds((width, width), F32),
            sds((width,), F32),
            sds((width, 4 * width), F32),
            sds((4 * width, width), F32),
            sds((width,), F32),
            sds((72, width), F32),
            sds((24, 128), F32),
        ],
        in_specs=vspec(3),
        out_specs=vspec(11),
        compiler_params=params(),
        name="outputs",
    )(sums, own_tok, far_tok)
    d_first = first.reshape(3, 3, MAPS, width).transpose(2, 0, 1, 3)
    d_rest = rest[:, :72].reshape(3, MAPS, 3, 3, MAPS)
    return (
        learned_all.astype(BF16), d_tokens, dg_attn, d_w_qkv, d_w_out, dg_mlp, d_w_up, d_w_down, dg_learn, d_first, d_rest,
    )


def solution(mesh):
    frames, seqs = mesh.shape["frame"], mesh.shape["seq"]
    both = P("seq", "frame", None)
    in_specs = (both, P("seq", "frame"), *([P()] * 9), both)
    out_specs = (both, both, *([P()] * 9))
    return jax.shard_map(
        functools.partial(on_device, frames, seqs),
        mesh=mesh,
        in_specs=in_specs,
        out_specs=out_specs,
        check_vma=False,
    )
```

```python
import functools

import jax
import jax.numpy as jnp
import numpy as np
from jax import lax
from jax.experimental import pallas as pl
from jax.experimental.pallas import tpu as pltpu
from jax.sharding import PartitionSpec as P

HEADS = 6
HEAD_DIM = 64
MAPS = 8
GRID = 14
CELLS = GRID * GRID
PAIRS = HEADS // 2
WIDE = 512
BIG = 1e30
LSE0 = 4
DEL0 = 4 + 3 * HEADS
AUG_END = 4 + 6 * HEADS
F32 = jnp.float32
BF16 = jnp.bfloat16
HIGH = lax.Precision.HIGHEST
MESH = pl.DeviceIdType.MESH
VMEM = pltpu.VMEM
MIB = 1 << 20


def nn(a, b, precision=None):
    return lax.dot_general(a, b, (((1,), (0,)), ((), ())), precision=precision, preferred_element_type=F32)


def nt(a, b, precision=None):
    return lax.dot_general(a, b, (((1,), (1,)), ((), ())), precision=precision, preferred_element_type=F32)


def tn(a, b, precision=None):
    return lax.dot_general(a, b, (((0,), (0,)), ((), ())), precision=precision, preferred_element_type=F32)


def iota(shape, dim):
    return lax.broadcasted_iota(jnp.int32, shape, dim)


def sixteen(v):
    return jnp.concatenate([v, jnp.zeros((8, v.shape[1]), v.dtype)], axis=0)


def normed(x):
    centered = x - jnp.mean(x, axis=-1, keepdims=True)
    rstd = lax.rsqrt(jnp.mean(centered * centered, axis=-1, keepdims=True) + 1e-06)
    return centered * rstd, rstd


def norm_back(vhat, rstd, dout, gain):
    e = dout * gain
    mean_e = jnp.mean(e, axis=-1, keepdims=True)
    mean_ev = jnp.mean(e * vhat, axis=-1, keepdims=True)
    return rstd * (e - mean_e - vhat * mean_ev), jnp.sum(dout * vhat, axis=0, keepdims=True)


C0 = 0.7978845608028654
C1 = 0.044715


def gelu(u):
    return 0.5 * u * (1.0 + jnp.tanh(C0 * (u + C1 * u * u * u)))


def gelu_grad(u):
    t = jnp.tanh(C0 * (u + C1 * u * u * u))
    return 0.5 * (1.0 + t) + 0.5 * u * (1.0 - t * t) * (C0 + (3.0 * C0 * C1) * u * u)


def flip(v, b):
    return v + b * (1 - 2 * ((v // b) % 2))


def bit_of(v, b):
    return (v // b) % 2


def rc(src, dst, send, recv, dev):
    return pltpu.make_async_remote_copy(
        src_ref=src, dst_ref=dst, send_sem=send, recv_sem=recv, device_id=dev, device_id_type=MESH
    )


def greet(partners):
    barrier = pltpu.get_barrier_semaphore()
    for dev in partners:
        pl.semaphore_signal(barrier, inc=1, device_id=dev, device_id_type=MESH)
    pl.semaphore_wait(barrier, len(partners))


class Gather:
    def __init__(self, half, base, turn, block, send, recv, first, fi, si):
        self.g, self.base, self.block, self.send, self.recv = fi % half, base, block, send, recv
        self.fi, self.si = fi, si
        bits = []
        b = 2
        while b < half:
            bits.append(b)
            b *= 2
        n = len(bits)
        self.n = n
        self.order = bits[turn % n :] + bits[: turn % n] if n else []
        self.pushes = [[] for _ in range(n + 2)]
        count = first
        for stage in range(n + 1):
            for j in range(1 << max(stage - 1, 0)):
                for bit in self.order[stage:] + [1]:
                    self.pushes[stage].append((stage, j, count, bit))
                    count += 1
        self.end = count
        self.last = n + 1

    def delta(self, bit):
        return bit * (1 - 2 * bit_of(self.g, bit))

    def arrivals(self, stage):
        return 1 << (self.n if stage == self.last else stage - 1)

    def slot(self, stage, j):
        at = self.base + self.g
        if stage == 0:
            return at
        passed = self.order if stage == self.last else self.order[: stage - 1]
        for k, bit in enumerate(passed):
            at = at + ((j // (1 << k)) % 2) * self.delta(bit)
        return at + self.delta(1 if stage == self.last else self.order[stage - 1])

    def copy(self, slot, k, bit):
        ref = self.block(slot)
        return rc(ref, ref, self.send.at[k], self.recv.at[slot], (flip(self.fi, bit), self.si))

    def run(self, stage):
        if stage > 0:
            for j in range(self.arrivals(stage)):
                slot = self.slot(stage, j)
                self.copy(slot, 0, 1).wait_recv()
                for st, i, k, bit in self.pushes[stage]:
                    if i == j:
                        self.copy(slot, k, bit).start()
        else:
            for st, i, k, bit in self.pushes[0]:
                self.copy(self.slot(0, 0), k, bit).start()

    def drain(self):
        for stage in self.pushes:
            for st, i, k, bit in stage:
                self.copy(self.slot(st, i), k, bit).wait_send()


def aug_masks(h):
    lane = iota((1, 128), 1)
    seg = lane < 4
    lse = seg | ((lane >= LSE0 + 3 * h) & (lane < LSE0 + 3 * h + 3))
    dlt = (lane >= DEL0 + 3 * h) & (lane < DEL0 + 3 * h + 3)
    return lse.astype(F32).astype(BF16), dlt.astype(F32).astype(BF16)


def pieces(value, which):
    hi = value.astype(BF16).astype(F32)
    rest = value - hi
    mid = rest.astype(BF16).astype(F32)
    low = rest - mid
    return jnp.where(which == 0, hi, jnp.where(which == 1, mid, low))


def half_masks():
    lane = iota((1, 128), 1)
    first = (lane < HEAD_DIM).astype(F32).astype(BF16)
    return first, (lane >= HEAD_DIM).astype(F32).astype(BF16)


def grad_pass(own_a, own_b, own_aug, all_a, all_b, all_aug, p, count, split, chunk, with_b, at_point):
    masks = half_masks()
    left_a, left_b = [], []
    for e in range(2):
        lse_mask, del_mask = aug_masks(2 * p + e)
        left_a.append(jnp.concatenate([own_a * masks[e], own_aug * lse_mask], axis=1))
        left_b.append(jnp.concatenate([own_b * masks[e], own_aug * del_mask], axis=1))
    acc = [jnp.zeros((own_a.shape[0], 128), F32) for _ in range(2 if with_b else 1)]
    for c in range(count):
        here = pl.ds(c * chunk, chunk)
        ra, rb, aug = all_a(here), all_b(here), all_aug(here)
        right_a = jnp.concatenate([ra, aug], axis=1)
        right_b = jnp.concatenate([rb, aug], axis=1)
        probs = [jnp.exp(nt(left_a[e], right_a)) for e in range(2)]
        ds = [(probs[e] * nt(left_b[e], right_b)).astype(BF16) for e in range(2)]
        acc[0] = acc[0] + nn(jnp.concatenate(ds, axis=1), jnp.concatenate([ra * m for m in masks], axis=0))
        if with_b:
            both = jnp.concatenate([prob.astype(BF16) for prob in probs], axis=1)
            acc[1] = acc[1] + nn(both, jnp.concatenate([rb * m for m in masks], axis=0))
        if c + 1 == split:
            at_point(0)
    at_point(1)
    return acc if with_b else acc[0]


def mesh_bits(frames, seqs):
    rest = []
    b = 1
    while b < seqs:
        rest.append(("seq", b))
        b *= 2
    b = 2
    while b < frames:
        rest.append(("frame", b))
        b *= 2
    return rest


TILE = 16


def at_tile(start, n):
    return pl.ds(start if isinstance(start, int) else pl.multiple_of(start, TILE), n)


def member(group, offset, fi, si):
    index = 0
    for i, (axis, bit) in enumerate(group):
        value = bit_of(fi if axis == "frame" else si, bit)
        if (offset >> i) & 1:
            value = 1 - value
            if axis == "frame":
                fi = flip(fi, bit)
            else:
                si = flip(si, bit)
        index = index + value * (1 << i)
    return (fi, si), index


def pairs_of(bits):
    return [bits[i : i + 2] for i in range(0, len(bits), 2)]


EARLY = 3584
LATE = 3 * 384 + 128
EARLY_CUTS = ((0, 1536), (1536, 2048))
LATE_CUTS = ((EARLY, 384), (EARLY + 384, 384), (EARLY + 768, 512))
EARLY_BITS = 5
LATE_BITS = 3


def early_groups(frames, seqs):
    rest = mesh_bits(frames, seqs)
    return [[("frame", 1)], rest[:1]] + pairs_of(rest[1:])


def late_groups(frames, seqs):
    return [[("frame", 1)]] + pairs_of(mesh_bits(frames, seqs))


def landing(length, groups, most_bits):
    rows = copies = bits = 0
    for group in groups:
        others = (1 << len(group)) - 1
        bits += len(group)
        copies += others
        if bits <= most_bits:
            length >>= len(group)
            copies += others
        rows += others * length
    return rows, copies


class Piece:
    def __init__(self, start, length, groups, most_bits, land_at, sem_at, fi, si, buf, land, out, send, recv):
        self.refs = buf, land, out, send, recv
        self.steps = []
        seg, n, sem, bits = start, length, sem_at, 0
        hist = []
        for group in groups:
            bits += len(group)
            offsets = range(1, 1 << len(group))
            moves = []
            if bits <= most_bits:
                hist.append((seg, n, group))
                n >>= len(group)
                _, index = member(group, 0, fi, si)
                for d in offsets:
                    dev, other = member(group, d, fi, si)
                    moves.append((seg + other * n, land_at, sem, dev))
                    land_at, sem = land_at + n, sem + 1
                seg = seg + index * n
            else:
                for d in offsets:
                    dev, _ = member(group, d, fi, si)
                    moves.append((seg, land_at, sem, dev))
                    land_at, sem = land_at + n, sem + 1
            self.steps.append(("add", seg, n, moves))
        self.adds = len(groups)
        for old, old_n, group in reversed(hist):
            moves = []
            for d in range(1, 1 << len(group)):
                moves.append((seg, 0, sem, member(group, d, fi, si)[0]))
                sem += 1
            self.steps.append(("copy", seg, n, moves))
            seg, n = old, old_n
        self.sem_end = sem
        self.land_end = land_at
        self.total = len(self.steps)

    def copies(self, i):
        buf, land, out, send, recv = self.refs
        kind, _, n, moves = self.steps[i]
        made = []
        for give, at, sem, dev in moves:
            src = (buf if kind == "add" else out).at[at_tile(give, n), :]
            dst = land.at[at_tile(at, n), :] if kind == "add" else src
            made.append(rc(src, dst, send.at[sem], recv.at[sem], dev))
        return made

    def start(self, i):
        if i < self.total:
            for cp in self.copies(i):
                cp.start()

    def finish(self, i):
        if i < 0 or i >= self.total:
            return
        buf, land, out, _, _ = self.refs
        for cp in self.copies(i):
            cp.wait()
        kind, keep, n, moves = self.steps[i]
        if kind == "copy":
            return
        to = out if i == self.adds - 1 else buf
        chunk = max(TILE * k for k in (1, 2, 3, 4, 6, 7) if n % (TILE * k) == 0)

        def add(j, carry):
            here = at_tile(keep + j * chunk, chunk)
            value = buf[here, :].astype(F32)
            for _, at, _, _ in moves:
                value = value + land[at_tile(at + j * chunk, chunk), :].astype(F32)
            to[here, :] = value.astype(BF16)
            return carry

        lax.fori_loop(0, n // chunk, add, 0)


def partners_of(all_groups, fi, si):
    seen, devs = set(), []
    for groups in all_groups:
        for group in groups:
            for d in range(1, 1 << len(group)):
                key = tuple(sorted(group[i] for i in range(len(group)) if (d >> i) & 1))
                if key not in seen:
                    seen.add(key)
                    devs.append(member(group, d, fi, si)[0])
    return devs


EARLY_POINTS = ((2, 5, 6, 7, 8, 10, 11), (4, 6, 7, 8, 9))


def whole_kernel(
    frames, seqs, rows, cells,
    tokens, segments, d_learned, g_attn, w_qkv, w_out, g_mlp, w_up, w_down, g_learn, first9, rest27, tapmask, blockones,
    sums, own_tok, far_tok,
    xp, xg, qkv, augk, dag, da_ext, dx2_scr, learned,
    augq, o_scr, x2_scr, y_scr, vhat2_scr, vhat3_scr, rstd2_scr, rstd3_scr,
    dh2_scr, u_scr, h3p, yp,
    dyp, w72_scr, spread_scr, rest_scr, gain_scr, conv_bw, conv_fw, dqkv,
    h1_scr, dh1_scr, buf, land, out, tok_send, tok_land, tsend,
    trecv, gsend, grecv, psend, precv, fsem, tsem,
):
    fi = lax.axis_index("frame")
    si = lax.axis_index("seq")
    half = frames // 2
    g = fi % half
    mine = fi // half
    total = frames * rows
    own = 2 * rows
    other = fi + half * (1 - 2 * mine)
    partner = (other, si)
    for k in range(2):
        body = tokens[k].astype(F32)[0:cells]
        seg = jnp.broadcast_to(segments[k : k + 1, 0:1].astype(F32), (1, 384))
        pad = jnp.zeros((rows - cells - 1 - MAPS, 384), F32)
        xp[k] = jnp.concatenate([body, seg, d_learned[k], pad], axis=0).astype(BF16)
    xg[fi] = xp[mine]
    singles = [[bit] for bit in mesh_bits(frames, seqs)]
    by_early, by_late = early_groups(frames, seqs), late_groups(frames, seqs)
    greet(partners_of((singles, by_early, by_late), fi, si))
    token_block = lambda slot: xg.at[slot]
    near = Gather(half, half * mine, 0, token_block, tsend, trecv, 1, fi, si)
    far = Gather(half, half * (1 - mine), 1, token_block, tsend, trecv, near.end, fi, si)
    to_partner = rc(xp.at[1 - mine], xg.at[fi], tsend.at[0], trecv.at[fi], partner)
    to_partner.start()
    near.run(0)
    da_block = lambda slot: dag.at[:, pl.ds(pl.multiple_of(slot * rows, rows), rows), :]
    da_near = Gather(half, 0, 0, da_block, gsend, grecv, 0, fi, si)
    da_far = Gather(half, half, 1, da_block, gsend, grecv, da_near.end, fi, si)
    refs = fi, si, buf, land, out, psend, precv
    early, late = [], []
    land_at = sem_at = 0
    for group, cuts, by, bits in ((early, EARLY_CUTS, by_early, EARLY_BITS), (late, LATE_CUTS, by_late, LATE_BITS)):
        for start, length in cuts:
            group.append(Piece(start, length, by, bits, land_at, sem_at, *refs))
            land_at, sem_at = group[-1].land_end, group[-1].sem_end

    h2_rows, a_rows, dm_rows = (pl.ds(own * k, own) for k in (4, 5, 6))

    def early_point(i):
        for piece, points in zip(early, EARLY_POINTS):
            if i in points:
                step = 1 + points.index(i)
                piece.finish(step)
                piece.start(step + 1)

    lane128 = iota((rows, 128), 1)
    row128 = iota((rows, 128), 0)
    valid_row = row128 < cells

    w72 = first9[...].reshape(72, 384)
    w72_scr[...] = sixteen(w72).astype(BF16)
    square_r, square_c = iota((128, 128), 0), iota((128, 128), 1)
    repeat = ((square_c & 7) == square_r).astype(F32)
    same_tap = (((square_r >> 3) == (square_c >> 3)) & (square_r < 72)).astype(F32)
    for layer in range(3):
        by_tap = rest27[9 * layer : 9 * layer + 9].reshape(72, MAPS)
        by_tap = jnp.concatenate([by_tap, jnp.zeros((72, 120), F32)], axis=1)
        conv_bw[layer] = sixteen(by_tap)
        by_tap = jnp.concatenate([by_tap, jnp.zeros((56, 128), F32)], axis=0)
        conv_fw[layer] = nn(repeat[0:16], nn(by_tap, repeat, HIGH) * same_tap, HIGH)

    def project(f, carry):
        x = xg[f].astype(F32)
        seg = x[cells : cells + 1, 0:128]
        x = jnp.where(iota(x.shape, 0) < cells, x, 0.0)
        vhat, _ = normed(x)
        h1 = (vhat * g_attn[...].reshape(1, -1)).astype(BF16)
        base = pl.multiple_of(f * rows, rows)
        whole = nn(h1, w_qkv[...])
        for b in range(9):
            part = whole[:, 128 * b : 128 * b + 128]
            if b < 3:
                part = part * HEAD_DIM**-0.5
            qkv[b, pl.ds(base, rows), :] = part.astype(BF16)
        same = (lane128.astype(F32) == seg) & valid_row
        augk[pl.ds(base, rows), :] = jnp.where(
            lane128 < 4, jnp.where(same, 0.0, -BIG), jnp.where(lane128 < AUG_END, -1.0, 0.0)
        ).astype(BF16)
        return carry

    def project_stage(gather, stage):
        gather.run(stage)
        if stage == 0:
            project(gather.slot(0, 0), 0)
        else:
            lax.fori_loop(0, gather.arrivals(stage), lambda j, c: project(gather.slot(stage, j), c), 0)

    project(near.slot(0, 0), 0)
    project_stage(near, 1)
    far_block = xg.at[other]
    rc(far_block, far_block, tsend.at[0], trecv.at[other], partner).wait_recv()
    project_stage(far, 0)
    for stage in range(2, near.last):
        project_stage(near, stage)
    for stage in range(1, near.last):
        project_stage(far, stage)
    project_stage(near, near.last)
    project_stage(far, far.last)
    to_partner.wait_send()
    near.drain()
    far.drain()

    ones = jnp.ones((frames * rows, 128), BF16)

    for k in range(2):
        f = g + half * k
        seg = xg[f].astype(F32)[cells : cells + 1, 0:128]
        same = (lane128.astype(F32) == seg) & valid_row & (lane128 < 4)
        augq[k * rows : (k + 1) * rows, :] = same.astype(F32)

    together = 2 if frames <= 16 else 1

    def attend(step, carry):
        p = step // (4 // together)
        k = step % 2
        f = g + half * k
        q = qkv[p, pl.ds(pl.multiple_of(f * rows, rows), rows), :]
        mine = pl.ds(pl.multiple_of(k * rows, rows), rows)
        aug = augq[mine, :]
        seg_aug = jnp.where(lane128 < 4, aug, 0.0).astype(BF16)
        keys = jnp.concatenate([qkv[3 + p], augk[...]], axis=1)
        values = jnp.concatenate([qkv[6 + p], ones], axis=1)
        mixed = o_scr[p, mine, :] if together == 1 else 0.0
        for n in range(together):
            e = n if together == 2 else (step // 2) % 2
            keep = (lane128 >= HEAD_DIM * e) & (lane128 < HEAD_DIM * (e + 1))
            s = nt(jnp.concatenate([q * keep.astype(F32).astype(BF16), seg_aug], axis=1), keys)
            top = jnp.max(s, axis=1, keepdims=True)
            prob = jnp.exp(s - top).astype(BF16)
            o = nn(prob, values)
            weight = o[:, 128:]
            mixed = jnp.where(keep, o[:, :128] / weight, mixed)
            lse = top + jnp.log(weight)
            which = lane128 - (LSE0 + 3 * (2 * p + e))
            aug = jnp.where((which >= 0) & (which < 3), pieces(lse, which), aug)
        augq[mine, :] = aug
        o_scr[p, mine, :] = mixed
        return carry

    lax.fori_loop(0, 4 * PAIRS // together, attend, 0)

    def apart(fn):
        pl.when(fi >= 0)(fn)

    @apart
    def _():
        a = jnp.concatenate([o_scr[p].astype(BF16) for p in range(PAIRS)], axis=1)
        out[a_rows, :] = a
        both = jnp.concatenate([xg[g], xg[g + half]], axis=0).astype(F32)
        r = iota(both.shape, 0)
        x = jnp.where((r < cells) | ((r >= rows) & (r < rows + cells)), both, 0.0)
        x2 = x + nn(a, w_out[...])
        x2_scr[...] = x2
        y_scr[...] = x2
        vhat, rstd = normed(x2)
        rstd2_scr[...] = jnp.broadcast_to(rstd, (own, 128))
        vhat2_scr[...] = vhat
        out[h2_rows, :] = (vhat * g_mlp[...].reshape(1, -1)).astype(BF16)

    def mlp(j, carry):
        cols = pl.ds(pl.multiple_of(384 * j, 384), 384)
        u = nn(out[h2_rows, :], w_up[:, cols])
        u_scr[j] = u
        hid = gelu(u).astype(BF16)
        out[pl.ds(pl.multiple_of(own * j, 16), own), :] = hid
        y_scr[...] += nn(hid, w_down[cols, :])
        return carry

    lax.fori_loop(0, 4, mlp, 0)

    @apart
    def _():
        y = y_scr[...]
        vhat, rstd = normed(y)
        vhat3_scr[...] = vhat
        rstd3_scr[...] = jnp.broadcast_to(rstd, (own, 128))
        h3 = (vhat * g_learn[...].reshape(1, -1)).astype(BF16)
        for k in range(2):
            yp[256 * k : 256 * k + rows, :] = y[k * rows : (k + 1) * rows, :]
            yp[256 * k + rows : 256 * k + 256, :] = jnp.zeros((256 - rows, 384), F32)
            h3p[256 * k : 256 * k + rows, :] = h3[k * rows : (k + 1) * rows, :]
            h3p[256 * k + rows : 256 * k + 256, :] = jnp.zeros((256 - rows, 384), BF16)

    def shift_of(t):
        return GRID * (t // 3 - 1) + (t % 3 - 1)

    def moved(v, s):
        return v if s == 0 else pltpu.roll(v, (-s) % WIDE, 1)

    def tap(t):
        return tapmask[t : t + 1, :]

    def im2col(v):
        parts = [moved(v, shift_of(t)) * tap(t) for t in range(9)]
        return jnp.concatenate(parts + [jnp.zeros((56, WIDE), F32)], axis=0)

    def spread_of(v):
        return jnp.concatenate([moved(v, -shift_of(t)) * tap(8 - t) for t in range(9)], axis=0)

    @apart
    def _():
        taps = nt(w72_scr[...], h3p[...])
        z1 = jnp.zeros((MAPS, WIDE), F32)
        for t in range(9):
            z1 = z1 + moved(taps[8 * t : 8 * t + 8, :], shift_of(t)) * tap(t)
        zs = [z1]
        cols_of = []
        for layer in range(3):
            col = im2col(gelu(zs[-1]))
            cols_of.append(col)
            zs.append(nn(conv_fw[layer], col, HIGH)[0:MAPS])
        maps = tap(4) / (1.0 + jnp.exp(-zs[3]))
        dmaps = []
        for k in range(2):
            f = g + half * k
            dl = xg[f].astype(F32)[cells + 1 : cells + 1 + MAPS, :] * (1.0 / cells)
            dl = sixteen(dl)
            mk = sixteen(maps[:, 256 * k : 256 * k + 256])
            yk = yp[256 * k : 256 * k + 256, :]
            learned[k] = nn(mk, yk, HIGH)[0:MAPS] * (1.0 / cells)
            dmaps.append(nt(dl, yk, HIGH)[0:MAPS])
            dyp[256 * k : 256 * k + 256, :] = tn(mk, dl, HIGH)
        dz = jnp.concatenate(dmaps, axis=1) * maps * (1.0 - maps)
        small = []
        for layer in (2, 1, 0):
            dw = nt(sixteen(dz), cols_of[layer], HIGH)[0:MAPS]
            small.insert(0, jnp.concatenate([dw, jnp.zeros((MAPS, 256), F32)], axis=1))
            dz = tn(conv_bw[layer], sixteen(spread_of(dz)), HIGH)[0:MAPS] * gelu_grad(zs[layer])
        dz = dz.astype(BF16).astype(F32) * tap(4)
        spread_scr[...] = sixteen(spread_of(dz)).astype(BF16)
        rest_scr[...] = jnp.concatenate(small + [jnp.zeros((8, 384), F32)], axis=0)

    @apart
    def _():
        dh3 = tn(spread_scr[...], w72_scr[...])
        dh3 = jnp.concatenate([dh3[0:rows], dh3[256 : 256 + rows]], axis=0)
        dy, dg3 = norm_back(vhat3_scr[...], rstd3_scr[:, 0:1], dh3, g_learn[...].reshape(1, -1))
        dy = dy + jnp.concatenate([dyp[0:rows, :], dyp[256 : 256 + rows, :]], axis=0)
        y_scr[...] = dy
        out[dm_rows, :] = dy.astype(BF16)
        dh2_scr[...] = jnp.zeros((own, 384), F32)
        gain_scr[...] = jnp.concatenate([dg3, jnp.zeros((7, 384), F32)], axis=0)

    def mlp_back(j, carry):
        cols = pl.ds(pl.multiple_of(384 * j, 384), 384)
        dm = out[dm_rows, :]
        du = (nt(dm, w_down[cols, :]) * gelu_grad(u_scr[j])).astype(BF16)
        buf[cols, :] = tn(out[h2_rows, :], du).astype(BF16)
        buf[pl.ds(pl.multiple_of(1536 + 384 * j, 384), 384), :] = tn(out[pl.ds(pl.multiple_of(own * j, 16), own), :], dm).astype(BF16)
        dh2_scr[...] += nt(du, w_up[:, cols])
        return carry

    lax.fori_loop(0, 4, mlp_back, 0)
    early[0].start(0)

    @apart
    def _():
        dx2, dg2 = norm_back(vhat2_scr[...], rstd2_scr[:, 0:1], dh2_scr[...], g_mlp[...].reshape(1, -1))
        dx2 = dx2 + y_scr[...]
        dx2_scr[...] = dx2
        out[dm_rows, :] = dx2.astype(BF16)
        gains = jnp.concatenate([dg2, gain_scr[0:1, :], jnp.zeros((6, 384), F32)], axis=0)
        d_first = nn(spread_scr[...], h3p[...])[0:72]
        small = [d_first, gains, rest_scr[...], jnp.zeros((16, 384), F32)]
        buf[3456:3584, :] = jnp.concatenate(small, axis=0).astype(BF16)

    early[0].finish(0)
    early[0].start(1)

    @apart
    def _():
        dzz = out[dm_rows, :]
        buf[3072:3456, :] = tn(out[a_rows, :], dzz).astype(BF16)
        da = nt(dzz, w_out[...]).astype(BF16)
        prod = jnp.concatenate([o_scr[p] for p in range(PAIRS)], axis=1) * da.astype(F32)
        lane = iota((own, 128), 1)
        which = lane - DEL0
        which = which - 3 * (which // 3)
        delta = pieces(nn(prod, blockones[...], HIGH), which)
        full = jnp.where((lane >= DEL0) & (lane < AUG_END), delta, augq[...])
        full = full.astype(BF16)
        for p in range(PAIRS):
            da_ext[p] = da[:, 128 * p : 128 * p + 128]
        da_ext[PAIRS] = full
        for k in range(2):
            there = pl.ds(pl.multiple_of((g + half * k) * rows, rows), rows)
            dag[:, there, :] = da_ext[:, k * rows : (k + 1) * rows, :]

    early[1].start(0)
    da_near.run(0)
    da_far.run(0)
    x = jnp.concatenate([xg[g], xg[g + half]], axis=0).astype(F32)
    r = iota(x.shape, 0)
    x = jnp.where((r < cells) | ((r >= rows) & (r < rows + cells)), x, 0.0)
    vhat, _ = normed(x)
    h1_scr[...] = (vhat * g_attn[...].reshape(1, -1)).astype(BF16)
    dh1_scr[...] = jnp.zeros((own, 384), F32)
    buf[EARLY + 1152 :, :] = jnp.zeros((128, 384), BF16)
    early[1].finish(0)
    early[1].start(1)

    def own_rows(b):
        at = [qkv[b, pl.ds(pl.multiple_of((g + half * k) * rows, rows), rows), :] for k in range(2)]
        return jnp.concatenate(at, axis=0)

    own_augk = jnp.concatenate(
        [augk[pl.ds(pl.multiple_of((g + half * k) * rows, rows), rows), :] for k in range(2)], axis=0
    )
    chunk = 256
    pieces_n = total // chunk
    split = (pieces_n + 1) // 2

    def query_pass(p, carry):
        def at_point(j):
            for k in range(PAIRS):
                i = 2 * k + j

                def point(i=i):
                    early_point(i)
                    stage = i // 2 + 1
                    if i % 2 == 1 and stage < da_near.last:
                        da_near.run(stage)
                        da_far.run(stage)

                pl.when(p == k)(point)

        dq = grad_pass(
            own_rows(p), da_ext[p], da_ext[PAIRS],
            lambda i: qkv[3 + p, i, :], lambda i: qkv[6 + p, i, :], lambda i: augk[i, :],
            p, pieces_n, split, chunk, False, at_point,
        )
        dqkv[p] = (dq * HEAD_DIM**-0.5).astype(BF16)
        return carry

    lax.fori_loop(0, PAIRS, query_pass, 0)
    for gather in (da_near, da_far):
        gather.run(gather.last)
        gather.drain()

    def key_pass(p, carry):
        def at_point(j):
            for k in range(PAIRS):
                i = 2 * PAIRS + 2 * k + j

                def point(i=i, k=k):
                    early_point(i)
                    for m in range(k):
                        step = 2 * (k - m - 1) + j
                        late[m].finish(step)
                        late[m].start(step + 1)

                pl.when(p == k)(point)

        dk, dv = grad_pass(
            own_rows(3 + p), own_rows(6 + p), own_augk,
            lambda i: qkv[p, i, :], lambda i: dag[p, i, :], lambda i: dag[PAIRS, i, :],
            p, pieces_n, split, chunk, True, at_point,
        )
        d = jnp.concatenate([dqkv[p], dk.astype(BF16), dv.astype(BF16)], axis=1)
        buf[pl.ds(pl.multiple_of(EARLY + 384 * p, 128), 384), :] = tn(h1_scr[...], d).astype(BF16)
        w = jnp.concatenate(
            [w_qkv[:, pl.ds(pl.multiple_of(384 * b + 128 * p, 128), 128)] for b in range(3)], axis=1
        )
        dh1_scr[...] += nt(d, w)
        for k in range(PAIRS - 1):
            pl.when(p == k)(lambda k=k: late[k].start(0))
        return carry

    lax.fori_loop(0, PAIRS, key_pass, 0)
    dx, dg = norm_back(*normed(x), dh1_scr[...], g_attn[...].reshape(1, -1))
    buf[EARLY + 1152 : EARLY + 1168, :] = jnp.concatenate([dg, jnp.zeros((15, 384), F32)], axis=0).astype(BF16)
    late[2].start(0)
    dx = dx + dx2_scr[...]
    for k in range(2):
        tail = jnp.concatenate([learned[k], jnp.zeros((rows - cells - MAPS, 384), F32)], axis=0)
        whole = jnp.concatenate([dx[k * rows : k * rows + cells, :], tail], axis=0)

        @pl.when(mine == k)
        def _():
            own_tok[...] = whole

        @pl.when(mine != k)
        def _():
            tok_send[...] = whole.astype(BF16)

    tok_copy = rc(tok_send, tok_land, tsem.at[0], tsem.at[1], (fi + half * (1 - 2 * mine), si))
    tok_copy.start()
    give = [
        pltpu.make_async_copy(out.at[pl.ds(at, n), :], sums.at[pl.ds(at, n), :], fsem.at[i])
        for i, (at, n) in enumerate((EARLY_CUTS[0], (EARLY_CUTS[1][0], EARLY + LATE - EARLY_CUTS[1][0])))
    ]
    running = [(piece, 1 + len(points)) for piece, points in zip(early, EARLY_POINTS)]
    running += [(piece, 2 * (PAIRS - 1 - m)) for m, piece in enumerate(late)]
    for piece, n in running[:1]:
        for i in range(n, piece.total):
            piece.finish(i)
            piece.start(i + 1)
    give[0].start()
    for i in range(max(piece.total - n for piece, n in running[1:])):
        for piece, n in running[1:]:
            piece.finish(n + i)
            piece.start(n + i + 1)
    give[1].start()
    tok_copy.wait()
    far_tok[...] = tok_land[...]
    for cp in give:
        cp.wait()


def finish_kernel(cells, half, sums, own_tok, far_tok, d_tokens, learned, g_attn, w_qkv, w_out, g_mlp, w_up, w_down, g_learn, first, rest):
    for j in range(4):
        w_up[:, 384 * j : 384 * j + 384] = sums[384 * j : 384 * j + 384, :].astype(F32)
    w_down[...] = sums[1536:3072, :].astype(F32)
    w_out[...] = sums[3072:3456, :].astype(F32)
    small = sums[3456:3584, :].astype(F32)
    first[...] = small[0:72]
    rest[...] = small[80:104, 0:128]
    g_mlp[...] = small[72:73].reshape(-1)
    g_learn[...] = small[73:74].reshape(-1)
    for p in range(PAIRS):
        block = sums[EARLY + 384 * p : EARLY + 384 * p + 384, :].astype(F32)
        for b in range(3):
            w_qkv[:, 384 * b + 128 * p : 384 * b + 128 * p + 128] = block[:, 128 * b : 128 * b + 128]
    g_attn[...] = sums[EARLY + 1152 : EARLY + 1168, :].astype(F32)[0:1].reshape(-1)
    mine = lax.axis_index("frame") // half
    far = far_tok[...].astype(F32)
    near = own_tok[...]
    d_tokens[mine] = near[0:cells]
    d_tokens[1 - mine] = far[0:cells]
    learned[mine] = near[cells : cells + MAPS]
    learned[1 - mine] = far[cells : cells + MAPS]


def vspec(n):
    return [pl.BlockSpec(memory_space=VMEM)] * n


def params(collective=None, mib=56):
    if collective is None:
        return pltpu.CompilerParams(vmem_limit_bytes=mib * MIB)
    return pltpu.CompilerParams(collective_id=collective, has_side_effects=True, vmem_limit_bytes=mib * MIB)


def tap_masks():
    p = np.arange(WIDE) % 256
    px, py = p // GRID, p % GRID
    out = np.zeros((16, WIDE), np.float32)
    for t in range(9):
        r, c = t // 3 - 1, t % 3 - 1
        out[t] = (p < CELLS) & (px + r >= 0) & (px + r < GRID) & (py + c >= 0) & (py + c < GRID)
    return out


def head_sums():
    out = np.zeros((HEADS * HEAD_DIM, 128), np.float32)
    for h in range(HEADS):
        out[h * HEAD_DIM : (h + 1) * HEAD_DIM, DEL0 + 3 * h : DEL0 + 3 * h + 3] = 1.0
    return out


def on_device(frames, seqs, tokens, segments, g_attn, w_qkv, w_out, g_mlp, w_up, w_down, g_learn, conv_first, conv_rest, d_learned):
    _, cells, width = tokens.shape
    rows = -(-(cells + 1 + MAPS) // 16) * 16
    own = 2 * rows
    total = frames * rows
    n_sems = 1 + 8 * frames
    sds = jax.ShapeDtypeStruct
    first9 = conv_first.transpose(1, 2, 0, 3).reshape(9, MAPS, width).astype(F32)
    rest27 = conv_rest.transpose(0, 2, 3, 1, 4).reshape(27, MAPS, MAPS).astype(F32)
    n_all = EARLY + LATE
    sizes = [landing(n, early_groups(frames, seqs), EARLY_BITS) for _, n in EARLY_CUTS]
    sizes += [landing(n, late_groups(frames, seqs), LATE_BITS) for _, n in LATE_CUTS]
    land_n, copies = (sum(v) for v in zip(*sizes))
    anywhere = pl.BlockSpec(memory_space=pl.ANY)
    sums, own_tok, far_tok = pl.pallas_call(
        functools.partial(whole_kernel, frames, seqs, rows, cells),
        out_shape=[sds((n_all, width), BF16), sds((rows, width), F32), sds((rows, width), BF16)],
        in_specs=vspec(14),
        out_specs=[anywhere] + vspec(2),
        scratch_shapes=[
            VMEM((2, rows, width), BF16),
            VMEM((frames, rows, width), BF16),
            VMEM((9, total, 128), BF16),
            VMEM((total, 128), BF16),
            VMEM((PAIRS + 1, total, 128), BF16),
            VMEM((PAIRS + 1, own, 128), BF16),
            VMEM((own, width), F32),
            VMEM((2, MAPS, width), F32),
            VMEM((own, 128), F32),
            VMEM((PAIRS, own, 128), F32),
            VMEM((own, width), F32),
            VMEM((own, width), F32),
            VMEM((own, width), F32),
            VMEM((own, width), F32),
            VMEM((own, 128), F32),
            VMEM((own, 128), F32),
            VMEM((own, width), F32),
            VMEM((4, own, width), F32),
            VMEM((WIDE, width), BF16),
            VMEM((WIDE, width), F32),
            VMEM((WIDE, width), F32),
            VMEM((80, width), BF16),
            VMEM((80, WIDE), BF16),
            VMEM((32, width), F32),
            VMEM((8, width), F32),
            VMEM((3, 80, 128), F32),
            VMEM((3, 16, 128), F32),
            VMEM((PAIRS, own, 128), BF16),
            VMEM((own, width), BF16),
            VMEM((own, width), F32),
            VMEM((n_all, width), BF16),
            VMEM((land_n, width), BF16),
            VMEM((n_all, width), BF16),
            VMEM((rows, width), BF16),
            VMEM((rows, width), BF16),
            pltpu.SemaphoreType.DMA((n_sems,)),
            pltpu.SemaphoreType.DMA((frames,)),
            pltpu.SemaphoreType.DMA((n_sems,)),
            pltpu.SemaphoreType.DMA((frames,)),
            pltpu.SemaphoreType.DMA((copies,)),
            pltpu.SemaphoreType.DMA((copies,)),
            pltpu.SemaphoreType.DMA((2,)),
            pltpu.SemaphoreType.DMA((2,)),
        ],
        compiler_params=params(0, 60),
        name="layer",
    )(
        jnp.pad(tokens, ((0, 0), (0, rows - cells), (0, 0))), segments, d_learned.astype(F32),
        g_attn, w_qkv, w_out, g_mlp, w_up, w_down, g_learn, first9, rest27,
        jnp.asarray(tap_masks()), jnp.asarray(head_sums()),
    )
    d_tokens, learned_all, dg_attn, d_w_qkv, d_w_out, dg_mlp, d_w_up, d_w_down, dg_learn, first, rest = pl.pallas_call(
        functools.partial(finish_kernel, cells, frames // 2),
        out_shape=[
            sds((2, cells, width), F32),
            sds((2, MAPS, width), F32),
            sds((width,), F32),
            sds((width, 3 * width), F32),
            sds((width, width), F32),
            sds((width,), F32),
            sds((width, 4 * width), F32),
            sds((4 * width, width), F32),
            sds((width,), F32),
            sds((72, width), F32),
            sds((24, 128), F32),
        ],
        in_specs=vspec(3),
        out_specs=vspec(11),
        compiler_params=params(),
        name="outputs",
    )(sums, own_tok, far_tok)
    d_first = first.reshape(3, 3, MAPS, width).transpose(2, 0, 1, 3)
    d_rest = rest[:, :72].reshape(3, MAPS, 3, 3, MAPS)
    return (
        learned_all.astype(BF16), d_tokens, dg_attn, d_w_qkv, d_w_out, dg_mlp, d_w_up, d_w_down, dg_learn, d_first, d_rest,
    )


def solution(mesh):
    frames, seqs = mesh.shape["frame"], mesh.shape["seq"]
    both = P("seq", "frame", None)
    in_specs = (both, P("seq", "frame"), *([P()] * 9), both)
    out_specs = (both, both, *([P()] * 9))
    return jax.shard_map(
        functools.partial(on_device, frames, seqs),
        mesh=mesh,
        in_specs=in_specs,
        out_specs=out_specs,
        check_vma=False,
    )
```

```python
import functools

import jax
import jax.numpy as jnp
import numpy as np
from jax import lax
from jax.experimental import pallas as pl
from jax.experimental.pallas import tpu as pltpu
from jax.sharding import PartitionSpec as P

HEADS = 6
HEAD_DIM = 64
MAPS = 8
GRID = 14
CELLS = GRID * GRID
PAIRS = HEADS // 2
WIDE = 512
BIG = 1e30
LSE0 = 4
DEL0 = 4 + 3 * HEADS
AUG_END = 4 + 6 * HEADS
F32 = jnp.float32
BF16 = jnp.bfloat16
HIGH = lax.Precision.HIGHEST
MESH = pl.DeviceIdType.MESH
VMEM = pltpu.VMEM
MIB = 1 << 20


def nn(a, b, precision=None):
    return lax.dot_general(a, b, (((1,), (0,)), ((), ())), precision=precision, preferred_element_type=F32)


def nt(a, b, precision=None):
    return lax.dot_general(a, b, (((1,), (1,)), ((), ())), precision=precision, preferred_element_type=F32)


def tn(a, b, precision=None):
    return lax.dot_general(a, b, (((0,), (0,)), ((), ())), precision=precision, preferred_element_type=F32)


def iota(shape, dim):
    return lax.broadcasted_iota(jnp.int32, shape, dim)


def sixteen(v):
    return jnp.concatenate([v, jnp.zeros((8, v.shape[1]), v.dtype)], axis=0)


def normed(x):
    centered = x - jnp.mean(x, axis=-1, keepdims=True)
    rstd = lax.rsqrt(jnp.mean(centered * centered, axis=-1, keepdims=True) + 1e-06)
    return centered * rstd, rstd


def norm_back(vhat, rstd, dout, gain):
    e = dout * gain
    mean_e = jnp.mean(e, axis=-1, keepdims=True)
    mean_ev = jnp.mean(e * vhat, axis=-1, keepdims=True)
    return rstd * (e - mean_e - vhat * mean_ev), jnp.sum(dout * vhat, axis=0, keepdims=True)


C0 = 0.7978845608028654
C1 = 0.044715


def gelu(u):
    return 0.5 * u * (1.0 + jnp.tanh(C0 * (u + C1 * u * u * u)))


def gelu_grad(u):
    t = jnp.tanh(C0 * (u + C1 * u * u * u))
    return 0.5 * (1.0 + t) + 0.5 * u * (1.0 - t * t) * (C0 + (3.0 * C0 * C1) * u * u)


def flip(v, b):
    return v + b * (1 - 2 * ((v // b) % 2))


def bit_of(v, b):
    return (v // b) % 2


def rc(src, dst, send, recv, dev):
    return pltpu.make_async_remote_copy(
        src_ref=src, dst_ref=dst, send_sem=send, recv_sem=recv, device_id=dev, device_id_type=MESH
    )


def greet(partners):
    barrier = pltpu.get_barrier_semaphore()
    for dev in partners:
        pl.semaphore_signal(barrier, inc=1, device_id=dev, device_id_type=MESH)
    pl.semaphore_wait(barrier, len(partners))


class Gather:
    def __init__(self, half, base, turn, block, send, recv, first, fi, si, shift=0):
        self.shift = shift
        self.g, self.base, self.block, self.send, self.recv = fi % half, base, block, send, recv
        self.fi, self.si = fi, si
        bits = []
        b = 2
        while b < half:
            bits.append(b)
            b *= 2
        n = len(bits)
        self.n = n
        self.order = bits[turn % n :] + bits[: turn % n] if n else []
        self.pushes = [[] for _ in range(n + 2)]
        count = first
        for stage in range(n + 1):
            for j in range(1 << max(stage - 1, 0)):
                for bit in self.order[stage:] + [1]:
                    self.pushes[stage].append((stage, j, count, bit))
                    count += 1
        self.end = count
        self.last = n + 1

    def delta(self, bit):
        return bit * (1 - 2 * bit_of(self.g, bit))

    def arrivals(self, stage):
        return 1 << (self.n if stage == self.last else stage - 1)

    def slot(self, stage, j):
        at = self.base + self.g
        if stage == 0:
            return at
        passed = self.order if stage == self.last else self.order[: stage - 1]
        for k, bit in enumerate(passed):
            at = at + ((j // (1 << k)) % 2) * self.delta(bit)
        return at + self.delta(1 if stage == self.last else self.order[stage - 1])

    def nearby(self, j, core):
        at = self.base + self.g
        for k, bit in enumerate(self.order):
            at = at + ((j // (1 << k)) % 2) * self.delta(bit)
        return at + self.delta(1) if core else at

    def copy(self, slot, k, bit):
        ref = self.block(slot)
        return rc(ref, ref, self.send.at[k], self.recv.at[slot + self.shift], (flip(self.fi, bit), self.si))

    def run(self, stage):
        if stage > 0:
            for j in range(self.arrivals(stage)):
                slot = self.slot(stage, j)
                self.copy(slot, 0, 1).wait_recv()
                for st, i, k, bit in self.pushes[stage]:
                    if i == j:
                        self.copy(slot, k, bit).start()
        else:
            for st, i, k, bit in self.pushes[0]:
                self.copy(self.slot(0, 0), k, bit).start()

    def drain(self):
        for stage in self.pushes:
            for st, i, k, bit in stage:
                self.copy(self.slot(st, i), k, bit).wait_send()


def aug_masks(h):
    lane = iota((1, 128), 1)
    seg = lane < 4
    lse = seg | ((lane >= LSE0 + 3 * h) & (lane < LSE0 + 3 * h + 3))
    dlt = (lane >= DEL0 + 3 * h) & (lane < DEL0 + 3 * h + 3)
    return lse.astype(F32).astype(BF16), dlt.astype(F32).astype(BF16)


def pieces(value, which):
    hi = value.astype(BF16).astype(F32)
    rest = value - hi
    mid = rest.astype(BF16).astype(F32)
    low = rest - mid
    return jnp.where(which == 0, hi, jnp.where(which == 1, mid, low))


def half_masks():
    lane = iota((1, 128), 1)
    first = (lane < HEAD_DIM).astype(F32).astype(BF16)
    return first, (lane >= HEAD_DIM).astype(F32).astype(BF16)


def grad_pass(own_a, own_b, own_aug, all_a, all_b, all_aug, p, count, split, chunk, with_b, at_point):
    masks = half_masks()
    left_a, left_b = [], []
    for e in range(2):
        lse_mask, del_mask = aug_masks(2 * p + e)
        left_a.append(jnp.concatenate([own_a * masks[e], own_aug * lse_mask], axis=1))
        left_b.append(jnp.concatenate([own_b * masks[e], own_aug * del_mask], axis=1))
    acc = [jnp.zeros((own_a.shape[0], 128), F32) for _ in range(2 if with_b else 1)]
    for c in range(count):
        here = pl.ds(c * chunk, chunk)
        ra, rb, aug = all_a(here), all_b(here), all_aug(here)
        right_a = jnp.concatenate([ra, aug], axis=1)
        right_b = jnp.concatenate([rb, aug], axis=1)
        probs = [jnp.exp(nt(left_a[e], right_a)) for e in range(2)]
        ds = [(probs[e] * nt(left_b[e], right_b)).astype(BF16) for e in range(2)]
        acc[0] = acc[0] + nn(jnp.concatenate(ds, axis=1), jnp.concatenate([ra * m for m in masks], axis=0))
        if with_b:
            both = jnp.concatenate([prob.astype(BF16) for prob in probs], axis=1)
            acc[1] = acc[1] + nn(both, jnp.concatenate([rb * m for m in masks], axis=0))
        if c + 1 == split:
            at_point(0)
    at_point(1)
    return acc if with_b else acc[0]


def mesh_bits(frames, seqs):
    rest = []
    b = 1
    while b < seqs:
        rest.append(("seq", b))
        b *= 2
    b = 2
    while b < frames:
        rest.append(("frame", b))
        b *= 2
    return rest


TILE = 16
UNROLL = 2


def at_tile(start, n):
    return pl.ds(start if isinstance(start, int) else pl.multiple_of(start, TILE), n)


def member(group, offset, fi, si):
    index = 0
    for i, (axis, bit) in enumerate(group):
        value = bit_of(fi if axis == "frame" else si, bit)
        if (offset >> i) & 1:
            value = 1 - value
            if axis == "frame":
                fi = flip(fi, bit)
            else:
                si = flip(si, bit)
        index = index + value * (1 << i)
    return (fi, si), index


def pairs_of(bits):
    return [bits[i : i + 2] for i in range(0, len(bits), 2)]


EARLY = 3584
LATE = 3 * 384 + 128
EARLY_CUTS = ((0, 1536), (1536, 2048))
LATE_CUTS = ((EARLY, 384, 0), (EARLY + 384, 384, 1), (EARLY + 768, 512, 2))
EARLY_BITS = 5
LATE_BITS = 3


def early_groups(frames, seqs):
    rest = mesh_bits(frames, seqs)
    return [[("frame", 1)], rest[:1]] + pairs_of(rest[1:])


def late_groups(frames, seqs):
    return [[("frame", 1)]] + pairs_of(mesh_bits(frames, seqs))


def landing(length, groups, most_bits):
    rows = copies = bits = 0
    for group in groups:
        others = (1 << len(group)) - 1
        bits += len(group)
        copies += others
        if bits <= most_bits:
            length >>= len(group)
            copies += others
        rows += others * length
    return rows, copies


class Piece:
    def __init__(self, start, length, groups, most_bits, land_at, sem_at, fi, si, buf, land, out, send, recv):
        self.refs = buf, land, out, send, recv
        self.steps = []
        seg, n, sem, bits = start, length, sem_at, 0
        hist = []
        for group in groups:
            bits += len(group)
            offsets = range(1, 1 << len(group))
            moves = []
            if bits <= most_bits:
                hist.append((seg, n, group))
                n >>= len(group)
                _, index = member(group, 0, fi, si)
                for d in offsets:
                    dev, other = member(group, d, fi, si)
                    moves.append((seg + other * n, land_at, sem, dev))
                    land_at, sem = land_at + n, sem + 1
                seg = seg + index * n
            else:
                for d in offsets:
                    dev, _ = member(group, d, fi, si)
                    moves.append((seg, land_at, sem, dev))
                    land_at, sem = land_at + n, sem + 1
            self.steps.append(("add", seg, n, moves))
        self.adds = len(groups)
        for old, old_n, group in reversed(hist):
            moves = []
            for d in range(1, 1 << len(group)):
                moves.append((seg, 0, sem, member(group, d, fi, si)[0]))
                sem += 1
            self.steps.append(("copy", seg, n, moves))
            seg, n = old, old_n
        self.sem_end = sem
        self.land_end = land_at
        self.total = len(self.steps)

    def copies(self, i):
        buf, land, out, send, recv = self.refs
        kind, _, n, moves = self.steps[i]
        made = []
        for give, at, sem, dev in moves:
            src = (buf if kind == "add" else out).at[at_tile(give, n), :]
            dst = land.at[at_tile(at, n), :] if kind == "add" else src
            made.append(rc(src, dst, send.at[sem], recv.at[sem], dev))
        return made

    def start(self, i):
        if i < self.total:
            for cp in self.copies(i):
                cp.start()

    def finish(self, i):
        if i < 0 or i >= self.total:
            return
        buf, land, out, _, _ = self.refs
        for cp in self.copies(i):
            cp.wait()
        kind, keep, n, moves = self.steps[i]
        if kind == "copy":
            return
        to = out if i == self.adds - 1 else buf
        chunk = max(TILE * k for k in (1, 2, 3, 4, 6, 7) if n % (TILE * k) == 0)

        def add(j, carry):
            here = at_tile(keep + j * chunk, chunk)
            value = buf[here, :].astype(F32)
            for _, at, _, _ in moves:
                value = value + land[at_tile(at + j * chunk, chunk), :].astype(F32)
            to[here, :] = value.astype(BF16)
            return carry

        lax.fori_loop(0, n // chunk, add, 0)


def partners_of(all_groups, fi, si):
    seen, devs = set(), []
    for groups in all_groups:
        for group in groups:
            for d in range(1, 1 << len(group)):
                key = tuple(sorted(group[i] for i in range(len(group)) if (d >> i) & 1))
                if key not in seen:
                    seen.add(key)
                    devs.append(member(group, d, fi, si)[0])
    return devs


EARLY_POINTS = ((2, 5, 6, 7, 8, 10, 11), (4, 6, 7, 8, 9))


def whole_kernel(
    frames, seqs, rows, cells,
    tokens, segments, small_in, g_attn, w_qkv, w_out_hbm, g_mlp, w_up_hbm, w_down_hbm, g_learn, tapmask, blockones,
    sums, own_tok, far_tok,
    xp, xg, qkv, augk, dag, da_ext, dx2_scr, learned,
    augq, o_scr, x2_scr, y_scr, vhat2_scr, vhat3_scr, rstd_scr,
    dh2_scr, u_scr, h3p, yp,
    dyp, w72_scr, spread_scr, rest_scr, gain_scr, conv_bw, conv_fw, dqkv,
    h1_scr, dh1_scr, buf, land, out, tok_send, tok_land, tsend,
    trecv, gsend, grecv, psend, precv, fsem, tsem, wsem, w_out, w_up, w_down,
):
    fi = lax.axis_index("frame")
    si = lax.axis_index("seq")
    half = frames // 2
    g = fi % half
    mine = fi // half
    total = frames * rows
    own = 2 * rows
    other = fi + half * (1 - 2 * mine)
    partner = (other, si)
    weights = [
        pltpu.make_async_copy(src, dst, wsem.at[i])
        for i, (src, dst) in enumerate(((w_out_hbm, w_out), (w_up_hbm, w_up), (w_down_hbm, w_down)))
    ]
    for cp in weights:
        cp.start()
    for k in range(2):
        body = tokens[k].astype(F32)[0:cells]
        seg = jnp.broadcast_to(segments[k : k + 1, 0:1].astype(F32), (1, 384))
        pad = jnp.zeros((rows - cells - 1 - MAPS, 384), F32)
        xp[k] = jnp.concatenate([body, seg, small_in[72 + MAPS * k : 72 + MAPS * (k + 1), :], pad], axis=0).astype(BF16)
    xg[fi] = xp[mine]
    singles = [[bit] for bit in mesh_bits(frames, seqs)]
    by_early, by_late = early_groups(frames, seqs), late_groups(frames, seqs)
    greet(partners_of((singles + [[("frame", 1)]],), fi, si))
    cut = (rows // 2 + 15) // 16 * 16
    near, far, to_partner = [], [], []
    end = 2
    for n, span in enumerate((pl.ds(0, cut), pl.ds(cut, rows - cut))):
        to_partner.append(rc(xp.at[1 - mine, span, :], xg.at[fi, span, :], tsend.at[n], trecv.at[fi + n * frames], partner))
        to_partner[n].start()
        block = lambda slot, span=span: xg.at[slot, span, :]
        for group, base in ((near, half * mine), (far, half * (1 - mine))):
            group.append(Gather(half, base, n, block, tsend, trecv, end, fi, si, n * frames))
            end = group[-1].end
    for piece in near:
        piece.run(0)
    da_block = lambda slot: dag.at[:, pl.ds(pl.multiple_of(slot * rows, rows), rows), :]
    da_near = Gather(half, 0, 0, da_block, gsend, grecv, 0, fi, si)
    da_far = Gather(half, half, 1, da_block, gsend, grecv, da_near.end, fi, si)
    refs = fi, si, buf, land, out, psend, precv
    early, late = [], []
    land_at = sem_at = 0
    for group, cuts, by, bits in ((early, EARLY_CUTS, by_early, EARLY_BITS), (late, LATE_CUTS, by_late, LATE_BITS)):
        for start, length, *_ in cuts:
            group.append(Piece(start, length, by, bits, land_at, sem_at, *refs))
            land_at, sem_at = group[-1].land_end, group[-1].sem_end

    h2_rows, a_rows, dm_rows = (pl.ds(own * k, own) for k in (4, 5, 6))

    def early_point(i):
        for piece, points in zip(early, EARLY_POINTS):
            if i in points:
                step = 1 + points.index(i)
                piece.finish(step)
                piece.start(step + 1)

    lane128 = iota((rows, 128), 1)
    row128 = iota((rows, 128), 0)
    valid_row = row128 < cells

    w72_scr[...] = sixteen(small_in[0:72, :]).astype(BF16)
    square_r, square_c = iota((128, 128), 0), iota((128, 128), 1)
    repeat = ((square_c & 7) == square_r).astype(F32)
    same_tap = (((square_r >> 3) == (square_c >> 3)) & (square_r < 72)).astype(F32)
    for layer in range(3):
        by_tap = small_in[88 + 72 * layer : 160 + 72 * layer, 0:128]
        conv_bw[layer] = sixteen(by_tap)
        by_tap = jnp.concatenate([by_tap, jnp.zeros((56, 128), F32)], axis=0)
        conv_fw[layer] = nn(repeat[0:16], nn(by_tap, repeat, HIGH) * same_tap, HIGH)

    def project(f, carry):
        x = xg[f].astype(F32)
        seg = x[cells : cells + 1, 0:128]
        x = jnp.where(iota(x.shape, 0) < cells, x, 0.0)
        vhat, _ = normed(x)
        h1 = (vhat * g_attn[...].reshape(1, -1)).astype(BF16)
        base = pl.multiple_of(f * rows, rows)
        whole = nn(h1, w_qkv[...])
        for b in range(9):
            part = whole[:, 128 * b : 128 * b + 128]
            if b < 3:
                part = part * HEAD_DIM**-0.5
            qkv[b, pl.ds(base, rows), :] = part.astype(BF16)
        same = (lane128.astype(F32) == seg) & valid_row
        augk[pl.ds(base, rows), :] = jnp.where(
            lane128 < 4, jnp.where(same, 0.0, -BIG), jnp.where(lane128 < AUG_END, -1.0, 0.0)
        ).astype(BF16)
        return carry

    def run(gather, stage):
        for piece in gather:
            piece.run(stage)

    def project_range(gather, start, core):
        n = 1 << gather[0].n

        def one(j, carry):
            return project(gather[0].nearby(j, core), carry)

        lax.fori_loop(start, n, one, 0, unroll=min(n - start, UNROLL))

    last = near[0].last
    project(fi, 0)
    run(near, 1)
    for n, piece in enumerate(far):
        here = piece.block(other)
        rc(here, here, tsend.at[0], trecv.at[other + n * frames], partner).wait_recv()
        piece.run(0)
    project(other, 0)
    for stage in range(2, last):
        run(near, stage)
    for stage in range(1, last):
        run(far, stage)
        if stage == 1:
            project_range(near, 1, False)
    run(near, last)
    project_range(far, 1, False)
    project_range(near, 0, True)
    run(far, last)
    project_range(far, 0, True)
    for cp in to_partner:
        cp.wait_send()
    for piece in near + far:
        piece.drain()

    ones = jnp.ones((frames * rows, 128), BF16)

    for k in range(2):
        f = g + half * k
        seg = xg[f].astype(F32)[cells : cells + 1, 0:128]
        same = (lane128.astype(F32) == seg) & valid_row & (lane128 < 4)
        augq[k * rows : (k + 1) * rows, :] = same.astype(F32)

    together = 2 if frames <= 16 else 1

    def attend(step, carry):
        p = step // (4 // together)
        k = step % 2
        f = g + half * k
        q = qkv[p, pl.ds(pl.multiple_of(f * rows, rows), rows), :]
        mine = pl.ds(pl.multiple_of(k * rows, rows), rows)
        aug = augq[mine, :]
        seg_aug = jnp.where(lane128 < 4, aug, 0.0).astype(BF16)
        keys = jnp.concatenate([qkv[3 + p], augk[...]], axis=1)
        values = jnp.concatenate([qkv[6 + p], ones], axis=1)
        mixed = o_scr[p, mine, :] if together == 1 else 0.0
        for n in range(together):
            e = n if together == 2 else (step // 2) % 2
            keep = (lane128 >= HEAD_DIM * e) & (lane128 < HEAD_DIM * (e + 1))
            s = nt(jnp.concatenate([q * keep.astype(F32).astype(BF16), seg_aug], axis=1), keys)
            top = jnp.max(s, axis=1, keepdims=True)
            prob = jnp.exp(s - top).astype(BF16)
            o = nn(prob, values)
            weight = o[:, 128:]
            mixed = jnp.where(keep, o[:, :128] / weight, mixed)
            lse = top + jnp.log(weight)
            which = lane128 - (LSE0 + 3 * (2 * p + e))
            aug = jnp.where((which >= 0) & (which < 3), pieces(lse, which), aug)
        augq[mine, :] = aug
        o_scr[p, mine, :] = mixed
        return carry

    lax.fori_loop(0, 4 * PAIRS // together, attend, 0)

    for cp in weights:
        cp.wait()

    def apart(fn):
        pl.when(fi >= 0)(fn)

    @apart
    def _():
        a = jnp.concatenate([o_scr[p].astype(BF16) for p in range(PAIRS)], axis=1)
        out[a_rows, :] = a
        both = jnp.concatenate([xg[g], xg[g + half]], axis=0).astype(F32)
        r = iota(both.shape, 0)
        x = jnp.where((r < cells) | ((r >= rows) & (r < rows + cells)), both, 0.0)
        x2 = x + nn(a, w_out[...])
        x2_scr[...] = x2
        y_scr[...] = x2
        vhat, rstd = normed(x2)
        rstd_scr[...] = jnp.broadcast_to(rstd, (own, 128))
        vhat2_scr[...] = vhat
        out[h2_rows, :] = (vhat * g_mlp[...].reshape(1, -1)).astype(BF16)

    def mlp(j, carry):
        cols = pl.ds(pl.multiple_of(384 * j, 384), 384)
        u = nn(out[h2_rows, :], w_up[:, cols])
        u_scr[j] = u
        hid = gelu(u).astype(BF16)
        out[pl.ds(pl.multiple_of(own * j, 16), own), :] = hid
        y_scr[...] += nn(hid, w_down[cols, :])
        return carry

    lax.fori_loop(0, 4, mlp, 0)

    @apart
    def _():
        y = y_scr[...]
        vhat, rstd = normed(y)
        vhat3_scr[...] = vhat
        rstd_scr[...] = jnp.where(iota((own, 128), 1) < 64, rstd_scr[...], rstd)
        h3 = (vhat * g_learn[...].reshape(1, -1)).astype(BF16)
        for k in range(2):
            yp[256 * k : 256 * k + rows, :] = y[k * rows : (k + 1) * rows, :]
            yp[256 * k + rows : 256 * k + 256, :] = jnp.zeros((256 - rows, 384), F32)
            h3p[256 * k : 256 * k + rows, :] = h3[k * rows : (k + 1) * rows, :]
            h3p[256 * k + rows : 256 * k + 256, :] = jnp.zeros((256 - rows, 384), BF16)

    def shift_of(t):
        return GRID * (t // 3 - 1) + (t % 3 - 1)

    def moved(v, s):
        return v if s == 0 else pltpu.roll(v, (-s) % WIDE, 1)

    def tap(t):
        return tapmask[t : t + 1, :]

    def im2col(v):
        parts = [moved(v, shift_of(t)) * tap(t) for t in range(9)]
        return jnp.concatenate(parts + [jnp.zeros((56, WIDE), F32)], axis=0)

    def spread_of(v):
        return jnp.concatenate([moved(v, -shift_of(t)) * tap(8 - t) for t in range(9)], axis=0)

    @apart
    def _():
        taps = nt(w72_scr[...], h3p[...])
        z1 = jnp.zeros((MAPS, WIDE), F32)
        for t in range(9):
            z1 = z1 + moved(taps[8 * t : 8 * t + 8, :], shift_of(t)) * tap(t)
        zs = [z1]
        cols_of = []
        for layer in range(3):
            col = im2col(gelu(zs[-1]))
            cols_of.append(col)
            zs.append(nn(conv_fw[layer], col, HIGH)[0:MAPS])
        maps = tap(4) / (1.0 + jnp.exp(-zs[3]))
        dmaps = []
        for k in range(2):
            f = g + half * k
            dl = xg[f].astype(F32)[cells + 1 : cells + 1 + MAPS, :] * (1.0 / cells)
            dl = sixteen(dl)
            mk = sixteen(maps[:, 256 * k : 256 * k + 256])
            yk = yp[256 * k : 256 * k + 256, :]
            learned[k] = nn(mk, yk, HIGH)[0:MAPS] * (1.0 / cells)
            dmaps.append(nt(dl, yk, HIGH)[0:MAPS])
            dyp[256 * k : 256 * k + 256, :] = tn(mk, dl, HIGH)
        dz = jnp.concatenate(dmaps, axis=1) * maps * (1.0 - maps)
        small = []
        for layer in (2, 1, 0):
            dw = nt(sixteen(dz), cols_of[layer], HIGH)[0:MAPS]
            small.insert(0, jnp.concatenate([dw, jnp.zeros((MAPS, 256), F32)], axis=1))
            dz = tn(conv_bw[layer], sixteen(spread_of(dz)), HIGH)[0:MAPS] * gelu_grad(zs[layer])
        dz = dz.astype(BF16).astype(F32) * tap(4)
        spread_scr[...] = sixteen(spread_of(dz)).astype(BF16)
        rest_scr[...] = jnp.concatenate(small + [jnp.zeros((8, 384), F32)], axis=0)

    @apart
    def _():
        dh3 = tn(spread_scr[...], w72_scr[...])
        dh3 = jnp.concatenate([dh3[0:rows], dh3[256 : 256 + rows]], axis=0)
        dy, dg3 = norm_back(vhat3_scr[...], rstd_scr[:, 64:65], dh3, g_learn[...].reshape(1, -1))
        dy = dy + jnp.concatenate([dyp[0:rows, :], dyp[256 : 256 + rows, :]], axis=0)
        y_scr[...] = dy
        out[dm_rows, :] = dy.astype(BF16)
        dh2_scr[...] = jnp.zeros((own, 384), F32)
        gain_scr[...] = jnp.concatenate([dg3, jnp.zeros((7, 384), F32)], axis=0)

    def mlp_back(j, carry):
        cols = pl.ds(pl.multiple_of(384 * j, 384), 384)
        dm = out[dm_rows, :]
        du = (nt(dm, w_down[cols, :]) * gelu_grad(u_scr[j])).astype(BF16)
        buf[cols, :] = tn(out[h2_rows, :], du).astype(BF16)
        buf[pl.ds(pl.multiple_of(1536 + 384 * j, 384), 384), :] = tn(out[pl.ds(pl.multiple_of(own * j, 16), own), :], dm).astype(BF16)
        dh2_scr[...] += nt(du, w_up[:, cols])
        return carry

    lax.fori_loop(0, 4, mlp_back, 0)
    early[0].start(0)

    @apart
    def _():
        dx2, dg2 = norm_back(vhat2_scr[...], rstd_scr[:, 0:1], dh2_scr[...], g_mlp[...].reshape(1, -1))
        dx2 = dx2 + y_scr[...]
        dx2_scr[...] = dx2
        out[dm_rows, :] = dx2.astype(BF16)
        gains = jnp.concatenate([dg2, gain_scr[0:1, :], jnp.zeros((6, 384), F32)], axis=0)
        d_first = nn(spread_scr[...], h3p[...])[0:72]
        small = [d_first, gains, rest_scr[...], jnp.zeros((16, 384), F32)]
        buf[3456:3584, :] = jnp.concatenate(small, axis=0).astype(BF16)

    early[0].finish(0)
    early[0].start(1)

    @apart
    def _():
        dzz = out[dm_rows, :]
        buf[3072:3456, :] = tn(out[a_rows, :], dzz).astype(BF16)
        da = nt(dzz, w_out[...]).astype(BF16)
        prod = jnp.concatenate([o_scr[p] for p in range(PAIRS)], axis=1) * da.astype(F32)
        lane = iota((own, 128), 1)
        which = lane - DEL0
        which = which - 3 * (which // 3)
        delta = pieces(nn(prod, blockones[...], HIGH), which)
        full = jnp.where((lane >= DEL0) & (lane < AUG_END), delta, augq[...])
        full = full.astype(BF16)
        for p in range(PAIRS):
            da_ext[p] = da[:, 128 * p : 128 * p + 128]
        da_ext[PAIRS] = full
        for k in range(2):
            there = pl.ds(pl.multiple_of((g + half * k) * rows, rows), rows)
            dag[:, there, :] = da_ext[:, k * rows : (k + 1) * rows, :]

    early[1].start(0)
    da_near.run(0)
    da_far.run(0)
    x = jnp.concatenate([xg[g], xg[g + half]], axis=0).astype(F32)
    r = iota(x.shape, 0)
    x = jnp.where((r < cells) | ((r >= rows) & (r < rows + cells)), x, 0.0)
    vhat, _ = normed(x)
    h1_scr[...] = (vhat * g_attn[...].reshape(1, -1)).astype(BF16)
    dh1_scr[...] = jnp.zeros((own, 384), F32)
    buf[EARLY + 1152 :, :] = jnp.zeros((128, 384), BF16)
    early[1].finish(0)
    early[1].start(1)

    def own_rows(b):
        at = [qkv[b, pl.ds(pl.multiple_of((g + half * k) * rows, rows), rows), :] for k in range(2)]
        return jnp.concatenate(at, axis=0)

    own_augk = jnp.concatenate(
        [augk[pl.ds(pl.multiple_of((g + half * k) * rows, rows), rows), :] for k in range(2)], axis=0
    )
    chunk = 256
    pieces_n = total // chunk
    split = (pieces_n + 1) // 2

    def query_pass(p, carry):
        def at_point(j):
            for k in range(PAIRS):
                i = 2 * k + j

                def point(i=i):
                    early_point(i)
                    stage = i // 2 + 1
                    if i % 2 == 1 and stage < da_near.last:
                        da_near.run(stage)
                        da_far.run(stage)

                pl.when(p == k)(point)

        dq = grad_pass(
            own_rows(p), da_ext[p], da_ext[PAIRS],
            lambda i: qkv[3 + p, i, :], lambda i: qkv[6 + p, i, :], lambda i: augk[i, :],
            p, pieces_n, split, chunk, False, at_point,
        )
        dqkv[p] = (dq * HEAD_DIM**-0.5).astype(BF16)
        return carry

    lax.fori_loop(0, PAIRS, query_pass, 0)
    for gather in (da_near, da_far):
        gather.run(gather.last)
        gather.drain()

    def key_pass(p, carry):
        def at_point(j):
            for k in range(PAIRS):
                i = 2 * PAIRS + 2 * k + j

                def point(i=i, k=k):
                    early_point(i)
                    for piece, (_, _, after) in zip(late, LATE_CUTS):
                        if after < k:
                            step = 2 * (k - after - 1) + j
                            piece.finish(step)
                            piece.start(step + 1)

                pl.when(p == k)(point)

        dk, dv = grad_pass(
            own_rows(3 + p), own_rows(6 + p), own_augk,
            lambda i: qkv[p, i, :], lambda i: dag[p, i, :], lambda i: dag[PAIRS, i, :],
            p, pieces_n, split, chunk, True, at_point,
        )
        d = jnp.concatenate([dqkv[p], dk.astype(BF16), dv.astype(BF16)], axis=1)
        buf[pl.ds(pl.multiple_of(EARLY + 384 * p, 128), 384), :] = tn(h1_scr[...], d).astype(BF16)
        w = jnp.concatenate(
            [w_qkv[:, pl.ds(pl.multiple_of(384 * b + 128 * p, 128), 128)] for b in range(3)], axis=1
        )
        dh1_scr[...] += nt(d, w)
        for piece, (_, _, after) in zip(late, LATE_CUTS):
            if after < PAIRS - 1:
                pl.when(p == after)(functools.partial(piece.start, 0))
        return carry

    lax.fori_loop(0, PAIRS, key_pass, 0)
    dx, dg = norm_back(*normed(x), dh1_scr[...], g_attn[...].reshape(1, -1))
    buf[EARLY + 1152 : EARLY + 1168, :] = jnp.concatenate([dg, jnp.zeros((15, 384), F32)], axis=0).astype(BF16)
    for piece, (_, _, after) in zip(late, LATE_CUTS):
        if after == PAIRS - 1:
            piece.start(0)
    dx = dx + dx2_scr[...]
    for k in range(2):
        tail = jnp.concatenate([learned[k], jnp.zeros((rows - cells - MAPS, 384), F32)], axis=0)
        whole = jnp.concatenate([dx[k * rows : k * rows + cells, :], tail], axis=0)

        @pl.when(mine == k)
        def _():
            own_tok[...] = whole

        @pl.when(mine != k)
        def _():
            tok_send[...] = whole.astype(BF16)

    tok_copy = rc(tok_send, tok_land, tsem.at[0], tsem.at[1], (fi + half * (1 - 2 * mine), si))
    tok_copy.start()
    give = [
        pltpu.make_async_copy(out.at[pl.ds(at, n), :], sums.at[pl.ds(at, n), :], fsem.at[i])
        for i, (at, n) in enumerate((EARLY_CUTS[0], (EARLY_CUTS[1][0], EARLY + LATE - EARLY_CUTS[1][0])))
    ]
    running = [(piece, 1 + len(points)) for piece, points in zip(early, EARLY_POINTS)]
    running += [(piece, 2 * (PAIRS - 1 - after)) for piece, (_, _, after) in zip(late, LATE_CUTS)]
    for piece, n in running[:1]:
        for i in range(n, piece.total):
            piece.finish(i)
            piece.start(i + 1)
    give[0].start()
    for i in range(max(piece.total - n for piece, n in running[1:])):
        for piece, n in running[1:]:
            piece.finish(n + i)
            piece.start(n + i + 1)
    give[1].start()
    tok_copy.wait()
    far_tok[...] = tok_land[...]
    for cp in give:
        cp.wait()


def finish_kernel(cells, half, sums, own_tok, far_tok, d_tokens, learned, g_attn, w_qkv, w_out, g_mlp, w_up, w_down, g_learn, first, rest):
    for j in range(4):
        w_up[:, 384 * j : 384 * j + 384] = sums[384 * j : 384 * j + 384, :].astype(F32)
    w_down[...] = sums[1536:3072, :].astype(F32)
    w_out[...] = sums[3072:3456, :].astype(F32)
    small = sums[3456:3584, :].astype(F32)
    first[...] = small[0:72].reshape(9, MAPS, 384)
    for n in range(27):
        layer, t = n // 9, n % 9
        rest[n] = small[80 + MAPS * layer : 88 + MAPS * layer, MAPS * t : MAPS * (t + 1)]
    g_mlp[...] = small[72:73].reshape(-1)
    g_learn[...] = small[73:74].reshape(-1)
    for p in range(PAIRS):
        block = sums[EARLY + 384 * p : EARLY + 384 * p + 384, :].astype(F32)
        for b in range(3):
            w_qkv[:, 384 * b + 128 * p : 384 * b + 128 * p + 128] = block[:, 128 * b : 128 * b + 128]
    g_attn[...] = sums[EARLY + 1152 : EARLY + 1168, :].astype(F32)[0:1].reshape(-1)
    mine = lax.axis_index("frame") // half
    far = far_tok[...].astype(F32)
    near = own_tok[...]
    d_tokens[mine] = near[0:cells]
    d_tokens[1 - mine] = far[0:cells]
    a, b = near[cells : cells + MAPS], far[cells : cells + MAPS]
    learned[...] = jnp.where(mine == 0, jnp.concatenate([a, b], axis=0), jnp.concatenate([b, a], axis=0)).astype(BF16)


def vspec(n):
    return [pl.BlockSpec(memory_space=VMEM)] * n


def params(collective=None, mib=56):
    if collective is None:
        return pltpu.CompilerParams(vmem_limit_bytes=mib * MIB)
    return pltpu.CompilerParams(collective_id=collective, has_side_effects=True, vmem_limit_bytes=mib * MIB)


def tap_masks():
    p = np.arange(WIDE) % 256
    px, py = p // GRID, p % GRID
    out = np.zeros((16, WIDE), np.float32)
    for t in range(9):
        r, c = t // 3 - 1, t % 3 - 1
        out[t] = (p < CELLS) & (px + r >= 0) & (px + r < GRID) & (py + c >= 0) & (py + c < GRID)
    return out


def head_sums():
    out = np.zeros((HEADS * HEAD_DIM, 128), np.float32)
    for h in range(HEADS):
        out[h * HEAD_DIM : (h + 1) * HEAD_DIM, DEL0 + 3 * h : DEL0 + 3 * h + 3] = 1.0
    return out


def on_device(frames, seqs, tokens, segments, g_attn, w_qkv, w_out, g_mlp, w_up, w_down, g_learn, conv_first, conv_rest, d_learned):
    _, cells, width = tokens.shape
    rows = -(-(cells + 1 + MAPS) // 16) * 16
    own = 2 * rows
    total = frames * rows
    n_sems = 2 + 16 * frames
    sds = jax.ShapeDtypeStruct
    rest = conv_rest.transpose(0, 2, 3, 1, 4).reshape(27 * MAPS, MAPS)
    small_in = jnp.concatenate(
        [
            conv_first.transpose(1, 2, 0, 3).reshape(9 * MAPS, width),
            d_learned.reshape(2 * MAPS, width),
            jnp.pad(rest, ((0, 0), (0, width - MAPS))),
        ],
        axis=0,
    ).astype(F32)
    n_all = EARLY + LATE
    sizes = [landing(n, early_groups(frames, seqs), EARLY_BITS) for _, n in EARLY_CUTS]
    sizes += [landing(n, late_groups(frames, seqs), LATE_BITS) for _, n, _ in LATE_CUTS]
    land_n, copies = (sum(v) for v in zip(*sizes))
    anywhere = pl.BlockSpec(memory_space=pl.ANY)
    sums, own_tok, far_tok = pl.pallas_call(
        functools.partial(whole_kernel, frames, seqs, rows, cells),
        out_shape=[sds((n_all, width), BF16), sds((rows, width), F32), sds((rows, width), BF16)],
        in_specs=vspec(5) + [anywhere] + vspec(1) + [anywhere] * 2 + vspec(3),
        out_specs=[anywhere] + vspec(2),
        scratch_shapes=[
            VMEM((2, rows, width), BF16),
            VMEM((frames, rows, width), BF16),
            VMEM((9, total, 128), BF16),
            VMEM((total, 128), BF16),
            VMEM((PAIRS + 1, total, 128), BF16),
            VMEM((PAIRS + 1, own, 128), BF16),
            VMEM((own, width), F32),
            VMEM((2, MAPS, width), F32),
            VMEM((own, 128), F32),
            VMEM((PAIRS, own, 128), F32),
            VMEM((own, width), F32),
            VMEM((own, width), F32),
            VMEM((own, width), F32),
            VMEM((own, width), F32),
            VMEM((own, 128), F32),
            VMEM((own, width), F32),
            VMEM((4, own, width), F32),
            VMEM((WIDE, width), BF16),
            VMEM((WIDE, width), F32),
            VMEM((WIDE, width), F32),
            VMEM((80, width), BF16),
            VMEM((80, WIDE), BF16),
            VMEM((32, width), F32),
            VMEM((8, width), F32),
            VMEM((3, 80, 128), F32),
            VMEM((3, 16, 128), F32),
            VMEM((PAIRS, own, 128), BF16),
            VMEM((own, width), BF16),
            VMEM((own, width), F32),
            VMEM((n_all, width), BF16),
            VMEM((land_n, width), BF16),
            VMEM((n_all, width), BF16),
            VMEM((rows, width), BF16),
            VMEM((rows, width), BF16),
            pltpu.SemaphoreType.DMA((n_sems,)),
            pltpu.SemaphoreType.DMA((2 * frames,)),
            pltpu.SemaphoreType.DMA((n_sems,)),
            pltpu.SemaphoreType.DMA((frames,)),
            pltpu.SemaphoreType.DMA((copies,)),
            pltpu.SemaphoreType.DMA((copies,)),
            pltpu.SemaphoreType.DMA((2,)),
            pltpu.SemaphoreType.DMA((2,)),
            pltpu.SemaphoreType.DMA((3,)),
            VMEM((width, width), BF16),
            VMEM((width, 4 * width), BF16),
            VMEM((4 * width, width), BF16),
        ],
        compiler_params=params(0, 61),
        name="layer",
    )(
        jnp.pad(tokens, ((0, 0), (0, rows - cells), (0, 0))), segments, small_in,
        g_attn, w_qkv, w_out, g_mlp, w_up, w_down, g_learn,
        jnp.asarray(tap_masks()), jnp.asarray(head_sums()),
    )
    d_tokens, learned_all, dg_attn, d_w_qkv, d_w_out, dg_mlp, d_w_up, d_w_down, dg_learn, first, rest = pl.pallas_call(
        functools.partial(finish_kernel, cells, frames // 2),
        out_shape=[
            sds((2, cells, width), F32),
            sds((2 * MAPS, width), BF16),
            sds((width,), F32),
            sds((width, 3 * width), F32),
            sds((width, width), F32),
            sds((width,), F32),
            sds((width, 4 * width), F32),
            sds((4 * width, width), F32),
            sds((width,), F32),
            sds((9, MAPS, width), F32),
            sds((27, MAPS, MAPS), F32),
        ],
        in_specs=vspec(3),
        out_specs=vspec(11),
        compiler_params=params(),
        name="outputs",
    )(sums, own_tok, far_tok)
    d_first = first.reshape(3, 3, MAPS, width).transpose(2, 0, 1, 3)
    d_rest = rest.reshape(3, 3, 3, MAPS, MAPS).transpose(0, 3, 1, 2, 4)
    return (
        learned_all.reshape(2, MAPS, width), d_tokens, dg_attn, d_w_qkv, d_w_out, dg_mlp, d_w_up, d_w_down, dg_learn, d_first, d_rest,
    )


def solution(mesh):
    frames, seqs = mesh.shape["frame"], mesh.shape["seq"]
    both = P("seq", "frame", None)
    in_specs = (both, P("seq", "frame"), *([P()] * 9), both)
    out_specs = (both, both, *([P()] * 9))
    return jax.shard_map(
        functools.partial(on_device, frames, seqs),
        mesh=mesh,
        in_specs=in_specs,
        out_specs=out_specs,
        check_vma=False,
    )
```

```python
import functools

import jax
import jax.numpy as jnp
import numpy as np
from jax import lax
from jax.experimental import pallas as pl
from jax.experimental.pallas import tpu as pltpu
from jax.sharding import PartitionSpec as P

HEADS = 6
HEAD_DIM = 64
MAPS = 8
GRID = 14
CELLS = GRID * GRID
PAIRS = HEADS // 2
WIDE = 512
BIG = 1e30
LSE0 = 4
DEL0 = 4 + 3 * HEADS
AUG_END = 4 + 6 * HEADS
F32 = jnp.float32
BF16 = jnp.bfloat16
HIGH = lax.Precision.HIGHEST
MESH = pl.DeviceIdType.MESH
VMEM = pltpu.VMEM
MIB = 1 << 20


def nn(a, b, precision=None):
    return lax.dot_general(a, b, (((1,), (0,)), ((), ())), precision=precision, preferred_element_type=F32)


def nt(a, b, precision=None):
    return lax.dot_general(a, b, (((1,), (1,)), ((), ())), precision=precision, preferred_element_type=F32)


def tn(a, b, precision=None):
    return lax.dot_general(a, b, (((0,), (0,)), ((), ())), precision=precision, preferred_element_type=F32)


def iota(shape, dim):
    return lax.broadcasted_iota(jnp.int32, shape, dim)


def sixteen(v):
    return jnp.concatenate([v, jnp.zeros((8, v.shape[1]), v.dtype)], axis=0)


def normed(x):
    centered = x - jnp.mean(x, axis=-1, keepdims=True)
    rstd = lax.rsqrt(jnp.mean(centered * centered, axis=-1, keepdims=True) + 1e-06)
    return centered * rstd, rstd


def norm_back(vhat, rstd, dout, gain):
    e = dout * gain
    mean_e = jnp.mean(e, axis=-1, keepdims=True)
    mean_ev = jnp.mean(e * vhat, axis=-1, keepdims=True)
    return rstd * (e - mean_e - vhat * mean_ev), jnp.sum(dout * vhat, axis=0, keepdims=True)


C0 = 0.7978845608028654
C1 = 0.044715


def gelu(u):
    return 0.5 * u * (1.0 + jnp.tanh(C0 * (u + C1 * u * u * u)))


def gelu_grad(u):
    t = jnp.tanh(C0 * (u + C1 * u * u * u))
    return 0.5 * (1.0 + t) + 0.5 * u * (1.0 - t * t) * (C0 + (3.0 * C0 * C1) * u * u)


def flip(v, b):
    return v + b * (1 - 2 * ((v // b) % 2))


def bit_of(v, b):
    return (v // b) % 2


def rc(src, dst, send, recv, dev):
    return pltpu.make_async_remote_copy(
        src_ref=src, dst_ref=dst, send_sem=send, recv_sem=recv, device_id=dev, device_id_type=MESH
    )


def greet(partners):
    barrier = pltpu.get_barrier_semaphore()
    for dev in partners:
        pl.semaphore_signal(barrier, inc=1, device_id=dev, device_id_type=MESH)
    pl.semaphore_wait(barrier, len(partners))


class Gather:
    def __init__(self, half, base, turn, block, send, recv, first, fi, si, shift=0):
        self.shift = shift
        self.g, self.base, self.block, self.send, self.recv = fi % half, base, block, send, recv
        self.fi, self.si = fi, si
        bits = []
        b = 2
        while b < half:
            bits.append(b)
            b *= 2
        n = len(bits)
        self.n = n
        self.order = bits[turn % n :] + bits[: turn % n] if n else []
        self.pushes = [[] for _ in range(n + 2)]
        count = first
        for stage in range(n + 1):
            for j in range(1 << max(stage - 1, 0)):
                for bit in self.order[stage:] + [1]:
                    self.pushes[stage].append((stage, j, count, bit))
                    count += 1
        self.end = count
        self.last = n + 1

    def delta(self, bit):
        return bit * (1 - 2 * bit_of(self.g, bit))

    def arrivals(self, stage):
        return 1 << (self.n if stage == self.last else stage - 1)

    def slot(self, stage, j):
        at = self.base + self.g
        if stage == 0:
            return at
        passed = self.order if stage == self.last else self.order[: stage - 1]
        for k, bit in enumerate(passed):
            at = at + ((j // (1 << k)) % 2) * self.delta(bit)
        return at + self.delta(1 if stage == self.last else self.order[stage - 1])

    def nearby(self, j, core):
        at = self.base + self.g
        for k, bit in enumerate(self.order):
            at = at + ((j // (1 << k)) % 2) * self.delta(bit)
        return at + self.delta(1) if core else at

    def copy(self, slot, k, bit):
        ref = self.block(slot)
        return rc(ref, ref, self.send.at[k], self.recv.at[slot + self.shift], (flip(self.fi, bit), self.si))

    def run(self, stage):
        if stage > 0:
            for j in range(self.arrivals(stage)):
                slot = self.slot(stage, j)
                self.copy(slot, 0, 1).wait_recv()
                for st, i, k, bit in self.pushes[stage]:
                    if i == j:
                        self.copy(slot, k, bit).start()
        else:
            for st, i, k, bit in self.pushes[0]:
                self.copy(self.slot(0, 0), k, bit).start()

    def drain(self):
        for stage in self.pushes:
            for st, i, k, bit in stage:
                self.copy(self.slot(st, i), k, bit).wait_send()


def aug_masks(h):
    lane = iota((1, 128), 1)
    seg = lane < 4
    lse = seg | ((lane >= LSE0 + 3 * h) & (lane < LSE0 + 3 * h + 3))
    dlt = (lane >= DEL0 + 3 * h) & (lane < DEL0 + 3 * h + 3)
    return lse.astype(F32).astype(BF16), dlt.astype(F32).astype(BF16)


def pieces(value, which):
    hi = value.astype(BF16).astype(F32)
    rest = value - hi
    mid = rest.astype(BF16).astype(F32)
    low = rest - mid
    return jnp.where(which == 0, hi, jnp.where(which == 1, mid, low))


def half_masks():
    lane = iota((1, 128), 1)
    first = (lane < HEAD_DIM).astype(F32).astype(BF16)
    return first, (lane >= HEAD_DIM).astype(F32).astype(BF16)


def grad_pass(own_a, own_b, own_aug, all_a, all_b, all_aug, p, count, split, chunk, with_b, at_point):
    masks = half_masks()
    left_a, left_b = [], []
    for e in range(2):
        lse_mask, del_mask = aug_masks(2 * p + e)
        left_a.append(jnp.concatenate([own_a * masks[e], own_aug * lse_mask], axis=1))
        left_b.append(jnp.concatenate([own_b * masks[e], own_aug * del_mask], axis=1))
    acc = [jnp.zeros((own_a.shape[0], 128), F32) for _ in range(2 if with_b else 1)]
    for c in range(count):
        here = pl.ds(c * chunk, chunk)
        ra, rb, aug = all_a(here), all_b(here), all_aug(here)
        right_a = jnp.concatenate([ra, aug], axis=1)
        right_b = jnp.concatenate([rb, aug], axis=1)
        probs = [jnp.exp(nt(left_a[e], right_a)) for e in range(2)]
        ds = [(probs[e] * nt(left_b[e], right_b)).astype(BF16) for e in range(2)]
        acc[0] = acc[0] + nn(jnp.concatenate(ds, axis=1), jnp.concatenate([ra * m for m in masks], axis=0))
        if with_b:
            both = jnp.concatenate([prob.astype(BF16) for prob in probs], axis=1)
            acc[1] = acc[1] + nn(both, jnp.concatenate([rb * m for m in masks], axis=0))
        if c + 1 == split:
            at_point(0)
    at_point(1)
    return acc if with_b else acc[0]


def mesh_bits(frames, seqs):
    rest = []
    b = 1
    while b < seqs:
        rest.append(("seq", b))
        b *= 2
    b = 2
    while b < frames:
        rest.append(("frame", b))
        b *= 2
    return rest


TILE = 16
UNROLL = 4


def at_tile(start, n):
    return pl.ds(start if isinstance(start, int) else pl.multiple_of(start, TILE), n)


def member(group, offset, fi, si):
    index = 0
    for i, (axis, bit) in enumerate(group):
        value = bit_of(fi if axis == "frame" else si, bit)
        if (offset >> i) & 1:
            value = 1 - value
            if axis == "frame":
                fi = flip(fi, bit)
            else:
                si = flip(si, bit)
        index = index + value * (1 << i)
    return (fi, si), index


def pairs_of(bits):
    return [bits[i : i + 2] for i in range(0, len(bits), 2)]


EARLY = 3584
LATE = 3 * 384 + 128
EARLY_CUTS = ((0, 1536), (1536, 2048))
LATE_CUTS = ((EARLY, 1280, 2),)
EARLY_BITS = 5
LATE_BITS = 3


def early_groups(frames, seqs):
    rest = mesh_bits(frames, seqs)
    return [[("frame", 1)], rest[:1]] + pairs_of(rest[1:])


def late_groups(frames, seqs):
    return [[("frame", 1)]] + pairs_of(mesh_bits(frames, seqs))


def landing(length, groups, most_bits):
    rows = copies = bits = 0
    for group in groups:
        others = (1 << len(group)) - 1
        bits += len(group)
        copies += others
        if bits <= most_bits:
            length >>= len(group)
            copies += others
        rows += others * length
    return rows, copies


class Piece:
    def __init__(self, start, length, groups, most_bits, land_at, sem_at, fi, si, buf, land, out, send, recv):
        self.refs = buf, land, out, send, recv
        self.steps = []
        seg, n, sem, bits = start, length, sem_at, 0
        hist = []
        for group in groups:
            bits += len(group)
            offsets = range(1, 1 << len(group))
            moves = []
            if bits <= most_bits:
                hist.append((seg, n, group))
                n >>= len(group)
                _, index = member(group, 0, fi, si)
                for d in offsets:
                    dev, other = member(group, d, fi, si)
                    moves.append((seg + other * n, land_at, sem, dev))
                    land_at, sem = land_at + n, sem + 1
                seg = seg + index * n
            else:
                for d in offsets:
                    dev, _ = member(group, d, fi, si)
                    moves.append((seg, land_at, sem, dev))
                    land_at, sem = land_at + n, sem + 1
            self.steps.append(("add", seg, n, moves))
        self.adds = len(groups)
        for old, old_n, group in reversed(hist):
            moves = []
            for d in range(1, 1 << len(group)):
                moves.append((seg, 0, sem, member(group, d, fi, si)[0]))
                sem += 1
            self.steps.append(("copy", seg, n, moves))
            seg, n = old, old_n
        self.sem_end = sem
        self.land_end = land_at
        self.total = len(self.steps)

    def copies(self, i):
        buf, land, out, send, recv = self.refs
        kind, _, n, moves = self.steps[i]
        made = []
        for give, at, sem, dev in moves:
            src = (buf if kind == "add" else out).at[at_tile(give, n), :]
            dst = land.at[at_tile(at, n), :] if kind == "add" else src
            made.append(rc(src, dst, send.at[sem], recv.at[sem], dev))
        return made

    def start(self, i):
        if i < self.total:
            for cp in self.copies(i):
                cp.start()

    def finish(self, i):
        if i < 0 or i >= self.total:
            return
        buf, land, out, _, _ = self.refs
        for cp in self.copies(i):
            cp.wait()
        kind, keep, n, moves = self.steps[i]
        if kind == "copy":
            return
        to = out if i == self.adds - 1 else buf
        chunk = max(TILE * k for k in (1, 2, 3, 4, 6, 7) if n % (TILE * k) == 0)

        def add(j, carry):
            here = at_tile(keep + j * chunk, chunk)
            value = buf[here, :].astype(F32)
            for _, at, _, _ in moves:
                value = value + land[at_tile(at + j * chunk, chunk), :].astype(F32)
            to[here, :] = value.astype(BF16)
            return carry

        lax.fori_loop(0, n // chunk, add, 0)


def partners_of(all_groups, fi, si):
    seen, devs = set(), []
    for groups in all_groups:
        for group in groups:
            for d in range(1, 1 << len(group)):
                key = tuple(sorted(group[i] for i in range(len(group)) if (d >> i) & 1))
                if key not in seen:
                    seen.add(key)
                    devs.append(member(group, d, fi, si)[0])
    return devs


EARLY_POINTS = ((3, 6, 7, 8, 9, 11), (5, 7, 8, 9, 10))


def whole_kernel(
    frames, seqs, rows, cells,
    tokens, segments, small_in, g_attn, w_qkv, w_out_hbm, g_mlp, w_up_hbm, w_down_hbm, g_learn, tapmask, blockones,
    sums, own_tok, far_tok,
    xp, xg, qkv, augk, dag, da_ext, dx2_scr, learned,
    augq, o_scr, x2_scr, y_scr, vhat2_scr, vhat3_scr, rstd_scr,
    dh2_scr, u_scr, h3p, yp,
    dyp, w72_scr, spread_scr, rest_scr, gain_scr, conv_bw, conv_fw, dqkv,
    h1_scr, dh1_scr, buf, land, out, tok_send, tok_land, tsend,
    trecv, gsend, grecv, psend, precv, fsem, tsem, wsem, w_out, w_up, w_down,
):
    fi = lax.axis_index("frame")
    si = lax.axis_index("seq")
    half = frames // 2
    g = fi % half
    mine = fi // half
    total = frames * rows
    own = 2 * rows
    other = fi + half * (1 - 2 * mine)
    partner = (other, si)
    weights = [
        pltpu.make_async_copy(src, dst, wsem.at[i])
        for i, (src, dst) in enumerate(((w_out_hbm, w_out), (w_up_hbm, w_up), (w_down_hbm, w_down)))
    ]
    for cp in weights:
        cp.start()
    for k in range(2):
        body = tokens[k].astype(F32)[0:cells]
        seg = jnp.broadcast_to(segments[k : k + 1, 0:1].astype(F32), (1, 384))
        pad = jnp.zeros((rows - cells - 1 - MAPS, 384), F32)
        xp[k] = jnp.concatenate([body, seg, small_in[72 + MAPS * k : 72 + MAPS * (k + 1), :], pad], axis=0).astype(BF16)
    xg[fi] = xp[mine]
    singles = [[bit] for bit in mesh_bits(frames, seqs)]
    by_early, by_late = early_groups(frames, seqs), late_groups(frames, seqs)
    greet(partners_of((singles + [[("frame", 1)]],), fi, si))
    cut = (rows // 2 + 15) // 16 * 16
    near, far, to_partner = [], [], []
    end = 2
    for n, span in enumerate((pl.ds(0, cut), pl.ds(cut, rows - cut))):
        to_partner.append(rc(xp.at[1 - mine, span, :], xg.at[fi, span, :], tsend.at[n], trecv.at[fi + n * frames], partner))
        to_partner[n].start()
        block = lambda slot, span=span: xg.at[slot, span, :]
        for group, base in ((near, half * mine), (far, half * (1 - mine))):
            group.append(Gather(half, base, n, block, tsend, trecv, end, fi, si, n * frames))
            end = group[-1].end
    for piece in near:
        piece.run(0)
    da_block = lambda slot: dag.at[:, pl.ds(pl.multiple_of(slot * rows, rows), rows), :]
    da_near = Gather(half, 0, 0, da_block, gsend, grecv, 0, fi, si)
    da_far = Gather(half, half, 1, da_block, gsend, grecv, da_near.end, fi, si)
    refs = fi, si, buf, land, out, psend, precv
    early, late = [], []
    land_at = sem_at = 0
    for group, cuts, by, bits in ((early, EARLY_CUTS, by_early, EARLY_BITS), (late, LATE_CUTS, by_late, LATE_BITS)):
        for start, length, *_ in cuts:
            group.append(Piece(start, length, by, bits, land_at, sem_at, *refs))
            land_at, sem_at = group[-1].land_end, group[-1].sem_end

    h2_rows, a_rows, dm_rows = (pl.ds(own * k, own) for k in (4, 5, 6))

    def early_point(i):
        for piece, points in zip(early, EARLY_POINTS):
            if i in points:
                step = 1 + points.index(i)
                piece.finish(step)
                piece.start(step + 1)

    lane128 = iota((rows, 128), 1)
    row128 = iota((rows, 128), 0)
    valid_row = row128 < cells

    w72_scr[...] = sixteen(small_in[0:72, :]).astype(BF16)
    square_r, square_c = iota((128, 128), 0), iota((128, 128), 1)
    repeat = ((square_c & 7) == square_r).astype(F32)
    same_tap = (((square_r >> 3) == (square_c >> 3)) & (square_r < 72)).astype(F32)
    for layer in range(3):
        by_tap = small_in[88 + 72 * layer : 160 + 72 * layer, 0:128]
        conv_bw[layer] = sixteen(by_tap)
        by_tap = jnp.concatenate([by_tap, jnp.zeros((56, 128), F32)], axis=0)
        conv_fw[layer] = nn(repeat[0:16], nn(by_tap, repeat, HIGH) * same_tap, HIGH)

    def project(f, carry):
        x = xg[f].astype(F32)
        seg = x[cells : cells + 1, 0:128]
        x = jnp.where(iota(x.shape, 0) < cells, x, 0.0)
        vhat, _ = normed(x)
        h1 = (vhat * g_attn[...].reshape(1, -1)).astype(BF16)
        base = pl.multiple_of(f * rows, rows)
        whole = nn(h1, w_qkv[...])
        for b in range(9):
            part = whole[:, 128 * b : 128 * b + 128]
            if b < 3:
                part = part * HEAD_DIM**-0.5
            qkv[b, pl.ds(base, rows), :] = part.astype(BF16)
        same = (lane128.astype(F32) == seg) & valid_row
        augk[pl.ds(base, rows), :] = jnp.where(
            lane128 < 4, jnp.where(same, 0.0, -BIG), jnp.where(lane128 < AUG_END, -1.0, 0.0)
        ).astype(BF16)
        return carry

    def run(gather, stage):
        for piece in gather:
            piece.run(stage)

    def project_range(gather, start, core):
        n = 1 << gather[0].n

        def one(j, carry):
            return project(gather[0].nearby(j, core), carry)

        lax.fori_loop(start, n, one, 0, unroll=min(n - start, UNROLL))

    last = near[0].last
    project(fi, 0)
    run(near, 1)
    for n, piece in enumerate(far):
        here = piece.block(other)
        rc(here, here, tsend.at[0], trecv.at[other + n * frames], partner).wait_recv()
        piece.run(0)
    project(other, 0)
    for stage in range(2, last):
        run(near, stage)
    for stage in range(1, last):
        run(far, stage)
        if stage == 1:
            project_range(near, 1, False)
    run(near, last)
    project_range(far, 1, False)
    project_range(near, 0, True)
    run(far, last)
    project_range(far, 0, True)
    for cp in to_partner:
        cp.wait_send()
    for piece in near + far:
        piece.drain()

    ones = jnp.ones((frames * rows, 128), BF16)

    for k in range(2):
        f = g + half * k
        seg = xg[f].astype(F32)[cells : cells + 1, 0:128]
        same = (lane128.astype(F32) == seg) & valid_row & (lane128 < 4)
        augq[k * rows : (k + 1) * rows, :] = same.astype(F32)

    together = 2 if frames <= 16 else 1

    def attend(step, carry):
        p = step // (4 // together)
        k = step % 2
        f = g + half * k
        q = qkv[p, pl.ds(pl.multiple_of(f * rows, rows), rows), :]
        mine = pl.ds(pl.multiple_of(k * rows, rows), rows)
        aug = augq[mine, :]
        seg_aug = jnp.where(lane128 < 4, aug, 0.0).astype(BF16)
        keys = jnp.concatenate([qkv[3 + p], augk[...]], axis=1)
        values = jnp.concatenate([qkv[6 + p], ones], axis=1)
        mixed = o_scr[p, mine, :] if together == 1 else 0.0
        for n in range(together):
            e = n if together == 2 else (step // 2) % 2
            keep = (lane128 >= HEAD_DIM * e) & (lane128 < HEAD_DIM * (e + 1))
            s = nt(jnp.concatenate([q * keep.astype(F32).astype(BF16), seg_aug], axis=1), keys)
            top = jnp.max(s, axis=1, keepdims=True)
            prob = jnp.exp(s - top).astype(BF16)
            o = nn(prob, values)
            weight = o[:, 128:]
            mixed = jnp.where(keep, o[:, :128] / weight, mixed)
            lse = top + jnp.log(weight)
            which = lane128 - (LSE0 + 3 * (2 * p + e))
            aug = jnp.where((which >= 0) & (which < 3), pieces(lse, which), aug)
        augq[mine, :] = aug
        o_scr[p, mine, :] = mixed
        return carry

    lax.fori_loop(0, 4 * PAIRS // together, attend, 0)

    for cp in weights:
        cp.wait()

    def apart(fn):
        pl.when(fi >= 0)(fn)

    @apart
    def _():
        a = jnp.concatenate([o_scr[p].astype(BF16) for p in range(PAIRS)], axis=1)
        out[a_rows, :] = a
        both = jnp.concatenate([xg[g], xg[g + half]], axis=0).astype(F32)
        r = iota(both.shape, 0)
        x = jnp.where((r < cells) | ((r >= rows) & (r < rows + cells)), both, 0.0)
        x2 = x + nn(a, w_out[...])
        x2_scr[...] = x2
        y_scr[...] = x2
        vhat, rstd = normed(x2)
        rstd_scr[...] = jnp.broadcast_to(rstd, (own, 128))
        vhat2_scr[...] = vhat
        out[h2_rows, :] = (vhat * g_mlp[...].reshape(1, -1)).astype(BF16)

    def mlp(j, carry):
        cols = pl.ds(pl.multiple_of(384 * j, 384), 384)
        u = nn(out[h2_rows, :], w_up[:, cols])
        u_scr[j] = u
        hid = gelu(u).astype(BF16)
        out[pl.ds(pl.multiple_of(own * j, 16), own), :] = hid
        y_scr[...] += nn(hid, w_down[cols, :])
        return carry

    lax.fori_loop(0, 4, mlp, 0)

    @apart
    def _():
        y = y_scr[...]
        vhat, rstd = normed(y)
        vhat3_scr[...] = vhat
        rstd_scr[...] = jnp.where(iota((own, 128), 1) < 64, rstd_scr[...], rstd)
        h3 = (vhat * g_learn[...].reshape(1, -1)).astype(BF16)
        for k in range(2):
            yp[256 * k : 256 * k + rows, :] = y[k * rows : (k + 1) * rows, :]
            yp[256 * k + rows : 256 * k + 256, :] = jnp.zeros((256 - rows, 384), F32)
            h3p[256 * k : 256 * k + rows, :] = h3[k * rows : (k + 1) * rows, :]
            h3p[256 * k + rows : 256 * k + 256, :] = jnp.zeros((256 - rows, 384), BF16)

    def shift_of(t):
        return GRID * (t // 3 - 1) + (t % 3 - 1)

    def moved(v, s):
        return v if s == 0 else pltpu.roll(v, (-s) % WIDE, 1)

    def tap(t):
        return tapmask[t : t + 1, :]

    def im2col(v):
        parts = [moved(v, shift_of(t)) * tap(t) for t in range(9)]
        return jnp.concatenate(parts + [jnp.zeros((56, WIDE), F32)], axis=0)

    def spread_of(v):
        return jnp.concatenate([moved(v, -shift_of(t)) * tap(8 - t) for t in range(9)], axis=0)

    @apart
    def _():
        taps = nt(w72_scr[...], h3p[...])
        z1 = jnp.zeros((MAPS, WIDE), F32)
        for t in range(9):
            z1 = z1 + moved(taps[8 * t : 8 * t + 8, :], shift_of(t)) * tap(t)
        zs = [z1]
        cols_of = []
        for layer in range(3):
            col = im2col(gelu(zs[-1]))
            cols_of.append(col)
            zs.append(nn(conv_fw[layer], col, HIGH)[0:MAPS])
        maps = tap(4) / (1.0 + jnp.exp(-zs[3]))
        dmaps = []
        for k in range(2):
            f = g + half * k
            dl = xg[f].astype(F32)[cells + 1 : cells + 1 + MAPS, :] * (1.0 / cells)
            dl = sixteen(dl)
            mk = sixteen(maps[:, 256 * k : 256 * k + 256])
            yk = yp[256 * k : 256 * k + 256, :]
            learned[k] = nn(mk, yk, HIGH)[0:MAPS] * (1.0 / cells)
            dmaps.append(nt(dl, yk, HIGH)[0:MAPS])
            dyp[256 * k : 256 * k + 256, :] = tn(mk, dl, HIGH)
        dz = jnp.concatenate(dmaps, axis=1) * maps * (1.0 - maps)
        small = []
        for layer in (2, 1, 0):
            dw = nt(sixteen(dz), cols_of[layer], HIGH)[0:MAPS]
            small.insert(0, jnp.concatenate([dw, jnp.zeros((MAPS, 256), F32)], axis=1))
            dz = tn(conv_bw[layer], sixteen(spread_of(dz)), HIGH)[0:MAPS] * gelu_grad(zs[layer])
        dz = dz.astype(BF16).astype(F32) * tap(4)
        spread_scr[...] = sixteen(spread_of(dz)).astype(BF16)
        rest_scr[...] = jnp.concatenate(small + [jnp.zeros((8, 384), F32)], axis=0)

    @apart
    def _():
        dh3 = tn(spread_scr[...], w72_scr[...])
        dh3 = jnp.concatenate([dh3[0:rows], dh3[256 : 256 + rows]], axis=0)
        dy, dg3 = norm_back(vhat3_scr[...], rstd_scr[:, 64:65], dh3, g_learn[...].reshape(1, -1))
        dy = dy + jnp.concatenate([dyp[0:rows, :], dyp[256 : 256 + rows, :]], axis=0)
        y_scr[...] = dy
        out[dm_rows, :] = dy.astype(BF16)
        dh2_scr[...] = jnp.zeros((own, 384), F32)
        gain_scr[...] = jnp.concatenate([dg3, jnp.zeros((7, 384), F32)], axis=0)

    def mlp_back(j, carry):
        cols = pl.ds(pl.multiple_of(384 * j, 384), 384)
        dm = out[dm_rows, :]
        du = (nt(dm, w_down[cols, :]) * gelu_grad(u_scr[j])).astype(BF16)
        buf[cols, :] = tn(out[h2_rows, :], du).astype(BF16)
        buf[pl.ds(pl.multiple_of(1536 + 384 * j, 384), 384), :] = tn(out[pl.ds(pl.multiple_of(own * j, 16), own), :], dm).astype(BF16)
        dh2_scr[...] += nt(du, w_up[:, cols])
        return carry

    lax.fori_loop(0, 4, mlp_back, 0)
    early[0].start(0)

    @apart
    def _():
        dx2, dg2 = norm_back(vhat2_scr[...], rstd_scr[:, 0:1], dh2_scr[...], g_mlp[...].reshape(1, -1))
        dx2 = dx2 + y_scr[...]
        dx2_scr[...] = dx2
        out[dm_rows, :] = dx2.astype(BF16)
        gains = jnp.concatenate([dg2, gain_scr[0:1, :], jnp.zeros((6, 384), F32)], axis=0)
        d_first = nn(spread_scr[...], h3p[...])[0:72]
        small = [d_first, gains, rest_scr[...], jnp.zeros((16, 384), F32)]
        buf[3456:3584, :] = jnp.concatenate(small, axis=0).astype(BF16)

    @apart
    def _():
        dzz = out[dm_rows, :]
        buf[3072:3456, :] = tn(out[a_rows, :], dzz).astype(BF16)
        da = nt(dzz, w_out[...]).astype(BF16)
        prod = jnp.concatenate([o_scr[p] for p in range(PAIRS)], axis=1) * da.astype(F32)
        lane = iota((own, 128), 1)
        which = lane - DEL0
        which = which - 3 * (which // 3)
        delta = pieces(nn(prod, blockones[...], HIGH), which)
        full = jnp.where((lane >= DEL0) & (lane < AUG_END), delta, augq[...])
        full = full.astype(BF16)
        for p in range(PAIRS):
            da_ext[p] = da[:, 128 * p : 128 * p + 128]
        da_ext[PAIRS] = full
        for k in range(2):
            there = pl.ds(pl.multiple_of((g + half * k) * rows, rows), rows)
            dag[:, there, :] = da_ext[:, k * rows : (k + 1) * rows, :]

    early[0].finish(0)
    early[0].start(1)
    early[1].start(0)
    da_near.run(0)
    da_far.run(0)
    x = jnp.concatenate([xg[g], xg[g + half]], axis=0).astype(F32)
    r = iota(x.shape, 0)
    x = jnp.where((r < cells) | ((r >= rows) & (r < rows + cells)), x, 0.0)
    vhat, _ = normed(x)
    h1_scr[...] = (vhat * g_attn[...].reshape(1, -1)).astype(BF16)
    dh1_scr[...] = jnp.zeros((own, 384), F32)
    buf[EARLY + 1152 :, :] = jnp.zeros((128, 384), BF16)
    early[1].finish(0)
    early[1].start(1)

    def own_rows(b):
        at = [qkv[b, pl.ds(pl.multiple_of((g + half * k) * rows, rows), rows), :] for k in range(2)]
        return jnp.concatenate(at, axis=0)

    own_augk = jnp.concatenate(
        [augk[pl.ds(pl.multiple_of((g + half * k) * rows, rows), rows), :] for k in range(2)], axis=0
    )
    chunk = 256
    pieces_n = total // chunk
    split = (pieces_n + 1) // 2

    def query_pass(p, carry):
        def at_point(j):
            for k in range(PAIRS):
                i = 2 * k + j

                def point(i=i):
                    early_point(i)
                    stage = i // 2 + 1
                    if i % 2 == 1 and stage < da_near.last:
                        da_near.run(stage)
                        da_far.run(stage)

                pl.when(p == k)(point)

        dq = grad_pass(
            own_rows(p), da_ext[p], da_ext[PAIRS],
            lambda i: qkv[3 + p, i, :], lambda i: qkv[6 + p, i, :], lambda i: augk[i, :],
            p, pieces_n, split, chunk, False, at_point,
        )
        dqkv[p] = (dq * HEAD_DIM**-0.5).astype(BF16)
        return carry

    lax.fori_loop(0, PAIRS, query_pass, 0)
    for gather in (da_near, da_far):
        gather.run(gather.last)
        gather.drain()

    def key_pass(p, carry):
        def at_point(j):
            for k in range(PAIRS):
                i = 2 * PAIRS + 2 * k + j

                def point(i=i, k=k):
                    early_point(i)
                    for piece, (_, _, after) in zip(late, LATE_CUTS):
                        if after < k:
                            step = 2 * (k - after - 1) + j
                            piece.finish(step)
                            piece.start(step + 1)

                pl.when(p == k)(point)

        dk, dv = grad_pass(
            own_rows(3 + p), own_rows(6 + p), own_augk,
            lambda i: qkv[p, i, :], lambda i: dag[p, i, :], lambda i: dag[PAIRS, i, :],
            p, pieces_n, split, chunk, True, at_point,
        )
        d = jnp.concatenate([dqkv[p], dk.astype(BF16), dv.astype(BF16)], axis=1)
        buf[pl.ds(pl.multiple_of(EARLY + 384 * p, 128), 384), :] = tn(h1_scr[...], d).astype(BF16)
        w = jnp.concatenate(
            [w_qkv[:, pl.ds(pl.multiple_of(384 * b + 128 * p, 128), 128)] for b in range(3)], axis=1
        )
        dh1_scr[...] += nt(d, w)
        for piece, (_, _, after) in zip(late, LATE_CUTS):
            if after < PAIRS - 1:
                pl.when(p == after)(functools.partial(piece.start, 0))
        return carry

    lax.fori_loop(0, PAIRS, key_pass, 0)
    dx, dg = norm_back(*normed(x), dh1_scr[...], g_attn[...].reshape(1, -1))
    buf[EARLY + 1152 : EARLY + 1168, :] = jnp.concatenate([dg, jnp.zeros((15, 384), F32)], axis=0).astype(BF16)
    for piece, (_, _, after) in zip(late, LATE_CUTS):
        if after == PAIRS - 1:
            piece.start(0)
    dx = dx + dx2_scr[...]
    for k in range(2):
        tail = jnp.concatenate([learned[k], jnp.zeros((rows - cells - MAPS, 384), F32)], axis=0)
        whole = jnp.concatenate([dx[k * rows : k * rows + cells, :], tail], axis=0)

        @pl.when(mine == k)
        def _():
            own_tok[...] = whole

        @pl.when(mine != k)
        def _():
            tok_send[...] = whole.astype(BF16)

    tok_copy = rc(tok_send, tok_land, tsem.at[0], tsem.at[1], (fi + half * (1 - 2 * mine), si))
    tok_copy.start()
    give = [
        pltpu.make_async_copy(out.at[pl.ds(at, n), :], sums.at[pl.ds(at, n), :], fsem.at[i])
        for i, (at, n) in enumerate((EARLY_CUTS[0], (EARLY_CUTS[1][0], EARLY + LATE - EARLY_CUTS[1][0])))
    ]
    running = [(piece, 1 + len(points)) for piece, points in zip(early, EARLY_POINTS)]
    running += [(piece, 2 * (PAIRS - 1 - after)) for piece, (_, _, after) in zip(late, LATE_CUTS)]
    for piece, n in running[:1]:
        for i in range(n, piece.total):
            piece.finish(i)
            piece.start(i + 1)
    give[0].start()
    for i in range(max(piece.total - n for piece, n in running[1:])):
        for piece, n in running[1:]:
            piece.finish(n + i)
            piece.start(n + i + 1)
    give[1].start()
    tok_copy.wait()
    far_tok[...] = tok_land[...]
    for cp in give:
        cp.wait()


def finish_kernel(cells, half, sums, own_tok, far_tok, d_tokens, learned, g_attn, w_qkv, w_out, g_mlp, w_up, w_down, g_learn, first, rest):
    for j in range(4):
        w_up[:, 384 * j : 384 * j + 384] = sums[384 * j : 384 * j + 384, :].astype(F32)
    w_down[...] = sums[1536:3072, :].astype(F32)
    w_out[...] = sums[3072:3456, :].astype(F32)
    small = sums[3456:3584, :].astype(F32)
    first[...] = small[0:72].reshape(9, MAPS, 384)
    for n in range(27):
        layer, t = n // 9, n % 9
        rest[n] = small[80 + MAPS * layer : 88 + MAPS * layer, MAPS * t : MAPS * (t + 1)]
    g_mlp[...] = small[72:73].reshape(-1)
    g_learn[...] = small[73:74].reshape(-1)
    for p in range(PAIRS):
        block = sums[EARLY + 384 * p : EARLY + 384 * p + 384, :].astype(F32)
        for b in range(3):
            w_qkv[:, 384 * b + 128 * p : 384 * b + 128 * p + 128] = block[:, 128 * b : 128 * b + 128]
    g_attn[...] = sums[EARLY + 1152 : EARLY + 1168, :].astype(F32)[0:1].reshape(-1)
    mine = lax.axis_index("frame") // half
    far = far_tok[...].astype(F32)
    near = own_tok[...]
    d_tokens[mine] = near[0:cells]
    d_tokens[1 - mine] = far[0:cells]
    a, b = near[cells : cells + MAPS], far[cells : cells + MAPS]
    learned[...] = jnp.where(mine == 0, jnp.concatenate([a, b], axis=0), jnp.concatenate([b, a], axis=0)).astype(BF16)


def vspec(n):
    return [pl.BlockSpec(memory_space=VMEM)] * n


def params(collective=None, mib=56):
    if collective is None:
        return pltpu.CompilerParams(vmem_limit_bytes=mib * MIB)
    return pltpu.CompilerParams(collective_id=collective, has_side_effects=True, vmem_limit_bytes=mib * MIB)


def tap_masks():
    p = np.arange(WIDE) % 256
    px, py = p // GRID, p % GRID
    out = np.zeros((16, WIDE), np.float32)
    for t in range(9):
        r, c = t // 3 - 1, t % 3 - 1
        out[t] = (p < CELLS) & (px + r >= 0) & (px + r < GRID) & (py + c >= 0) & (py + c < GRID)
    return out


def head_sums():
    out = np.zeros((HEADS * HEAD_DIM, 128), np.float32)
    for h in range(HEADS):
        out[h * HEAD_DIM : (h + 1) * HEAD_DIM, DEL0 + 3 * h : DEL0 + 3 * h + 3] = 1.0
    return out


def on_device(frames, seqs, tokens, segments, g_attn, w_qkv, w_out, g_mlp, w_up, w_down, g_learn, conv_first, conv_rest, d_learned):
    _, cells, width = tokens.shape
    rows = -(-(cells + 1 + MAPS) // 16) * 16
    own = 2 * rows
    total = frames * rows
    n_sems = 2 + 16 * frames
    sds = jax.ShapeDtypeStruct
    rest = conv_rest.transpose(0, 2, 3, 1, 4).reshape(27 * MAPS, MAPS)
    small_in = jnp.concatenate(
        [
            conv_first.transpose(1, 2, 0, 3).reshape(9 * MAPS, width),
            d_learned.reshape(2 * MAPS, width),
            jnp.pad(rest, ((0, 0), (0, width - MAPS))),
        ],
        axis=0,
    ).astype(F32)
    n_all = EARLY + LATE
    sizes = [landing(n, early_groups(frames, seqs), EARLY_BITS) for _, n in EARLY_CUTS]
    sizes += [landing(n, late_groups(frames, seqs), LATE_BITS) for _, n, _ in LATE_CUTS]
    land_n, copies = (sum(v) for v in zip(*sizes))
    anywhere = pl.BlockSpec(memory_space=pl.ANY)
    sums, own_tok, far_tok = pl.pallas_call(
        functools.partial(whole_kernel, frames, seqs, rows, cells),
        out_shape=[sds((n_all, width), BF16), sds((rows, width), F32), sds((rows, width), BF16)],
        in_specs=vspec(5) + [anywhere] + vspec(1) + [anywhere] * 2 + vspec(3),
        out_specs=[anywhere] + vspec(2),
        scratch_shapes=[
            VMEM((2, rows, width), BF16),
            VMEM((frames, rows, width), BF16),
            VMEM((9, total, 128), BF16),
            VMEM((total, 128), BF16),
            VMEM((PAIRS + 1, total, 128), BF16),
            VMEM((PAIRS + 1, own, 128), BF16),
            VMEM((own, width), F32),
            VMEM((2, MAPS, width), F32),
            VMEM((own, 128), F32),
            VMEM((PAIRS, own, 128), F32),
            VMEM((own, width), F32),
            VMEM((own, width), F32),
            VMEM((own, width), F32),
            VMEM((own, width), F32),
            VMEM((own, 128), F32),
            VMEM((own, width), F32),
            VMEM((4, own, width), F32),
            VMEM((WIDE, width), BF16),
            VMEM((WIDE, width), F32),
            VMEM((WIDE, width), F32),
            VMEM((80, width), BF16),
            VMEM((80, WIDE), BF16),
            VMEM((32, width), F32),
            VMEM((8, width), F32),
            VMEM((3, 80, 128), F32),
            VMEM((3, 16, 128), F32),
            VMEM((PAIRS, own, 128), BF16),
            VMEM((own, width), BF16),
            VMEM((own, width), F32),
            VMEM((n_all, width), BF16),
            VMEM((land_n, width), BF16),
            VMEM((n_all, width), BF16),
            VMEM((rows, width), BF16),
            VMEM((rows, width), BF16),
            pltpu.SemaphoreType.DMA((n_sems,)),
            pltpu.SemaphoreType.DMA((2 * frames,)),
            pltpu.SemaphoreType.DMA((n_sems,)),
            pltpu.SemaphoreType.DMA((frames,)),
            pltpu.SemaphoreType.DMA((copies,)),
            pltpu.SemaphoreType.DMA((copies,)),
            pltpu.SemaphoreType.DMA((2,)),
            pltpu.SemaphoreType.DMA((2,)),
            pltpu.SemaphoreType.DMA((3,)),
            VMEM((width, width), BF16),
            VMEM((width, 4 * width), BF16),
            VMEM((4 * width, width), BF16),
        ],
        compiler_params=params(0, 61),
        name="layer",
    )(
        jnp.pad(tokens, ((0, 0), (0, rows - cells), (0, 0))), segments, small_in,
        g_attn, w_qkv, w_out, g_mlp, w_up, w_down, g_learn,
        jnp.asarray(tap_masks()), jnp.asarray(head_sums()),
    )
    d_tokens, learned_all, dg_attn, d_w_qkv, d_w_out, dg_mlp, d_w_up, d_w_down, dg_learn, first, rest = pl.pallas_call(
        functools.partial(finish_kernel, cells, frames // 2),
        out_shape=[
            sds((2, cells, width), F32),
            sds((2 * MAPS, width), BF16),
            sds((width,), F32),
            sds((width, 3 * width), F32),
            sds((width, width), F32),
            sds((width,), F32),
            sds((width, 4 * width), F32),
            sds((4 * width, width), F32),
            sds((width,), F32),
            sds((9, MAPS, width), F32),
            sds((27, MAPS, MAPS), F32),
        ],
        in_specs=vspec(3),
        out_specs=vspec(11),
        compiler_params=params(),
        name="outputs",
    )(sums, own_tok, far_tok)
    d_first = first.reshape(3, 3, MAPS, width).transpose(2, 0, 1, 3)
    d_rest = rest.reshape(3, 3, 3, MAPS, MAPS).transpose(0, 3, 1, 2, 4)
    return (
        learned_all.reshape(2, MAPS, width), d_tokens, dg_attn, d_w_qkv, d_w_out, dg_mlp, d_w_up, d_w_down, dg_learn, d_first, d_rest,
    )


def solution(mesh):
    frames, seqs = mesh.shape["frame"], mesh.shape["seq"]
    both = P("seq", "frame", None)
    in_specs = (both, P("seq", "frame"), *([P()] * 9), both)
    out_specs = (both, both, *([P()] * 9))
    return jax.shard_map(
        functools.partial(on_device, frames, seqs),
        mesh=mesh,
        in_specs=in_specs,
        out_specs=out_specs,
        check_vma=False,
    )
```

```python
import functools

import jax
import jax.numpy as jnp
import numpy as np
from jax import lax
from jax.experimental import pallas as pl
from jax.experimental.pallas import tpu as pltpu
from jax.sharding import PartitionSpec as P

HEADS = 6
HEAD_DIM = 64
MAPS = 8
GRID = 14
CELLS = GRID * GRID
PAIRS = HEADS // 2
WIDE = 512
BIG = 1e30
LSE0 = 4
DEL0 = 4 + 3 * HEADS
AUG_END = 4 + 6 * HEADS
F32 = jnp.float32
BF16 = jnp.bfloat16
HIGH = lax.Precision.HIGHEST
MESH = pl.DeviceIdType.MESH
VMEM = pltpu.VMEM
MIB = 1 << 20


def nn(a, b, precision=None):
    return lax.dot_general(a, b, (((1,), (0,)), ((), ())), precision=precision, preferred_element_type=F32)


def nt(a, b, precision=None):
    return lax.dot_general(a, b, (((1,), (1,)), ((), ())), precision=precision, preferred_element_type=F32)


def tn(a, b, precision=None):
    return lax.dot_general(a, b, (((0,), (0,)), ((), ())), precision=precision, preferred_element_type=F32)


def iota(shape, dim):
    return lax.broadcasted_iota(jnp.int32, shape, dim)


def sixteen(v):
    return jnp.concatenate([v, jnp.zeros((8, v.shape[1]), v.dtype)], axis=0)


def normed(x):
    centered = x - jnp.mean(x, axis=-1, keepdims=True)
    rstd = lax.rsqrt(jnp.mean(centered * centered, axis=-1, keepdims=True) + 1e-06)
    return centered * rstd, rstd


def norm_back(vhat, rstd, dout, gain):
    e = dout * gain
    mean_e = jnp.mean(e, axis=-1, keepdims=True)
    mean_ev = jnp.mean(e * vhat, axis=-1, keepdims=True)
    return rstd * (e - mean_e - vhat * mean_ev), jnp.sum(dout * vhat, axis=0, keepdims=True)


C0 = 0.7978845608028654
C1 = 0.044715


def gelu(u):
    return 0.5 * u * (1.0 + jnp.tanh(C0 * (u + C1 * u * u * u)))


def gelu_grad(u):
    t = jnp.tanh(C0 * (u + C1 * u * u * u))
    return 0.5 * (1.0 + t) + 0.5 * u * (1.0 - t * t) * (C0 + (3.0 * C0 * C1) * u * u)


def flip(v, b):
    return v + b * (1 - 2 * ((v // b) % 2))


def bit_of(v, b):
    return (v // b) % 2


def rc(src, dst, send, recv, dev):
    return pltpu.make_async_remote_copy(
        src_ref=src, dst_ref=dst, send_sem=send, recv_sem=recv, device_id=dev, device_id_type=MESH
    )


def greet(partners):
    barrier = pltpu.get_barrier_semaphore()
    for dev in partners:
        pl.semaphore_signal(barrier, inc=1, device_id=dev, device_id_type=MESH)
    pl.semaphore_wait(barrier, len(partners))


class Gather:
    def __init__(self, half, base, turn, block, send, recv, first, fi, si, shift=0):
        self.shift = shift
        self.g, self.base, self.block, self.send, self.recv = fi % half, base, block, send, recv
        self.fi, self.si = fi, si
        bits = []
        b = 2
        while b < half:
            bits.append(b)
            b *= 2
        n = len(bits)
        self.n = n
        self.order = bits[turn % n :] + bits[: turn % n] if n else []
        self.pushes = [[] for _ in range(n + 2)]
        count = first
        for stage in range(n + 1):
            for j in range(1 << max(stage - 1, 0)):
                for bit in self.order[stage:] + [1]:
                    self.pushes[stage].append((stage, j, count, bit))
                    count += 1
        self.end = count
        self.last = n + 1

    def delta(self, bit):
        return bit * (1 - 2 * bit_of(self.g, bit))

    def arrivals(self, stage):
        return 1 << (self.n if stage == self.last else stage - 1)

    def slot(self, stage, j):
        at = self.base + self.g
        if stage == 0:
            return at
        passed = self.order if stage == self.last else self.order[: stage - 1]
        for k, bit in enumerate(passed):
            at = at + ((j // (1 << k)) % 2) * self.delta(bit)
        return at + self.delta(1 if stage == self.last else self.order[stage - 1])

    def nearby(self, j, core):
        at = self.base + self.g
        for k, bit in enumerate(self.order):
            at = at + ((j // (1 << k)) % 2) * self.delta(bit)
        return at + self.delta(1) if core else at

    def copy(self, slot, k, bit):
        ref = self.block(slot)
        return rc(ref, ref, self.send.at[k], self.recv.at[slot + self.shift], (flip(self.fi, bit), self.si))

    def run(self, stage):
        if stage > 0:
            for j in range(self.arrivals(stage)):
                slot = self.slot(stage, j)
                self.copy(slot, 0, 1).wait_recv()
                for st, i, k, bit in self.pushes[stage]:
                    if i == j:
                        self.copy(slot, k, bit).start()
        else:
            for st, i, k, bit in self.pushes[0]:
                self.copy(self.slot(0, 0), k, bit).start()

    def drain(self):
        for stage in self.pushes:
            for st, i, k, bit in stage:
                self.copy(self.slot(st, i), k, bit).wait_send()


def aug_masks(h):
    lane = iota((1, 128), 1)
    seg = lane < 4
    lse = seg | ((lane >= LSE0 + 3 * h) & (lane < LSE0 + 3 * h + 3))
    dlt = (lane >= DEL0 + 3 * h) & (lane < DEL0 + 3 * h + 3)
    return lse.astype(F32).astype(BF16), dlt.astype(F32).astype(BF16)


def pieces(value, which):
    hi = value.astype(BF16).astype(F32)
    rest = value - hi
    mid = rest.astype(BF16).astype(F32)
    low = rest - mid
    return jnp.where(which == 0, hi, jnp.where(which == 1, mid, low))


def half_masks():
    lane = iota((1, 128), 1)
    first = (lane < HEAD_DIM).astype(F32).astype(BF16)
    return first, (lane >= HEAD_DIM).astype(F32).astype(BF16)


def grad_pass(own_a, own_b, own_aug, all_a, all_b, all_aug, p, count, split, chunk, with_b, at_point):
    masks = half_masks()
    left_a, left_b = [], []
    for e in range(2):
        lse_mask, del_mask = aug_masks(2 * p + e)
        left_a.append(jnp.concatenate([own_a * masks[e], own_aug * lse_mask], axis=1))
        left_b.append(jnp.concatenate([own_b * masks[e], own_aug * del_mask], axis=1))
    acc = [jnp.zeros((own_a.shape[0], 128), F32) for _ in range(2 if with_b else 1)]
    for c in range(count):
        here = pl.ds(c * chunk, chunk)
        ra, rb, aug = all_a(here), all_b(here), all_aug(here)
        right_a = jnp.concatenate([ra, aug], axis=1)
        right_b = jnp.concatenate([rb, aug], axis=1)
        probs = [jnp.exp(nt(left_a[e], right_a)) for e in range(2)]
        ds = [(probs[e] * nt(left_b[e], right_b)).astype(BF16) for e in range(2)]
        acc[0] = acc[0] + nn(jnp.concatenate(ds, axis=1), jnp.concatenate([ra * m for m in masks], axis=0))
        if with_b:
            both = jnp.concatenate([prob.astype(BF16) for prob in probs], axis=1)
            acc[1] = acc[1] + nn(both, jnp.concatenate([rb * m for m in masks], axis=0))
        if c + 1 == split:
            at_point(0)
    at_point(1)
    return acc if with_b else acc[0]


def mesh_bits(frames, seqs):
    rest = []
    b = 1
    while b < seqs:
        rest.append(("seq", b))
        b *= 2
    b = 2
    while b < frames:
        rest.append(("frame", b))
        b *= 2
    return rest


TILE = 16
UNROLL = 4


def at_tile(start, n):
    return pl.ds(start if isinstance(start, int) else pl.multiple_of(start, TILE), n)


def member(group, offset, fi, si):
    index = 0
    for i, (axis, bit) in enumerate(group):
        value = bit_of(fi if axis == "frame" else si, bit)
        if (offset >> i) & 1:
            value = 1 - value
            if axis == "frame":
                fi = flip(fi, bit)
            else:
                si = flip(si, bit)
        index = index + value * (1 << i)
    return (fi, si), index


def pairs_of(bits):
    return [bits[i : i + 2] for i in range(0, len(bits), 2)]


EARLY = 3584
LATE = 3 * 384 + 128
EARLY_CUTS = ((0, 1536), (1536, 2048))
LATE_CUTS = ((EARLY, 1152, 2), (EARLY + 1152, 128, 2))
EARLY_BITS = 5
LATE_BITS = 3


def early_groups(frames, seqs):
    rest = mesh_bits(frames, seqs)
    return [[("frame", 1)], rest[:1]] + pairs_of(rest[1:])


def late_groups(frames, seqs):
    return [[("frame", 1)]] + pairs_of(mesh_bits(frames, seqs))


def landing(length, groups, most_bits):
    rows = copies = bits = 0
    for group in groups:
        others = (1 << len(group)) - 1
        bits += len(group)
        copies += others
        if bits <= most_bits:
            length >>= len(group)
            copies += others
        rows += others * length
    return rows, copies


class Piece:
    def __init__(self, start, length, groups, most_bits, land_at, sem_at, fi, si, buf, land, out, send, recv):
        self.refs = buf, land, out, send, recv
        self.steps = []
        seg, n, sem, bits = start, length, sem_at, 0
        hist = []
        for group in groups:
            bits += len(group)
            offsets = range(1, 1 << len(group))
            moves = []
            if bits <= most_bits:
                hist.append((seg, n, group))
                n >>= len(group)
                _, index = member(group, 0, fi, si)
                for d in offsets:
                    dev, other = member(group, d, fi, si)
                    moves.append((seg + other * n, land_at, sem, dev))
                    land_at, sem = land_at + n, sem + 1
                seg = seg + index * n
            else:
                for d in offsets:
                    dev, _ = member(group, d, fi, si)
                    moves.append((seg, land_at, sem, dev))
                    land_at, sem = land_at + n, sem + 1
            self.steps.append(("add", seg, n, moves))
        self.adds = len(groups)
        for old, old_n, group in reversed(hist):
            moves = []
            for d in range(1, 1 << len(group)):
                moves.append((seg, 0, sem, member(group, d, fi, si)[0]))
                sem += 1
            self.steps.append(("copy", seg, n, moves))
            seg, n = old, old_n
        self.sem_end = sem
        self.land_end = land_at
        self.total = len(self.steps)

    def copies(self, i):
        buf, land, out, send, recv = self.refs
        kind, _, n, moves = self.steps[i]
        made = []
        for give, at, sem, dev in moves:
            src = (buf if kind == "add" else out).at[at_tile(give, n), :]
            dst = land.at[at_tile(at, n), :] if kind == "add" else src
            made.append(rc(src, dst, send.at[sem], recv.at[sem], dev))
        return made

    def start(self, i):
        if i < self.total:
            for cp in self.copies(i):
                cp.start()

    def finish(self, i):
        if i < 0 or i >= self.total:
            return
        buf, land, out, _, _ = self.refs
        for cp in self.copies(i):
            cp.wait()
        kind, keep, n, moves = self.steps[i]
        if kind == "copy":
            return
        to = out if i == self.adds - 1 else buf
        chunk = max(TILE * k for k in (1, 2, 3, 4, 6, 7) if n % (TILE * k) == 0)

        def add(j, carry):
            here = at_tile(keep + j * chunk, chunk)
            value = buf[here, :].astype(F32)
            for _, at, _, _ in moves:
                value = value + land[at_tile(at + j * chunk, chunk), :].astype(F32)
            to[here, :] = value.astype(BF16)
            return carry

        lax.fori_loop(0, n // chunk, add, 0)


def partners_of(all_groups, fi, si):
    seen, devs = set(), []
    for groups in all_groups:
        for group in groups:
            for d in range(1, 1 << len(group)):
                key = tuple(sorted(group[i] for i in range(len(group)) if (d >> i) & 1))
                if key not in seen:
                    seen.add(key)
                    devs.append(member(group, d, fi, si)[0])
    return devs


EARLY_POINTS = ((3, 6, 7, 8, 9, 11), (5, 7, 8, 9, 10))


def whole_kernel(
    frames, seqs, rows, cells,
    tokens, segments, small_in, g_attn, w_qkv, w_out_hbm, g_mlp, w_up_hbm, w_down_hbm, g_learn, tapmask, blockones,
    sums, own_tok, far_tok,
    xp, xg, qkv, augk, dag, da_ext, dx2_scr, learned,
    augq, o_scr, x2_scr, y_scr, vhat2_scr, vhat3_scr, rstd_scr,
    dh2_scr, u_scr, h3p, yp,
    dyp, w72_scr, spread_scr, rest_scr, gain_scr, conv_bw, conv_fw, dqkv,
    h1_scr, dh1_scr, buf, land, out, tok_send, tok_land, tsend,
    trecv, gsend, grecv, psend, precv, fsem, tsem, wsem, w_out, w_up, w_down,
):
    fi = lax.axis_index("frame")
    si = lax.axis_index("seq")
    half = frames // 2
    g = fi % half
    mine = fi // half
    total = frames * rows
    own = 2 * rows
    other = fi + half * (1 - 2 * mine)
    partner = (other, si)
    weights = [
        pltpu.make_async_copy(src, dst, wsem.at[i])
        for i, (src, dst) in enumerate(((w_out_hbm, w_out), (w_up_hbm, w_up), (w_down_hbm, w_down)))
    ]
    for cp in weights:
        cp.start()
    for k in range(2):
        body = tokens[k].astype(F32)[0:cells]
        seg = jnp.broadcast_to(segments[k : k + 1, 0:1].astype(F32), (1, 384))
        pad = jnp.zeros((rows - cells - 1 - MAPS, 384), F32)
        xp[k] = jnp.concatenate([body, seg, small_in[72 + MAPS * k : 72 + MAPS * (k + 1), :], pad], axis=0).astype(BF16)
    xg[fi] = xp[mine]
    singles = [[bit] for bit in mesh_bits(frames, seqs)]
    by_early, by_late = early_groups(frames, seqs), late_groups(frames, seqs)
    greet(partners_of((singles + [[("frame", 1)]],), fi, si))
    cut = (rows // 2 + 15) // 16 * 16
    near, far, to_partner = [], [], []
    end = 2
    for n, span in enumerate((pl.ds(0, cut), pl.ds(cut, rows - cut))):
        to_partner.append(rc(xp.at[1 - mine, span, :], xg.at[fi, span, :], tsend.at[n], trecv.at[fi + n * frames], partner))
        to_partner[n].start()
        block = lambda slot, span=span: xg.at[slot, span, :]
        for group, base in ((near, half * mine), (far, half * (1 - mine))):
            group.append(Gather(half, base, n, block, tsend, trecv, end, fi, si, n * frames))
            end = group[-1].end
    for piece in near:
        piece.run(0)
    da_block = lambda slot: dag.at[:, pl.ds(pl.multiple_of(slot * rows, rows), rows), :]
    da_near = Gather(half, 0, 0, da_block, gsend, grecv, 0, fi, si)
    da_far = Gather(half, half, 1, da_block, gsend, grecv, da_near.end, fi, si)
    refs = fi, si, buf, land, out, psend, precv
    early, late = [], []
    land_at = sem_at = 0
    for group, cuts, by, bits in ((early, EARLY_CUTS, by_early, EARLY_BITS), (late, LATE_CUTS, by_late, LATE_BITS)):
        for start, length, *_ in cuts:
            group.append(Piece(start, length, by, bits, land_at, sem_at, *refs))
            land_at, sem_at = group[-1].land_end, group[-1].sem_end

    h2_rows, a_rows, dm_rows = (pl.ds(own * k, own) for k in (4, 5, 6))

    def early_point(i):
        for piece, points in zip(early, EARLY_POINTS):
            if i in points:
                step = 1 + points.index(i)
                piece.finish(step)
                piece.start(step + 1)

    lane128 = iota((rows, 128), 1)
    row128 = iota((rows, 128), 0)
    valid_row = row128 < cells

    w72_scr[...] = sixteen(small_in[0:72, :]).astype(BF16)
    square_r, square_c = iota((128, 128), 0), iota((128, 128), 1)
    repeat = ((square_c & 7) == square_r).astype(F32)
    same_tap = (((square_r >> 3) == (square_c >> 3)) & (square_r < 72)).astype(F32)
    for layer in range(3):
        by_tap = small_in[88 + 72 * layer : 160 + 72 * layer, 0:128]
        conv_bw[layer] = sixteen(by_tap)
        by_tap = jnp.concatenate([by_tap, jnp.zeros((56, 128), F32)], axis=0)
        conv_fw[layer] = nn(repeat[0:16], nn(by_tap, repeat, HIGH) * same_tap, HIGH)

    def project(f, carry):
        x = xg[f].astype(F32)
        seg = x[cells : cells + 1, 0:128]
        x = jnp.where(iota(x.shape, 0) < cells, x, 0.0)
        vhat, _ = normed(x)
        h1 = (vhat * g_attn[...].reshape(1, -1)).astype(BF16)
        base = pl.multiple_of(f * rows, rows)
        whole = nn(h1, w_qkv[...])
        for b in range(9):
            part = whole[:, 128 * b : 128 * b + 128]
            if b < 3:
                part = part * HEAD_DIM**-0.5
            qkv[b, pl.ds(base, rows), :] = part.astype(BF16)
        same = (lane128.astype(F32) == seg) & valid_row
        augk[pl.ds(base, rows), :] = jnp.where(
            lane128 < 4, jnp.where(same, 0.0, -BIG), jnp.where(lane128 < AUG_END, -1.0, 0.0)
        ).astype(BF16)
        return carry

    def run(gather, stage):
        for piece in gather:
            piece.run(stage)

    def project_range(gather, start, core):
        n = 1 << gather[0].n

        def one(j, carry):
            return project(gather[0].nearby(j, core), carry)

        lax.fori_loop(start, n, one, 0, unroll=min(n - start, UNROLL))

    last = near[0].last
    project(fi, 0)
    run(near, 1)
    for n, piece in enumerate(far):
        here = piece.block(other)
        rc(here, here, tsend.at[0], trecv.at[other + n * frames], partner).wait_recv()
        piece.run(0)
    project(other, 0)
    for stage in range(2, last):
        run(near, stage)
    for stage in range(1, last):
        run(far, stage)
        if stage == 1:
            project_range(near, 1, False)
    run(near, last)
    project_range(far, 1, False)
    project_range(near, 0, True)
    run(far, last)
    project_range(far, 0, True)
    for cp in to_partner:
        cp.wait_send()
    for piece in near + far:
        piece.drain()

    ones = jnp.ones((frames * rows, 128), BF16)

    for k in range(2):
        f = g + half * k
        seg = xg[f].astype(F32)[cells : cells + 1, 0:128]
        same = (lane128.astype(F32) == seg) & valid_row & (lane128 < 4)
        augq[k * rows : (k + 1) * rows, :] = same.astype(F32)

    together = 2 if frames <= 16 else 1

    def attend(step, carry):
        p = step // (4 // together)
        k = step % 2
        f = g + half * k
        q = qkv[p, pl.ds(pl.multiple_of(f * rows, rows), rows), :]
        mine = pl.ds(pl.multiple_of(k * rows, rows), rows)
        aug = augq[mine, :]
        seg_aug = jnp.where(lane128 < 4, aug, 0.0).astype(BF16)
        keys = jnp.concatenate([qkv[3 + p], augk[...]], axis=1)
        values = jnp.concatenate([qkv[6 + p], ones], axis=1)
        mixed = o_scr[p, mine, :] if together == 1 else 0.0
        for n in range(together):
            e = n if together == 2 else (step // 2) % 2
            keep = (lane128 >= HEAD_DIM * e) & (lane128 < HEAD_DIM * (e + 1))
            s = nt(jnp.concatenate([q * keep.astype(F32).astype(BF16), seg_aug], axis=1), keys)
            top = jnp.max(s, axis=1, keepdims=True)
            prob = jnp.exp(s - top).astype(BF16)
            o = nn(prob, values)
            weight = o[:, 128:]
            mixed = jnp.where(keep, o[:, :128] / weight, mixed)
            lse = top + jnp.log(weight)
            which = lane128 - (LSE0 + 3 * (2 * p + e))
            aug = jnp.where((which >= 0) & (which < 3), pieces(lse, which), aug)
        augq[mine, :] = aug
        o_scr[p, mine, :] = mixed
        return carry

    lax.fori_loop(0, 4 * PAIRS // together, attend, 0)

    for cp in weights:
        cp.wait()

    def apart(fn):
        pl.when(fi >= 0)(fn)

    @apart
    def _():
        a = jnp.concatenate([o_scr[p].astype(BF16) for p in range(PAIRS)], axis=1)
        out[a_rows, :] = a
        both = jnp.concatenate([xg[g], xg[g + half]], axis=0).astype(F32)
        r = iota(both.shape, 0)
        x = jnp.where((r < cells) | ((r >= rows) & (r < rows + cells)), both, 0.0)
        x2 = x + nn(a, w_out[...])
        x2_scr[...] = x2
        y_scr[...] = x2
        vhat, rstd = normed(x2)
        rstd_scr[...] = jnp.broadcast_to(rstd, (own, 128))
        vhat2_scr[...] = vhat
        out[h2_rows, :] = (vhat * g_mlp[...].reshape(1, -1)).astype(BF16)

    def mlp(j, carry):
        cols = pl.ds(pl.multiple_of(384 * j, 384), 384)
        u = nn(out[h2_rows, :], w_up[:, cols])
        u_scr[j] = u
        hid = gelu(u).astype(BF16)
        out[pl.ds(pl.multiple_of(own * j, 16), own), :] = hid
        y_scr[...] += nn(hid, w_down[cols, :])
        return carry

    lax.fori_loop(0, 4, mlp, 0)

    @apart
    def _():
        y = y_scr[...]
        vhat, rstd = normed(y)
        vhat3_scr[...] = vhat
        rstd_scr[...] = jnp.where(iota((own, 128), 1) < 64, rstd_scr[...], rstd)
        h3 = (vhat * g_learn[...].reshape(1, -1)).astype(BF16)
        for k in range(2):
            yp[256 * k : 256 * k + rows, :] = y[k * rows : (k + 1) * rows, :]
            yp[256 * k + rows : 256 * k + 256, :] = jnp.zeros((256 - rows, 384), F32)
            h3p[256 * k : 256 * k + rows, :] = h3[k * rows : (k + 1) * rows, :]
            h3p[256 * k + rows : 256 * k + 256, :] = jnp.zeros((256 - rows, 384), BF16)

    def shift_of(t):
        return GRID * (t // 3 - 1) + (t % 3 - 1)

    def moved(v, s):
        return v if s == 0 else pltpu.roll(v, (-s) % WIDE, 1)

    def tap(t):
        return tapmask[t : t + 1, :]

    def im2col(v):
        parts = [moved(v, shift_of(t)) * tap(t) for t in range(9)]
        return jnp.concatenate(parts + [jnp.zeros((56, WIDE), F32)], axis=0)

    def spread_of(v):
        return jnp.concatenate([moved(v, -shift_of(t)) * tap(8 - t) for t in range(9)], axis=0)

    @apart
    def _():
        taps = nt(w72_scr[...], h3p[...])
        z1 = jnp.zeros((MAPS, WIDE), F32)
        for t in range(9):
            z1 = z1 + moved(taps[8 * t : 8 * t + 8, :], shift_of(t)) * tap(t)
        zs = [z1]
        cols_of = []
        for layer in range(3):
            col = im2col(gelu(zs[-1]))
            cols_of.append(col)
            zs.append(nn(conv_fw[layer], col, HIGH)[0:MAPS])
        maps = tap(4) / (1.0 + jnp.exp(-zs[3]))
        dmaps = []
        for k in range(2):
            f = g + half * k
            dl = xg[f].astype(F32)[cells + 1 : cells + 1 + MAPS, :] * (1.0 / cells)
            dl = sixteen(dl)
            mk = sixteen(maps[:, 256 * k : 256 * k + 256])
            yk = yp[256 * k : 256 * k + 256, :]
            learned[k] = nn(mk, yk, HIGH)[0:MAPS] * (1.0 / cells)
            dmaps.append(nt(dl, yk, HIGH)[0:MAPS])
            dyp[256 * k : 256 * k + 256, :] = tn(mk, dl, HIGH)
        dz = jnp.concatenate(dmaps, axis=1) * maps * (1.0 - maps)
        small = []
        for layer in (2, 1, 0):
            dw = nt(sixteen(dz), cols_of[layer], HIGH)[0:MAPS]
            small.insert(0, jnp.concatenate([dw, jnp.zeros((MAPS, 256), F32)], axis=1))
            dz = tn(conv_bw[layer], sixteen(spread_of(dz)), HIGH)[0:MAPS] * gelu_grad(zs[layer])
        dz = dz.astype(BF16).astype(F32) * tap(4)
        spread_scr[...] = sixteen(spread_of(dz)).astype(BF16)
        rest_scr[...] = jnp.concatenate(small + [jnp.zeros((8, 384), F32)], axis=0)

    @apart
    def _():
        dh3 = tn(spread_scr[...], w72_scr[...])
        dh3 = jnp.concatenate([dh3[0:rows], dh3[256 : 256 + rows]], axis=0)
        dy, dg3 = norm_back(vhat3_scr[...], rstd_scr[:, 64:65], dh3, g_learn[...].reshape(1, -1))
        dy = dy + jnp.concatenate([dyp[0:rows, :], dyp[256 : 256 + rows, :]], axis=0)
        y_scr[...] = dy
        out[dm_rows, :] = dy.astype(BF16)
        dh2_scr[...] = jnp.zeros((own, 384), F32)
        gain_scr[...] = jnp.concatenate([dg3, jnp.zeros((7, 384), F32)], axis=0)

    def mlp_back(j, carry):
        cols = pl.ds(pl.multiple_of(384 * j, 384), 384)
        dm = out[dm_rows, :]
        du = (nt(dm, w_down[cols, :]) * gelu_grad(u_scr[j])).astype(BF16)
        buf[cols, :] = tn(out[h2_rows, :], du).astype(BF16)
        buf[pl.ds(pl.multiple_of(1536 + 384 * j, 384), 384), :] = tn(out[pl.ds(pl.multiple_of(own * j, 16), own), :], dm).astype(BF16)
        dh2_scr[...] += nt(du, w_up[:, cols])
        return carry

    lax.fori_loop(0, 4, mlp_back, 0)
    early[0].start(0)

    @apart
    def _():
        dx2, dg2 = norm_back(vhat2_scr[...], rstd_scr[:, 0:1], dh2_scr[...], g_mlp[...].reshape(1, -1))
        dx2 = dx2 + y_scr[...]
        dx2_scr[...] = dx2
        out[dm_rows, :] = dx2.astype(BF16)
        gains = jnp.concatenate([dg2, gain_scr[0:1, :], jnp.zeros((6, 384), F32)], axis=0)
        d_first = nn(spread_scr[...], h3p[...])[0:72]
        small = [d_first, gains, rest_scr[...], jnp.zeros((16, 384), F32)]
        buf[3456:3584, :] = jnp.concatenate(small, axis=0).astype(BF16)

    @apart
    def _():
        dzz = out[dm_rows, :]
        buf[3072:3456, :] = tn(out[a_rows, :], dzz).astype(BF16)
        da = nt(dzz, w_out[...]).astype(BF16)
        prod = jnp.concatenate([o_scr[p] for p in range(PAIRS)], axis=1) * da.astype(F32)
        lane = iota((own, 128), 1)
        which = lane - DEL0
        which = which - 3 * (which // 3)
        delta = pieces(nn(prod, blockones[...], HIGH), which)
        full = jnp.where((lane >= DEL0) & (lane < AUG_END), delta, augq[...])
        full = full.astype(BF16)
        for p in range(PAIRS):
            da_ext[p] = da[:, 128 * p : 128 * p + 128]
        da_ext[PAIRS] = full
        for k in range(2):
            there = pl.ds(pl.multiple_of((g + half * k) * rows, rows), rows)
            dag[:, there, :] = da_ext[:, k * rows : (k + 1) * rows, :]

    early[0].finish(0)
    early[0].start(1)
    early[1].start(0)
    da_near.run(0)
    da_far.run(0)
    x = jnp.concatenate([xg[g], xg[g + half]], axis=0).astype(F32)
    r = iota(x.shape, 0)
    x = jnp.where((r < cells) | ((r >= rows) & (r < rows + cells)), x, 0.0)
    vhat, _ = normed(x)
    h1_scr[...] = (vhat * g_attn[...].reshape(1, -1)).astype(BF16)
    dh1_scr[...] = jnp.zeros((own, 384), F32)
    buf[EARLY + 1152 :, :] = jnp.zeros((128, 384), BF16)
    early[1].finish(0)
    early[1].start(1)

    def own_rows(b):
        at = [qkv[b, pl.ds(pl.multiple_of((g + half * k) * rows, rows), rows), :] for k in range(2)]
        return jnp.concatenate(at, axis=0)

    own_augk = jnp.concatenate(
        [augk[pl.ds(pl.multiple_of((g + half * k) * rows, rows), rows), :] for k in range(2)], axis=0
    )
    chunk = 256
    pieces_n = total // chunk
    split = pieces_n // 2 - 1

    def query_pass(p, carry):
        def at_point(j):
            for k in range(PAIRS):
                i = 2 * k + j

                def point(i=i):
                    early_point(i)
                    stage = i // 2 + 1
                    if i % 2 == 1 and stage < da_near.last:
                        da_near.run(stage)
                        da_far.run(stage)

                pl.when(p == k)(point)

        dq = grad_pass(
            own_rows(p), da_ext[p], da_ext[PAIRS],
            lambda i: qkv[3 + p, i, :], lambda i: qkv[6 + p, i, :], lambda i: augk[i, :],
            p, pieces_n, split, chunk, False, at_point,
        )
        dqkv[p] = (dq * HEAD_DIM**-0.5).astype(BF16)
        return carry

    lax.fori_loop(0, PAIRS, query_pass, 0)
    for gather in (da_near, da_far):
        gather.run(gather.last)
        gather.drain()

    def key_pass(p, carry):
        def at_point(j):
            for k in range(PAIRS):
                i = 2 * PAIRS + 2 * k + j

                def point(i=i, k=k):
                    early_point(i)
                    for piece, (_, _, after) in zip(late, LATE_CUTS):
                        if after < k:
                            step = 2 * (k - after - 1) + j
                            piece.finish(step)
                            piece.start(step + 1)

                pl.when(p == k)(point)

        dk, dv = grad_pass(
            own_rows(3 + p), own_rows(6 + p), own_augk,
            lambda i: qkv[p, i, :], lambda i: dag[p, i, :], lambda i: dag[PAIRS, i, :],
            p, pieces_n, split, chunk, True, at_point,
        )
        d = jnp.concatenate([dqkv[p], dk.astype(BF16), dv.astype(BF16)], axis=1)
        buf[pl.ds(pl.multiple_of(EARLY + 384 * p, 128), 384), :] = tn(h1_scr[...], d).astype(BF16)
        w = jnp.concatenate(
            [w_qkv[:, pl.ds(pl.multiple_of(384 * b + 128 * p, 128), 128)] for b in range(3)], axis=1
        )
        dh1_scr[...] += nt(d, w)
        for piece, (_, _, after) in zip(late, LATE_CUTS):
            if after < PAIRS - 1:
                pl.when(p == after)(functools.partial(piece.start, 0))
        return carry

    lax.fori_loop(0, PAIRS, key_pass, 0)
    late[0].start(0)
    dx, dg = norm_back(*normed(x), dh1_scr[...], g_attn[...].reshape(1, -1))
    buf[EARLY + 1152 : EARLY + 1168, :] = jnp.concatenate([dg, jnp.zeros((15, 384), F32)], axis=0).astype(BF16)
    late[1].start(0)
    dx = dx + dx2_scr[...]
    for k in range(2):
        tail = jnp.concatenate([learned[k], jnp.zeros((rows - cells - MAPS, 384), F32)], axis=0)
        whole = jnp.concatenate([dx[k * rows : k * rows + cells, :], tail], axis=0)

        @pl.when(mine == k)
        def _():
            own_tok[...] = whole

        @pl.when(mine != k)
        def _():
            tok_send[...] = whole.astype(BF16)

    tok_copy = rc(tok_send, tok_land, tsem.at[0], tsem.at[1], (fi + half * (1 - 2 * mine), si))
    tok_copy.start()
    give = [
        pltpu.make_async_copy(out.at[pl.ds(at, n), :], sums.at[pl.ds(at, n), :], fsem.at[i])
        for i, (at, n) in enumerate((EARLY_CUTS[0], (EARLY_CUTS[1][0], EARLY + LATE - EARLY_CUTS[1][0])))
    ]
    running = [(piece, 1 + len(points)) for piece, points in zip(early, EARLY_POINTS)]
    running += [(piece, 2 * (PAIRS - 1 - after)) for piece, (_, _, after) in zip(late, LATE_CUTS)]
    for piece, n in running[:1]:
        for i in range(n, piece.total):
            piece.finish(i)
            piece.start(i + 1)
    give[0].start()
    for i in range(max(piece.total - n for piece, n in running[1:])):
        for piece, n in running[1:]:
            piece.finish(n + i)
            piece.start(n + i + 1)
    give[1].start()
    tok_copy.wait()
    far_tok[...] = tok_land[...]
    for cp in give:
        cp.wait()


def finish_kernel(cells, half, sums, own_tok, far_tok, d_tokens, learned, g_attn, w_qkv, w_out, g_mlp, w_up, w_down, g_learn, first, rest):
    for j in range(4):
        w_up[:, 384 * j : 384 * j + 384] = sums[384 * j : 384 * j + 384, :].astype(F32)
    w_down[...] = sums[1536:3072, :].astype(F32)
    w_out[...] = sums[3072:3456, :].astype(F32)
    small = sums[3456:3584, :].astype(F32)
    first[...] = small[0:72].reshape(9, MAPS, 384)
    for n in range(27):
        layer, t = n // 9, n % 9
        rest[n] = small[80 + MAPS * layer : 88 + MAPS * layer, MAPS * t : MAPS * (t + 1)]
    g_mlp[...] = small[72:73].reshape(-1)
    g_learn[...] = small[73:74].reshape(-1)
    for p in range(PAIRS):
        block = sums[EARLY + 384 * p : EARLY + 384 * p + 384, :].astype(F32)
        for b in range(3):
            w_qkv[:, 384 * b + 128 * p : 384 * b + 128 * p + 128] = block[:, 128 * b : 128 * b + 128]
    g_attn[...] = sums[EARLY + 1152 : EARLY + 1168, :].astype(F32)[0:1].reshape(-1)
    mine = lax.axis_index("frame") // half
    far = far_tok[...].astype(F32)
    near = own_tok[...]
    a, b = near[0:cells], far[0:cells]
    d_tokens[:, 0, :] = jnp.where(mine == 0, a, b)
    d_tokens[:, 1, :] = jnp.where(mine == 0, b, a)
    a, b = near[cells : cells + MAPS], far[cells : cells + MAPS]
    learned[...] = jnp.where(mine == 0, jnp.concatenate([a, b], axis=0), jnp.concatenate([b, a], axis=0)).astype(BF16)


def vspec(n):
    return [pl.BlockSpec(memory_space=VMEM)] * n


def params(collective=None, mib=56):
    if collective is None:
        return pltpu.CompilerParams(vmem_limit_bytes=mib * MIB)
    return pltpu.CompilerParams(collective_id=collective, has_side_effects=True, vmem_limit_bytes=mib * MIB)


def tap_masks():
    p = np.arange(WIDE) % 256
    px, py = p // GRID, p % GRID
    out = np.zeros((16, WIDE), np.float32)
    for t in range(9):
        r, c = t // 3 - 1, t % 3 - 1
        out[t] = (p < CELLS) & (px + r >= 0) & (px + r < GRID) & (py + c >= 0) & (py + c < GRID)
    return out


def head_sums():
    out = np.zeros((HEADS * HEAD_DIM, 128), np.float32)
    for h in range(HEADS):
        out[h * HEAD_DIM : (h + 1) * HEAD_DIM, DEL0 + 3 * h : DEL0 + 3 * h + 3] = 1.0
    return out


def on_device(frames, seqs, tokens, segments, g_attn, w_qkv, w_out, g_mlp, w_up, w_down, g_learn, conv_first, conv_rest, d_learned):
    _, cells, width = tokens.shape
    rows = -(-(cells + 1 + MAPS) // 16) * 16
    own = 2 * rows
    total = frames * rows
    n_sems = 2 + 16 * frames
    sds = jax.ShapeDtypeStruct
    rest = conv_rest.transpose(0, 2, 3, 1, 4).reshape(27 * MAPS, MAPS)
    small_in = jnp.concatenate(
        [
            conv_first.transpose(1, 2, 0, 3).reshape(9 * MAPS, width),
            d_learned.reshape(2 * MAPS, width),
            jnp.pad(rest, ((0, 0), (0, width - MAPS))),
        ],
        axis=0,
    ).astype(F32)
    n_all = EARLY + LATE
    sizes = [landing(n, early_groups(frames, seqs), EARLY_BITS) for _, n in EARLY_CUTS]
    sizes += [landing(n, late_groups(frames, seqs), LATE_BITS) for _, n, _ in LATE_CUTS]
    land_n, copies = (sum(v) for v in zip(*sizes))
    anywhere = pl.BlockSpec(memory_space=pl.ANY)
    sums, own_tok, far_tok = pl.pallas_call(
        functools.partial(whole_kernel, frames, seqs, rows, cells),
        out_shape=[sds((n_all, width), BF16), sds((rows, width), F32), sds((rows, width), BF16)],
        in_specs=vspec(5) + [anywhere] + vspec(1) + [anywhere] * 2 + vspec(3),
        out_specs=[anywhere] + vspec(2),
        scratch_shapes=[
            VMEM((2, rows, width), BF16),
            VMEM((frames, rows, width), BF16),
            VMEM((9, total, 128), BF16),
            VMEM((total, 128), BF16),
            VMEM((PAIRS + 1, total, 128), BF16),
            VMEM((PAIRS + 1, own, 128), BF16),
            VMEM((own, width), F32),
            VMEM((2, MAPS, width), F32),
            VMEM((own, 128), F32),
            VMEM((PAIRS, own, 128), F32),
            VMEM((own, width), F32),
            VMEM((own, width), F32),
            VMEM((own, width), F32),
            VMEM((own, width), F32),
            VMEM((own, 128), F32),
            VMEM((own, width), F32),
            VMEM((4, own, width), F32),
            VMEM((WIDE, width), BF16),
            VMEM((WIDE, width), F32),
            VMEM((WIDE, width), F32),
            VMEM((80, width), BF16),
            VMEM((80, WIDE), BF16),
            VMEM((32, width), F32),
            VMEM((8, width), F32),
            VMEM((3, 80, 128), F32),
            VMEM((3, 16, 128), F32),
            VMEM((PAIRS, own, 128), BF16),
            VMEM((own, width), BF16),
            VMEM((own, width), F32),
            VMEM((n_all, width), BF16),
            VMEM((land_n, width), BF16),
            VMEM((n_all, width), BF16),
            VMEM((rows, width), BF16),
            VMEM((rows, width), BF16),
            pltpu.SemaphoreType.DMA((n_sems,)),
            pltpu.SemaphoreType.DMA((2 * frames,)),
            pltpu.SemaphoreType.DMA((n_sems,)),
            pltpu.SemaphoreType.DMA((frames,)),
            pltpu.SemaphoreType.DMA((copies,)),
            pltpu.SemaphoreType.DMA((copies,)),
            pltpu.SemaphoreType.DMA((2,)),
            pltpu.SemaphoreType.DMA((2,)),
            pltpu.SemaphoreType.DMA((3,)),
            VMEM((width, width), BF16),
            VMEM((width, 4 * width), BF16),
            VMEM((4 * width, width), BF16),
        ],
        compiler_params=params(0, 61),
        name="layer",
    )(
        jnp.pad(tokens, ((0, 0), (0, rows - cells), (0, 0))), segments, small_in,
        g_attn, w_qkv, w_out, g_mlp, w_up, w_down, g_learn,
        jnp.asarray(tap_masks()), jnp.asarray(head_sums()),
    )
    d_tokens, learned_all, dg_attn, d_w_qkv, d_w_out, dg_mlp, d_w_up, d_w_down, dg_learn, first, rest = pl.pallas_call(
        functools.partial(finish_kernel, cells, frames // 2),
        out_shape=[
            sds((cells, 2, width), F32),
            sds((2 * MAPS, width), BF16),
            sds((width,), F32),
            sds((width, 3 * width), F32),
            sds((width, width), F32),
            sds((width,), F32),
            sds((width, 4 * width), F32),
            sds((4 * width, width), F32),
            sds((width,), F32),
            sds((9, MAPS, width), F32),
            sds((27, MAPS, MAPS), F32),
        ],
        in_specs=vspec(3),
        out_specs=vspec(11),
        compiler_params=params(),
        name="outputs",
    )(sums, own_tok, far_tok)
    d_first = first.reshape(3, 3, MAPS, width).transpose(2, 0, 1, 3)
    d_rest = rest.reshape(3, 3, 3, MAPS, MAPS).transpose(0, 3, 1, 2, 4)
    return (
        learned_all.reshape(2, MAPS, width), d_tokens.transpose(1, 0, 2), dg_attn, d_w_qkv, d_w_out, dg_mlp, d_w_up, d_w_down, dg_learn, d_first, d_rest,
    )


def solution(mesh):
    frames, seqs = mesh.shape["frame"], mesh.shape["seq"]
    both = P("seq", "frame", None)
    in_specs = (both, P("seq", "frame"), *([P()] * 9), both)
    out_specs = (both, both, *([P()] * 9))
    return jax.shard_map(
        functools.partial(on_device, frames, seqs),
        mesh=mesh,
        in_specs=in_specs,
        out_specs=out_specs,
        check_vma=False,
    )
```
